128 devices in a mesh: rows: 32 (over y, z, core), ch: 4 (over x).
Axes of the slice: x: 4, y: 4, z: 4, core: 2. Of those that a mesh axis runs over, the one named last changes fastest.
Arguments:
- tile_image: bfloat16 [768, 256, 256], P('ch', 'rows'), may hold values from -23 to 23
- spectral_filter: float32 [2, 768, 256, 256], P(None, 'ch', 'rows'), may hold values from -4 to 4
- conv_taps: float32 [768, 9], P('ch'), may hold values from -4 to 4
- norm_gain: float32 [768], replicated, may hold values from 0.25 to 1.75
- up_weight: bfloat16 [768, 3072], P(None, 'ch'), may hold values from -0.21875 to 0.21875
- down_weight: bfloat16 [3072, 768], P('ch'), may hold values from -0.109375 to 0.109375
- upstream: bfloat16 [768, 256, 256], P('ch', 'rows'), may hold values from -5 to 5
Outputs:
- block_out: bfloat16 [768, 256, 256], P('ch', 'rows')
- grad_image: float32 [768, 256, 256], P('ch', 'rows')
- grad_filter: float32 [2, 768, 256, 256], P(None, 'ch', 'rows')
The draws below stay inside these ranges and needn't reach their ends.
All inputs are finite; a program needn't handle non-finite values.
Results may differ from the reference program's by a relative error of at most 0.012.
Values may be sent and summed in bfloat16 or wider, within the bound.
No kernel may reach another device: no remote copies, remote signals or barrier semaphores. Data moves between devices by JAX's collectives and lax.ppermute only.
A program may use at most 128 MiB of HBM per device.

```python
import math
import jax
import jax.numpy as jnp
from jax import lax

CHANNEL_COUNT = 768
FF = 3072
H = 256
GRID_COLUMNS = 256
N_CH = 4


def draw_tile_image(key, part):
    entry_key, chan_key, place_key = jax.random.split(key, 3)
    chan_scale = jnp.exp(jax.random.uniform(chan_key, (CHANNEL_COUNT, 1, 1), jnp.float32, math.log(0.3), math.log(3.0)))
    place_scale = jnp.exp(jax.random.uniform(place_key, (1, H, GRID_COLUMNS), jnp.float32, math.log(0.5), math.log(2.0)))
    entries = jax.random.truncated_normal(entry_key, -3.0, 3.0, (CHANNEL_COUNT, H, GRID_COLUMNS), jnp.float32)
    return (entries * chan_scale * place_scale).astype(jnp.bfloat16)


def levels(rng, extent, shards, low, high):
    loudness, own = 1.0, jax.random.fold_in(rng, 6)
    for axis_at, parts in shards:
        heights = jnp.exp(jax.random.uniform(jax.random.fold_in(own, axis_at), (parts,), jnp.float32, low / len(shards), high / len(shards)))
        loudness = loudness * jnp.repeat(heights, extent[axis_at] // parts).reshape([-1 if axis == axis_at else 1 for axis in range(len(extent))])
    return loudness


def normal_values(key, dims, scale, most, cuts=(), held_as=jnp.bfloat16):
    result = scale * jax.random.normal(key, dims, jnp.float32)
    if cuts:
        result = result * levels(key, dims, cuts, -0.22, 0.18)
    return jnp.clip(result, -most, most).astype(held_as)


def setup_inputs(seed: int = 0) -> dict:
    key_list = jax.random.split(jax.random.key(seed), 8)
    return {
        "tile_image": draw_tile_image(jax.random.fold_in(key_list[7], 71), 0),
        "spectral_filter": normal_values(key_list[1], (2, CHANNEL_COUNT, GRID_COLUMNS, H), 0.7, 4.0, ((1, 4), (2, 32)), jnp.float32),
        "conv_taps": normal_values(key_list[2], (CHANNEL_COUNT, 9), 0.33, 4.0, ((0, 4),), jnp.float32),
        "norm_gain": jnp.clip(1.0 + 0.15 * jax.random.normal(key_list[3], (CHANNEL_COUNT,), jnp.float32), 0.25, 1.75),
        "up_weight": normal_values(key_list[4], (CHANNEL_COUNT, FF), CHANNEL_COUNT ** -0.5, 0.21875, ((1, 4),)),
        "down_weight": normal_values(key_list[5], (FF, CHANNEL_COUNT), FF ** -0.5, 0.109375, ((0, 4),)),
        "upstream": normal_values(key_list[6], (CHANNEL_COUNT, H, GRID_COLUMNS), 1.0, 5.0, ((0, 4), (1, 32))),
    }


norm_epsilon = 1e-05
root_half = 0.7071067811865476
density = 0.3989422804014327

def depthwise(values, tap_weights):
    token_row_count, col_count = (values.shape[1], values.shape[2])
    padded = jnp.pad(values, ((0, 0), (1, 1), (1, 1)))
    running = jnp.zeros_like(values)
    for row_off in range(3):
        for col_off in range(3):
            running = running + tap_weights[:, 3 * row_off + col_off][:, None, None] * padded[:, row_off:row_off + token_row_count, col_off:col_off + col_count]
    return running

def layer_norm(whole):
    values = whole.astype(jnp.float32)
    centred = values - lax.optimization_barrier(jnp.mean(values, axis=0))[None]
    inv_std = lax.rsqrt(lax.optimization_barrier(jnp.mean(centred * centred, axis=0)) + norm_epsilon)
    return (centred * inv_std[None], inv_std)

def gelu_slope(pre_act):
    return 0.5 * (1.0 + lax.erf(pre_act * root_half)) + pre_act * density * jnp.exp(-0.5 * pre_act * pre_act)

def norm_back(normed_gradient, normed, inv_std, gain):
    weighted = normed_gradient * gain[None, :, None, None]
    mean_one = lax.optimization_barrier(jnp.mean(weighted, axis=1, keepdims=True))
    second = lax.optimization_barrier(jnp.mean(weighted * normed[None], axis=1, keepdims=True))
    return inv_std[None, None] * (weighted - mean_one - normed[None] * second)

def settle(partials):
    return lax.optimization_barrier(jnp.sum(lax.optimization_barrier(partials.astype(jnp.bfloat16)).astype(jnp.float32), axis=0))

def rounded_copy(values):
    return lax.optimization_barrier(values.astype(jnp.bfloat16)).astype(jnp.float32)

def reference(tile_image, spectral_filter, conv_taps, norm_gain, up_weight, down_weight, upstream):
    signal = tile_image.astype(jnp.float32)
    kernel = jnp.transpose(spectral_filter[0] + 1j * spectral_filter[1], (0, 2, 1))
    spectrum = jnp.fft.fft2(signal, axes=(1, 2))
    filtered = jnp.real(jnp.fft.ifft2(kernel * spectrum, axes=(1, 2)))
    hidden_state = signal + depthwise(filtered, conv_taps)
    complete_up_weight = up_weight.astype(jnp.float32)
    down_full = down_weight.astype(jnp.float32)
    hidden_share_units = FF // N_CH

    def mlp_rows(pieces):
        hidden_rows, grad_rows = pieces
        token_row_count = hidden_rows.shape[1]
        normed, inv_std = layer_norm(lax.optimization_barrier(hidden_rows.astype(jnp.bfloat16)))
        scaled = rounded_copy(normed * norm_gain[:, None, None])
        pre_act = jnp.einsum('chw,cf->fhw', scaled, complete_up_weight)
        activated = rounded_copy(jax.nn.gelu(pre_act, approximate=False))
        partials = jnp.einsum('bfhw,bfc->bchw', activated.reshape(N_CH, hidden_share_units, token_row_count, GRID_COLUMNS), down_full.reshape(N_CH, hidden_share_units, CHANNEL_COUNT))
        out_rows = (hidden_rows + settle(partials)).astype(jnp.bfloat16)
        grad_act = jnp.einsum('chw,fc->fhw', grad_rows.astype(jnp.float32), down_full)
        preactivation_gradient = rounded_copy(grad_act * gelu_slope(pre_act))
        normed_gradient = jnp.einsum('pjra,spj->psra', preactivation_gradient.reshape(N_CH, hidden_share_units, token_row_count, GRID_COLUMNS), complete_up_weight.reshape(CHANNEL_COUNT, N_CH, hidden_share_units))
        return (out_rows, settle(norm_back(normed_gradient, normed, inv_std, norm_gain)))
    block_count = H // 8

    def split_rows(values):
        return jnp.transpose(values.reshape(CHANNEL_COUNT, block_count, 8, GRID_COLUMNS), (1, 0, 2, 3))

    def join_rows(values):
        return jnp.transpose(values, (1, 0, 2, 3)).reshape(CHANNEL_COUNT, H, GRID_COLUMNS)
    out_parts, grad_parts = lax.map(mlp_rows, (split_rows(hidden_state), split_rows(upstream)))
    block_out = join_rows(out_parts)
    grad_hidden = upstream.astype(jnp.float32) + join_rows(grad_parts)
    grad_filtered = depthwise(grad_hidden, conv_taps[:, ::-1])
    grad_spectrum = jnp.fft.fft2(grad_filtered, axes=(1, 2))
    grad_image = grad_hidden + jnp.real(jnp.fft.ifft2(jnp.conj(kernel) * grad_spectrum, axes=(1, 2)))
    factor = 1.0 / (H * GRID_COLUMNS)
    first_part = (grad_spectrum.real * spectrum.real + grad_spectrum.imag * spectrum.imag) * factor
    second_part = (grad_spectrum.imag * spectrum.real - grad_spectrum.real * spectrum.imag) * factor
    grad_filter = jnp.transpose(jnp.stack([first_part, second_part]), (0, 1, 3, 2))
    return (block_out, grad_image, grad_filter)
```

```python
import functools

import jax
import jax.numpy as jnp
import ml_dtypes
import numpy as np
from jax import lax
from jax.experimental import pallas as pl
from jax.experimental.pallas import tpu as pltpu
from jax.sharding import PartitionSpec as P

norm_epsilon = 1e-05
root_half = 0.7071067811865476
density = 0.3989422804014327

ROWS_DEVICES = 32
CH_DEVICES = 4
LEN = 256
SLAB = 8
CH = 192
ALL_CH = 768
LANES = SLAB * CH
WIDE = SLAB * 128
POINTS = LEN * LEN
HALF_UNITS = 384
F32 = jnp.float32
BF16 = jnp.bfloat16
MIB = 1 << 20


def narrow_at(h):
    return WIDE + 64 * (2 * (h % 4) + h // 4)


def columns_of(device):
    base = SLAB * device
    return [base + 1, base + 2, base + 3, base + 4 if device < 16 else base]


def column_tables():
    w = np.arange(LEN)
    forward, inverse = np.zeros((LEN, LEN)), np.zeros((LEN, LEN))
    for device in range(ROWS_DEVICES):
        for j, kw in enumerate(columns_of(device)):
            turn = 2 * np.pi * (kw * w % LEN) / LEN
            re, im = SLAB * device + j, SLAB * device + 4 + j
            if device == 16 and j == 3:
                forward[re] = inverse[re] = 1.0
                forward[im] = inverse[im] = np.where(w % 2 == 0, 1.0, -1.0)
            else:
                forward[re], forward[im] = np.cos(turn), -np.sin(turn)
                inverse[re], inverse[im] = 2 * np.cos(turn), -2 * np.sin(turn)
    return forward, inverse


def row_tables():
    k1, src = np.arange(32)[:, None], np.arange(32)[None, :]
    turn = 2 * np.pi * (k1 * src % 32) / 32
    cos, sin = np.cos(turn), np.sin(turn)
    forward = np.zeros((2, 5, 32, 32, 2, 4))
    inverse = np.zeros((32, 2, 4, 2, 4, 32))
    for j in range(4):
        forward[0, j, :, :, 0, j], forward[0, j, :, :, 1, j] = cos, sin
        forward[1, j, :, :, 0, j], forward[1, j, :, :, 1, j] = -sin, cos
        inverse[:, 0, j, 0, j, :], inverse[:, 0, j, 1, j, :] = cos.T, -sin.T
        inverse[:, 1, j, 0, j, :], inverse[:, 1, j, 1, j, :] = sin.T, cos.T
    forward[0, 4, :, :, 0, 3], forward[0, 4, :, :, 1, 3] = cos, -sin
    forward[1, 4, :, :, 0, 3], forward[1, 4, :, :, 1, 3] = -sin, -cos
    return forward.reshape(320, 256), inverse.reshape(256, 256)


def twiddle_tables():
    token_row = np.zeros(LANES, np.int64)
    for h in range(SLAB):
        token_row[128 * h : 128 * h + 128] = h
        token_row[narrow_at(h) : narrow_at(h) + 64] = h
    turn = 2 * np.pi * (np.arange(32)[:, None] * token_row[None, :] % LEN) / LEN
    return np.cos(turn), np.sin(turn)


def turn_tables():
    k2, k1 = np.divmod(np.arange(LEN), 32)
    kh = k1 + 32 * k2
    straight, mirrored = np.zeros((LEN, LEN)), np.zeros((LEN, LEN))
    straight[np.arange(LEN), kh] = 1.0
    mirrored[np.arange(LEN), -kh % LEN] = 1.0
    return straight, mirrored


def narrow(table):
    return np.asarray(table, np.float64).astype(ml_dtypes.bfloat16)


FORWARD_COLUMNS, INVERSE_COLUMNS = (narrow(t) for t in column_tables())
FORWARD_ROWS, INVERSE_ROWS = (narrow(t) for t in row_tables())
TWIDDLE_COS, TWIDDLE_SIN = (t.astype(np.float32) for t in twiddle_tables())
STRAIGHT, MIRRORED = (narrow(t) for t in turn_tables())
UNIT = narrow(np.eye(LEN))


def nn(a, b):
    return lax.dot_general(a, b, (((1,), (0,)), ((), ())), preferred_element_type=F32)


def nt(a, b):
    return lax.dot_general(a, b, (((1,), (1,)), ((), ())), preferred_element_type=F32)


def tn(a, b):
    return lax.dot_general(a, b, (((0,), (0,)), ((), ())), preferred_element_type=F32)


def kernel_call(body, name, outs, scratch, operands, vmem, flops=0, smem=0):
    whole = pl.BlockSpec(memory_space=pltpu.VMEM)
    scalar = pl.BlockSpec(memory_space=pltpu.SMEM)
    moved = sum(a.size * a.dtype.itemsize for a in operands)
    moved += sum(o.size * np.dtype(o.dtype).itemsize for o in outs)
    return pl.pallas_call(
        body,
        name=name,
        out_shape=tuple(outs),
        in_specs=[scalar] * smem + [whole] * (len(operands) - smem),
        out_specs=tuple(whole for _ in outs),
        scratch_shapes=scratch,
        cost_estimate=pl.CostEstimate(flops=flops, bytes_accessed=moved, transcendentals=0),
        compiler_params=pltpu.CompilerParams(vmem_limit_bytes=vmem * MIB),
    )(*operands)


def shape(dims, dtype):
    return jax.ShapeDtypeStruct(dims, dtype)


def fill_wide(wide_ref, values):
    for side in range(2):
        wide_ref[side] = values[:, side * 128 : side * 128 + 128]


def every_eighth(wide_ref, h):
    return jnp.concatenate([wide_ref[side, pl.ds(h, CH, stride=SLAB), :] for side in range(2)], axis=1)


def put_eighth(wide_ref, first, values):
    for side in range(2):
        at = pl.ds(first, values.shape[0], stride=SLAB)
        wide_ref[side, at, :] = values[:, side * 128 : side * 128 + 128]


def take_wide(wide_ref):
    return jnp.concatenate([wide_ref[side] for side in range(2)], axis=1)


def unfold_rows(source_ref, wide_ref):
    fill_wide(wide_ref, source_ref[...].astype(F32))
    for h in range(SLAB):
        yield h, every_eighth(wide_ref, h).astype(BF16)


def columns_kernel(image_ref, table_ref, message_ref, kept_ref, wide_ref, lanes_ref):
    for h, rows in unfold_rows(image_ref, wide_ref):
        kept_ref[h * CH : (h + 1) * CH] = rows
        lanes_ref[h * 128 : h * 128 + 128] = rows[:128]
        lanes_ref[narrow_at(h) : narrow_at(h) + 64] = rows[128:]
    send_columns(table_ref, lanes_ref, message_ref)


def send_columns(table_ref, lanes_ref, message_ref):
    for at in range(0, LANES, 512):
        message_ref[:, at : at + 512] = nt(table_ref[...], lanes_ref[at : at + 512]).astype(BF16)


def unfold_kernel(source_ref, kept_ref, wide_ref):
    for h, rows in unfold_rows(source_ref, wide_ref):
        kept_ref[h * CH : (h + 1) * CH] = rows


def filter_split_kernel(filter_ref, turned_ref, wide_ref):
    for part in range(2):
        fill_wide(wide_ref, filter_ref[part])
        for i in range(SLAB):
            turned_ref[i, part] = every_eighth(wide_ref, i).astype(BF16)


def put_spectrum(target_ref, part, column, block):
    rows = slice(column * 32, column * 32 + 32)
    for k2 in range(SLAB):
        piece = block[k2 * 32 : k2 * 32 + 32]
        target_ref[part, rows, k2 * 128 : k2 * 128 + 128] = piece[:, :128]
        at = WIDE + 64 * k2
        target_ref[part, rows, at : at + 64] = piece[:, 128:]


def filter_kernel(
    place_ref, own_ref, pair_ref, lone_ref, straight_ref, mirrored_ref, main_ref, cross_ref
):
    device = place_ref[0]
    low, special = device < 16, device == 16
    scale = 0.5 / POINTS
    for part in range(2):
        sign = 1.0 if part == 0 else -1.0
        for j in range(3):
            straight = nt(straight_ref[...], own_ref[1 + j, part])
            mirrored = nt(mirrored_ref[...], pair_ref[3 - j, part])
            put_spectrum(main_ref, part, j, (straight + sign * mirrored) * scale)
        own = jnp.where(low, own_ref[4, part], own_ref[0, part])
        other = jnp.where(low, pair_ref[0, part], lone_ref[part])
        o, q = nt(straight_ref[...], own), nt(straight_ref[...], other)
        o_back = nt(mirrored_ref[...], own) * sign
        q_back = nt(mirrored_ref[...], other) * sign
        usual = (o + q_back) * scale
        put_spectrum(
            main_ref, part, 3, jnp.where(special, (o + o_back + q + q_back) * (0.5 * scale), usual)
        )
        put_spectrum(
            cross_ref,
            part,
            0,
            jnp.where(special, (q + q_back - o - o_back) * (0.5 * scale), 0.0 * usual),
        )


def eighth_turn(value, step, sign):
    re, im = value
    if step == 0:
        return value
    if step == 1:
        return (re + sign * im) * root_half, (im - sign * re) * root_half
    if step == 2:
        return sign * im, -sign * re
    return (sign * im - re) * root_half, (-sign * re - im) * root_half


def add(a, b):
    return a[0] + b[0], a[1] + b[1]


def sub(a, b):
    return a[0] - b[0], a[1] - b[1]


def four_points(x, sign):
    s, d = add(x[0], x[2]), sub(x[0], x[2])
    t, u = add(x[1], x[3]), eighth_turn(sub(x[1], x[3]), 2, sign)
    return [add(s, t), add(d, u), sub(s, t), sub(d, u)]


def eight_points(x, sign):
    even = four_points([add(x[m], x[m + 4]) for m in range(4)], sign)
    odd = four_points([eighth_turn(sub(x[m], x[m + 4]), m, sign) for m in range(4)], sign)
    return [part[q] for q in range(4) for part in (even, odd)]


def upper_lanes(like):
    return lax.broadcasted_iota(jnp.int32, like.shape, 1) >= 64


def halves(value):
    upper = upper_lanes(value)
    return pltpu.roll(value, 64, axis=1) + jnp.where(upper, -value, value)


def upper_turn(value, step, sign):
    upper = upper_lanes(value[0])
    return tuple(jnp.where(upper, b, a) for a, b in zip(value, eighth_turn(value, step, sign)))


def narrow_forward(x, sign):
    turned = [upper_turn((halves(re), halves(im)), m, sign) for m, (re, im) in enumerate(x)]
    return four_points(turned, sign)


def narrow_inverse(x, sign):
    turned = [upper_turn(v, m, sign) for m, v in enumerate(four_points(x, sign))]
    return [(halves(re), halves(im)) for re, im in turned]


def lane_blocks(re, im):
    return [(re[:, at : at + 128], im[:, at : at + 128]) for at in range(0, LANES, 128)]


def to_frequencies(re, im, cos, sin):
    x = lane_blocks(re * cos + im * sin, im * cos - re * sin)
    return eight_points(x[:SLAB], 1.0) + narrow_forward(x[SLAB:], 1.0)


def to_tokens_rows(blocks, cos, sin):
    y = eight_points(blocks[:SLAB], -1.0) + narrow_inverse(blocks[SLAB:], -1.0)
    re = jnp.concatenate([v[0] for v in y], axis=1)
    im = jnp.concatenate([v[1] for v in y], axis=1)
    return re * cos - im * sin, im * cos + re * sin


def row_body(saves, refs):
    place_ref, received_ref, fwd_ref, inv_ref, cos_ref, sin_ref, main_ref, cross_ref = refs[:8]
    if saves:
        message_ref, seen_ref, mixed_ref, ready_ref = refs[8:]
    else:
        seen_ref, message_ref, product_ref, mixed_ref, ready_ref = refs[8:]
    for at in range(0, LANES, 512):
        mixed_ref[:, at : at + 512] = nn(fwd_ref[...], received_ref[:, at : at + 512])

    def spectrum(group):
        at = pl.multiple_of(group * 16, 16)
        table = pl.ds(pl.multiple_of(lax.rem(group, 2) * 16, 16), 16)
        return to_frequencies(
            mixed_ref[pl.ds(at, 16), :],
            mixed_ref[pl.ds(160 + at, 16), :],
            cos_ref[table, :],
            sin_ref[table, :],
        )

    def save(group, blocks):
        at = pl.ds(pl.multiple_of(group * 16, 16), 16)
        for n, value in enumerate(blocks):
            for part in range(2):
                seen_ref[part, at, n * 128 : n * 128 + 128] = value[part].astype(BF16)

    def times(value, n, source_ref, at):
        k_re = source_ref[0, at, n * 128 : n * 128 + 128]
        k_im = source_ref[1, at, n * 128 : n * 128 + 128]
        re, im = value
        if saves:
            return re * k_re - im * k_im, im * k_re + re * k_im
        return re * k_re + im * k_im, im * k_re - re * k_im

    def store_back(group, blocks):
        table = pl.ds(pl.multiple_of(lax.rem(group, 2) * 16, 16), 16)
        re, im = to_tokens_rows(blocks, cos_ref[table, :], sin_ref[table, :])
        at = pl.multiple_of(group * 16, 16)
        ready_ref[pl.ds(at, 16), :] = re.astype(BF16)
        ready_ref[pl.ds(128 + at, 16), :] = im.astype(BF16)

    def seen(group, n):
        at = pl.ds(pl.multiple_of(group * 16, 16), 16)
        return tuple(seen_ref[part, at, n * 128 : n * 128 + 128].astype(F32) for part in range(2))

    def product(a, b, factor):
        re = (a[0] * b[0] + a[1] * b[1]) * factor
        return re, (b[1] * a[0] - b[0] * a[1]) * factor

    def put_product(group, n, value):
        at = pl.ds(pl.multiple_of(group * 16, 16), 16)
        for part in range(2):
            product_ref[part, at, n * 128 : n * 128 + 128] = value[part].astype(BF16)

    def plain(group, carry):
        at = pl.ds(pl.multiple_of(group * 16, 16), 16)
        values = spectrum(group)
        if saves:
            save(group, values)
        else:
            for n, value in enumerate(values):
                put_product(group, n, product(seen(group, n), value, 1.0 / POINTS))
        store_back(group, [times(v, n, main_ref, at) for n, v in enumerate(values)])
        return carry

    def packed(group, carry):
        at = pl.ds(pl.multiple_of(group * 16, 16), 16)
        cross_at = pl.ds(pl.multiple_of((group - 6) * 16, 16), 16)
        values, mirrors = spectrum(group), spectrum(group + 2)
        if saves:
            save(group, values)
            save(group + 2, mirrors)
        else:
            special = place_ref[0] == 16
            for n, (value, mirror) in enumerate(zip(values, mirrors)):
                first, first_mirror = seen(group, n), seen(group + 2, n)
                usual = product(first, value, 1.0 / POINTS)
                odd = product(sub(first, first_mirror), sub(value, mirror), 0.25 / POINTS)
                even = product(add(first, first_mirror), add(value, mirror), 0.25 / POINTS)
                put_product(group, n, [jnp.where(special, a, b) for a, b in zip(odd, usual)])
                put_product(group + 2, n, [jnp.where(special, a, b) for a, b in zip(even, usual)])
        store_back(
            group,
            [
                add(times(v, n, main_ref, at), times(m, n, cross_ref, cross_at))
                for n, (v, m) in enumerate(zip(values, mirrors))
            ],
        )
        return carry

    lax.fori_loop(0, 6, plain, 0)
    lax.fori_loop(6, 8, packed, 0)
    for at in range(0, LANES, 512):
        block = nn(inv_ref[...], ready_ref[:, at : at + 512])
        message_ref[:, at : at + 512] = block.astype(BF16)


def rows_forward_kernel(*refs):
    row_body(True, refs)


def rows_backward_kernel(*refs):
    row_body(False, refs)


def token_rows(received_ref, table_ref, place):
    for h in range(SLAB):
        place(h, 0, tn(received_ref[:, h * 128 : h * 128 + 128], table_ref[...]))
    for m in range(4):
        at = WIDE + 128 * m
        block = tn(received_ref[:, at : at + 128], table_ref[...])
        place(m, 128, block[:64])
        place(m + 4, 128, block[64:])


def tokens_kernel(received_ref, table_ref, filtered_ref, first_ref, last_ref):
    def place(h, channel, block):
        rows = block.astype(BF16)
        filtered_ref[h * CH + channel : h * CH + channel + block.shape[0]] = rows
        if h == 0:
            first_ref[channel : channel + block.shape[0]] = rows
        if h == SLAB - 1:
            last_ref[channel : channel + block.shape[0]] = rows

    token_rows(received_ref, table_ref, place)


def convolve(load, taps, put):
    lane = lax.broadcasted_iota(jnp.int32, (16, LEN), 1)
    window = [load(-1), load(0)]
    for h in range(SLAB):
        window.append(load(h + 1))
        sums = [sum(taps[3 * a + b] * window[a] for a in range(3)) for b in range(3)]
        left = jnp.where(lane == 0, 0.0, pltpu.roll(sums[0], 1, axis=1))
        right = jnp.where(lane == LEN - 1, 0.0, pltpu.roll(sums[2], LEN - 1, axis=1))
        put(h, sums[1] + left + right, window[1])
        window.pop(0)


def rows_at(h, start):
    return pl.ds(pl.multiple_of(h * CH + start, 16), 16)


def spread_taps(taps_ref, start, order):
    taps = taps_ref[pl.ds(start, 16), :]
    return [jnp.broadcast_to(taps[:, k : k + 1], (16, LEN)) for k in order]


def hidden_kernel(filtered_ref, above_ref, below_ref, taps_ref, signal_ref, hidden_ref):
    def chunk(index, carry):
        start = pl.multiple_of(index * 16, 16)

        def load(h):
            if h < 0:
                return above_ref[pl.ds(start, 16), :].astype(F32)
            if h == SLAB:
                return below_ref[pl.ds(start, 16), :].astype(F32)
            return filtered_ref[rows_at(h, start), :].astype(F32)

        def put(h, convolved, middle):
            at = rows_at(h, start)
            hidden_ref[at, :] = (signal_ref[at, :].astype(F32) + convolved).astype(BF16)

        convolve(load, spread_taps(taps_ref, start, range(9)), put)
        return carry

    lax.fori_loop(0, CH // 16, chunk, 0)


def gradient_columns_kernel(
    upstream_ref, mlp_ref, above_ref, below_ref, taps_ref, table_ref, message_ref, natural_ref, lanes_ref
):
    def chunk(index, carry):
        start = pl.multiple_of(index * 16, 16)

        def load(h):
            if h < 0:
                return above_ref[pl.ds(start, 16), :].astype(F32)
            if h == SLAB:
                return below_ref[pl.ds(start, 16), :].astype(F32)
            at = rows_at(h, start)
            return upstream_ref[at, :].astype(F32) + mlp_ref[at, :].astype(F32)

        def put(h, convolved, middle):
            natural_ref[rows_at(h, start), :] = convolved.astype(BF16)

        convolve(load, spread_taps(taps_ref, start, range(8, -1, -1)), put)
        return carry

    lax.fori_loop(0, CH // 16, chunk, 0)
    for h in range(SLAB):
        lanes_ref[h * 128 : h * 128 + 128] = natural_ref[h * CH : h * CH + 128]
        lanes_ref[narrow_at(h) : narrow_at(h) + 64] = natural_ref[h * CH + 128 : (h + 1) * CH]
    send_columns(table_ref, lanes_ref, message_ref)


def gelu_parts(pre_act):
    cumulative = 0.5 * (1.0 + lax.erf(pre_act * root_half))
    bell = density * jnp.exp(-0.5 * pre_act * pre_act)
    return pre_act * cumulative, cumulative + pre_act * bell


def mlp_kernel(
    hidden_ref,
    upstream_ref,
    gain_ref,
    unit_ref,
    mine_ref,
    other_ref,
    out_ref,
    grad_ref,
    gathered_ref,
    scaled_ref,
    dy_ref,
    normed_ref,
    inv_ref,
    out_sum_ref,
    grad_sum_ref,
):
    step = pl.program_id(0)

    def turn_in(source_ref, half):
        for src in range(CH_DEVICES):
            at = src * 2 * CH + half * CH
            gathered_ref[src * CH : (src + 1) * CH] = source_ref[at : at + CH]
        return nt(unit_ref[...], gathered_ref[...])

    @pl.when(step == 0)
    def _():
        for half in range(2):
            rows = slice(half * LEN, half * LEN + LEN)
            values = turn_in(hidden_ref, half)
            centred = values - jnp.mean(values, axis=1, keepdims=True)
            variance = jnp.mean(centred * centred, axis=1, keepdims=True)
            inv_std = lax.rsqrt(variance + norm_epsilon)
            normed = centred * inv_std
            normed_ref[rows] = normed
            inv_ref[rows] = jnp.broadcast_to(inv_std, (LEN, 128))
            scaled_ref[rows] = (normed * gain_ref[...]).astype(BF16)
            dy_ref[rows] = turn_in(upstream_ref, half).astype(BF16)
        out_sum_ref[...] = jnp.zeros_like(out_sum_ref)
        grad_sum_ref[...] = jnp.zeros_like(grad_sum_ref)

    for weights_ref in (mine_ref, other_ref):
        up, down = weights_ref[:, :ALL_CH], weights_ref[:, ALL_CH:]
        pre_act = nt(scaled_ref[...], up)
        grad_act = nt(dy_ref[...], down)
        activated, slope = gelu_parts(pre_act)
        out_sum_ref[...] += nn(activated.astype(BF16), down)
        grad_sum_ref[...] += nn((grad_act * slope).astype(BF16), up)

    def turn_out(values, half, target_ref):
        for block in range(3):
            piece = nt(unit_ref[...], values[:, block * LEN : (block + 1) * LEN])
            gathered_ref[block * LEN : (block + 1) * LEN] = piece.astype(BF16)
        for dst in range(CH_DEVICES):
            at = (dst * 2 + half) * CH
            target_ref[at : at + CH] = gathered_ref[dst * CH : (dst + 1) * CH]

    @pl.when(step == pl.num_programs(0) - 1)
    def _():
        for half in range(2):
            rows = slice(half * LEN, half * LEN + LEN)
            weighted = grad_sum_ref[rows] * gain_ref[...]
            normed = normed_ref[rows]
            first = jnp.mean(weighted, axis=1, keepdims=True)
            second = jnp.mean(weighted * normed, axis=1, keepdims=True)
            term = inv_ref[rows, 0:1] * (weighted - first - normed * second)
            turn_out(term.astype(BF16), half, grad_ref)
            turn_out(out_sum_ref[rows].astype(BF16), half, out_ref)


def mlp(hidden, upstream, gain, mine, other, block=256):
    tokens, units = 2 * LEN, CH_DEVICES * HALF_UNITS
    whole = pl.BlockSpec(memory_space=pltpu.VMEM)
    weights = pl.BlockSpec((block, 2 * ALL_CH), lambda i: (i, 0))
    return pl.pallas_call(
        mlp_kernel,
        name="mlp",
        grid=(units // block,),
        out_shape=(shape((LANES, LEN), BF16),) * 2,
        in_specs=[whole] * 4 + [weights] * 2,
        out_specs=(whole,) * 2,
        scratch_shapes=[
            pltpu.VMEM((ALL_CH, LEN), BF16),
            pltpu.VMEM((tokens, ALL_CH), BF16),
            pltpu.VMEM((tokens, ALL_CH), BF16),
            pltpu.VMEM((tokens, ALL_CH), F32),
            pltpu.VMEM((tokens, 128), F32),
            pltpu.VMEM((tokens, ALL_CH), F32),
            pltpu.VMEM((tokens, ALL_CH), F32),
        ],
        cost_estimate=pl.CostEstimate(
            flops=16 * tokens * units * ALL_CH,
            bytes_accessed=8 * units * ALL_CH + 8 * LANES * LEN,
            transcendentals=2 * tokens * units,
        ),
        compiler_params=pltpu.CompilerParams(vmem_limit_bytes=48 * MIB),
    )(hidden, upstream, gain, jnp.asarray(UNIT), mine, other)


def block_out_kernel(hidden_ref, sum_ref, out_ref, wide_ref):
    for h in range(SLAB):
        rows = slice(h * CH, (h + 1) * CH)
        total = hidden_ref[rows].astype(F32) + sum_ref[rows].astype(F32)
        put_eighth(wide_ref, h, total)
    out_ref[...] = take_wide(wide_ref).astype(BF16)


def image_kernel(received_ref, table_ref, upstream_ref, mlp_ref, out_ref, wide_ref):
    def place(h, channel, block):
        count = block.shape[0]
        rows = slice(h * CH + channel, h * CH + channel + count)
        total = block + upstream_ref[rows].astype(F32) + mlp_ref[rows].astype(F32)
        put_eighth(wide_ref, channel * SLAB + h, total)

    token_rows(received_ref, table_ref, place)
    out_ref[...] = take_wide(wide_ref)


def unturn_kernel(product_ref, straight_ref, mirrored_ref, own_ref, pair_ref, lone_ref, block_ref):
    def gather(part, column):
        rows = slice(column * 32, column * 32 + 32)
        for k2 in range(SLAB):
            to = slice(k2 * 32, k2 * 32 + 32)
            at = WIDE + 64 * k2
            block_ref[to, :128] = product_ref[part, rows, k2 * 128 : k2 * 128 + 128]
            block_ref[to, 128:] = product_ref[part, rows, at : at + 64]

    for part in range(2):
        sign = 1.0 if part == 0 else -1.0
        for j in range(4):
            gather(part, j)
            own_ref[j, part] = tn(block_ref[...], straight_ref[...]).astype(BF16)
            pair_ref[3 - j, part] = (tn(block_ref[...], mirrored_ref[...]) * sign).astype(BF16)
        gather(part, 4)
        lone_ref[part] = (tn(block_ref[...], mirrored_ref[...]) * sign).astype(BF16)


def grad_filter_kernel(place_ref, own_ref, pair_ref, lone_ref, out_ref, wide_ref):
    low = place_ref[0] < 16
    for part in range(2):
        parts = [jnp.where(low, lone_ref[part], own_ref[3, part])]
        parts += [own_ref[j, part] for j in range(3)]
        parts += [jnp.where(low, own_ref[3, part], pair_ref[0, part])]
        parts += [pair_ref[n, part] for n in range(1, 4)]
        for i, value in enumerate(parts):
            put_eighth(wide_ref, i, value.astype(F32))
        out_ref[part] = take_wide(wide_ref)


def to_peers(values, axis):
    return lax.all_to_all(values, axis, split_axis=0, concat_axis=0, tiled=True)


def halo(first, last):
    down = [(i, i + 1) for i in range(ROWS_DEVICES - 1)]
    up = [(i + 1, i) for i in range(ROWS_DEVICES - 1)]
    return lax.ppermute(last, "rows", down), lax.ppermute(first, "rows", up)


def on_device(tile_image, spectral_filter, conv_taps, norm_gain, up_weight, down_weight, upstream):
    device = lax.axis_index("rows")
    place = device.reshape(1).astype(jnp.int32)
    flat = (LANES, LEN)
    tables = [jnp.asarray(t) for t in (FORWARD_ROWS, INVERSE_ROWS, TWIDDLE_COS, TWIDDLE_SIN)]
    forward_columns, inverse_columns = jnp.asarray(FORWARD_COLUMNS), jnp.asarray(INVERSE_COLUMNS)
    straight, mirrored = jnp.asarray(STRAIGHT), jnp.asarray(MIRRORED)

    start = lax.rem(device, 2) * HALF_UNITS
    own_up = lax.dynamic_slice_in_dim(up_weight, start, HALF_UNITS, axis=1).T
    own_down = lax.dynamic_slice_in_dim(down_weight, start, HALF_UNITS, axis=0)
    mine = lax.all_gather(jnp.concatenate([own_up, own_down], axis=1), "ch", axis=0, tiled=True)
    other = lax.ppermute(mine, "rows", [(i, i ^ 1) for i in range(ROWS_DEVICES)])

    wide = pltpu.VMEM((2, LANES, 128), F32)
    lanes = pltpu.VMEM(flat, BF16)
    message, signal = kernel_call(
        columns_kernel,
        "columns",
        [shape((LEN, LANES), BF16), shape(flat, BF16)],
        [wide, lanes],
        [tile_image.reshape(flat), forward_columns],
        24,
        2 * LEN * LEN * LANES,
    )
    received = to_peers(message, "rows")
    (dy,) = kernel_call(
        unfold_kernel, "unfold", [shape(flat, BF16)], [wide], [upstream.reshape(flat)], 16
    )
    (own_filter,) = kernel_call(
        filter_split_kernel,
        "filter_split",
        [shape((SLAB, 2, CH, LEN), BF16)],
        [wide],
        [spectral_filter.reshape(2, LANES, LEN)],
        24,
    )
    opposite = [(i, ROWS_DEVICES - 1 - i) for i in range(ROWS_DEVICES)]
    lone_in = [(i, ROWS_DEVICES - i) for i in range(1, 16)] + [(0, 16)]
    pair_filter = lax.ppermute(own_filter[4:], "rows", opposite)
    lone_filter = lax.ppermute(own_filter[0], "rows", lone_in)
    main, cross = kernel_call(
        filter_kernel,
        "filter",
        [shape((2, 128, LANES), F32), shape((2, 32, LANES), F32)],
        [],
        [place, own_filter, pair_filter, lone_filter, straight, mirrored],
        32,
        2 * 14 * LEN * LEN * CH,
        smem=1,
    )
    dy_tokens = to_peers(dy, "ch")

    row_scratch = [pltpu.VMEM((320, LANES), F32), pltpu.VMEM((LEN, LANES), BF16)]
    message, seen = kernel_call(
        rows_forward_kernel,
        "rows_forward",
        [shape((LEN, LANES), BF16), shape((2, 160, LANES), BF16)],
        row_scratch,
        [place, received, *tables, main, cross],
        24,
        2 * 576 * LEN * LANES,
        smem=1,
    )
    received = to_peers(message, "rows")
    filtered, first, last = kernel_call(
        tokens_kernel,
        "tokens",
        [shape(flat, BF16), shape((CH, LEN), BF16), shape((CH, LEN), BF16)],
        [],
        [received, inverse_columns],
        24,
        2 * LEN * LEN * LANES,
    )
    above, below = halo(first, last)
    (hidden,) = kernel_call(
        hidden_kernel,
        "hidden",
        [shape(flat, BF16)],
        [],
        [filtered, above, below, conv_taps, signal],
        24,
    )
    hidden_tokens = to_peers(hidden, "ch")
    out_message, grad_message = mlp(
        hidden_tokens, dy_tokens, norm_gain.reshape(1, ALL_CH), mine, other
    )
    grad_mlp = to_peers(grad_message, "ch")
    edges = [
        (dy[at].astype(F32) + grad_mlp[at].astype(F32)).astype(BF16)
        for at in (slice(0, CH), slice(LANES - CH, LANES))
    ]
    above, below = halo(*edges)
    (message,) = kernel_call(
        gradient_columns_kernel,
        "gradient_columns",
        [shape((LEN, LANES), BF16)],
        [lanes, lanes],
        [dy, grad_mlp, above, below, conv_taps, forward_columns],
        24,
        2 * LEN * LEN * LANES,
    )
    received = to_peers(message, "rows")
    out_sum = to_peers(out_message, "ch")
    (block_out,) = kernel_call(
        block_out_kernel, "block_out", [shape(flat, BF16)], [wide], [hidden, out_sum], 24
    )
    message, products = kernel_call(
        rows_backward_kernel,
        "rows_backward",
        [shape((LEN, LANES), BF16), shape((2, 160, LANES), BF16)],
        row_scratch,
        [place, received, *tables, main, cross, seen],
        24,
        2 * 576 * LEN * LANES,
        smem=1,
    )
    received = to_peers(message, "rows")
    own, pair, lone = kernel_call(
        unturn_kernel,
        "unturn",
        [shape((4, 2, CH, LEN), BF16), shape((4, 2, CH, LEN), BF16), shape((2, CH, LEN), BF16)],
        [pltpu.VMEM((LEN, CH), BF16)],
        [products, straight, mirrored],
        24,
        2 * 18 * LEN * LEN * CH,
    )
    pair = lax.ppermute(pair, "rows", opposite)
    lone = lax.ppermute(lone, "rows", [(b, a) for a, b in lone_in])
    (grad_filter,) = kernel_call(
        grad_filter_kernel,
        "grad_filter",
        [shape((2, LANES, LEN), F32)],
        [wide],
        [place, own, pair, lone],
        24,
        smem=1,
    )
    (grad_image,) = kernel_call(
        image_kernel,
        "image",
        [shape(flat, F32)],
        [wide],
        [received, inverse_columns, dy, grad_mlp],
        24,
        2 * LEN * LEN * LANES,
    )
    slab = (CH, SLAB, LEN)
    return (
        block_out.reshape(slab),
        grad_image.reshape(slab),
        grad_filter.reshape(2, CH, SLAB, LEN),
    )


def solution(mesh):
    return jax.shard_map(
        on_device,
        mesh=mesh,
        in_specs=(
            P("ch", "rows", None),
            P(None, "ch", "rows", None),
            P("ch", None),
            P(),
            P(None, "ch"),
            P("ch", None),
            P("ch", "rows", None),
        ),
        out_specs=(P("ch", "rows", None), P("ch", "rows", None), P(None, "ch", "rows", None)),
        check_vma=False,
    )
```

```python
import functools

import jax
import jax.numpy as jnp
import ml_dtypes
import numpy as np
from jax import lax
from jax.experimental import pallas as pl
from jax.experimental.pallas import tpu as pltpu
from jax.sharding import PartitionSpec as P

norm_epsilon = 1e-05
root_half = 0.7071067811865476
density = 0.3989422804014327

ROWS_DEVICES = 32
CH_DEVICES = 4
LEN = 256
SLAB = 8
CH = 192
ALL_CH = 768
LANES = SLAB * CH
WIDE = SLAB * 128
POINTS = LEN * LEN
HALF_UNITS = 384
UNITS = 3072
ROWS = ("y", "z", "core")
SENT = (SLAB + 2) * CH
F32 = jnp.float32
BF16 = jnp.bfloat16
MIB = 1 << 20


def wide_at(h):
    return {-1: LANES, SLAB: LANES + 128}.get(h, 128 * h)


def narrow_at(h):
    return {-1: LANES + 256, SLAB: LANES + 320}.get(h, WIDE + 64 * (2 * (h % 4) + h // 4))


def columns_of(device):
    base = SLAB * device
    return [base + 1, base + 2, base + 3, base + 4 if device < 16 else base]


def column_tables():
    w = np.arange(LEN)
    forward, inverse = np.zeros((LEN, LEN)), np.zeros((LEN, LEN))
    for device in range(ROWS_DEVICES):
        for j, kw in enumerate(columns_of(device)):
            turn = 2 * np.pi * (kw * w % LEN) / LEN
            re, im = SLAB * device + j, SLAB * device + 4 + j
            if device == 16 and j == 3:
                forward[re] = inverse[re] = 1.0
                forward[im] = inverse[im] = np.where(w % 2 == 0, 1.0, -1.0)
            else:
                forward[re], forward[im] = np.cos(turn), -np.sin(turn)
                inverse[re], inverse[im] = 2 * np.cos(turn), -2 * np.sin(turn)
    return forward, inverse


def row_tables():
    k1, src = np.arange(32)[:, None], np.arange(32)[None, :]
    turn = 2 * np.pi * (k1 * src % 32) / 32
    cos, sin = np.cos(turn), np.sin(turn)
    forward = np.zeros((2, 5, 32, 32, 2, 4))
    inverse = np.zeros((32, 2, 4, 2, 4, 32))
    for j in range(4):
        forward[0, j, :, :, 0, j], forward[0, j, :, :, 1, j] = cos, sin
        forward[1, j, :, :, 0, j], forward[1, j, :, :, 1, j] = -sin, cos
        inverse[:, 0, j, 0, j, :], inverse[:, 0, j, 1, j, :] = cos.T, -sin.T
        inverse[:, 1, j, 0, j, :], inverse[:, 1, j, 1, j, :] = sin.T, cos.T
    forward[0, 4, :, :, 0, 3], forward[0, 4, :, :, 1, 3] = cos, -sin
    forward[1, 4, :, :, 0, 3], forward[1, 4, :, :, 1, 3] = -sin, -cos
    return forward.reshape(320, 256), inverse.reshape(256, 256)


def twiddle_tables():
    token_row = np.zeros(LANES, np.int64)
    for h in range(SLAB):
        token_row[128 * h : 128 * h + 128] = h
        token_row[narrow_at(h) : narrow_at(h) + 64] = h
    turn = 2 * np.pi * (np.arange(32)[:, None] * token_row[None, :] % LEN) / LEN
    return np.cos(turn), np.sin(turn)


def turn_tables():
    k2, k1 = np.divmod(np.arange(LEN), 32)
    kh = k1 + 32 * k2
    straight, mirrored = np.zeros((LEN, LEN)), np.zeros((LEN, LEN))
    straight[np.arange(LEN), kh] = 1.0
    mirrored[np.arange(LEN), -kh % LEN] = 1.0
    return straight, mirrored


def narrow(table):
    return np.asarray(table, np.float64).astype(ml_dtypes.bfloat16)


FORWARD_COLUMNS, INVERSE_COLUMNS = (narrow(t) for t in column_tables())
FORWARD_ROWS, INVERSE_ROWS = (narrow(t) for t in row_tables())
TWIDDLE_COS, TWIDDLE_SIN = (t.astype(np.float32) for t in twiddle_tables())
STRAIGHT, MIRRORED = (narrow(t) for t in turn_tables())
UNIT = narrow(np.eye(LEN))


def nn(a, b):
    return lax.dot_general(a, b, (((1,), (0,)), ((), ())), preferred_element_type=F32)


def nt(a, b):
    return lax.dot_general(a, b, (((1,), (1,)), ((), ())), preferred_element_type=F32)


def tn(a, b):
    return lax.dot_general(a, b, (((0,), (0,)), ((), ())), preferred_element_type=F32)


def whole_block(dims):
    return pl.BlockSpec(dims, lambda *_: (0,) * len(dims), pipeline_mode=pl.Buffered(1))


def kernel_call(body, name, outs, scratch, operands, vmem, flops=0, smem=0, hint=0):
    scalar = pl.BlockSpec(memory_space=pltpu.SMEM)
    moved = sum(a.size * a.dtype.itemsize for a in operands)
    moved += sum(o.size * np.dtype(o.dtype).itemsize for o in outs)
    return pl.pallas_call(
        body,
        name=name,
        grid=(1,),
        out_shape=tuple(outs),
        in_specs=[scalar] * smem + [whole_block(a.shape) for a in operands[smem:]],
        out_specs=tuple(whole_block(o.shape) for o in outs),
        scratch_shapes=scratch,
        cost_estimate=pl.CostEstimate(
            flops=flops + hint * 10**9, bytes_accessed=moved, transcendentals=0
        ),
        compiler_params=pltpu.CompilerParams(vmem_limit_bytes=vmem * MIB),
    )(*operands)


def shape(dims, dtype):
    return jax.ShapeDtypeStruct(dims, dtype)


def fill_wide(wide_ref, values):
    for side in range(2):
        wide_ref[side] = values[:, side * 128 : side * 128 + 128]


def every_eighth(wide_ref, h):
    return jnp.concatenate([wide_ref[side, pl.ds(h, CH, stride=SLAB), :] for side in range(2)], axis=1)


def put_eighth(wide_ref, first, values):
    for side in range(2):
        at = pl.ds(first, values.shape[0], stride=SLAB)
        wide_ref[side, at, :] = values[:, side * 128 : side * 128 + 128]


def take_wide(wide_ref):
    return jnp.concatenate([wide_ref[side] for side in range(2)], axis=1)


def unfold_rows(source_ref, wide_ref):
    fill_wide(wide_ref, source_ref[...].astype(F32))
    for h in range(SLAB):
        yield h, every_eighth(wide_ref, h).astype(BF16)


def columns_kernel(image_ref, table_ref, message_ref, kept_ref, wide_ref, lanes_ref):
    for h, rows in unfold_rows(image_ref, wide_ref):
        kept_ref[h * CH : (h + 1) * CH] = rows
        lanes_ref[h * 128 : h * 128 + 128] = rows[:128]
        lanes_ref[narrow_at(h) : narrow_at(h) + 64] = rows[128:]
    send_columns(table_ref, lanes_ref, message_ref)


def send_columns(table_ref, lanes_ref, message_ref):
    for at in range(0, lanes_ref.shape[0], 384):
        message_ref[:, at : at + 384] = nt(table_ref[...], lanes_ref[at : at + 384]).astype(BF16)


def unfold_kernel(channel_ref, source_ref, kept_ref, *refs):
    *turned_refs, wide_ref = refs
    for h, rows in unfold_rows(source_ref, wide_ref):
        kept_ref[h * CH : (h + 1) * CH] = rows
    for turn, turned_ref in enumerate(turned_refs):
        peer = lax.rem(channel_ref[0] + turn, CH_DEVICES)
        for half in range(2):
            rows = every_eighth(wide_ref, peer * 2 + half)
            turned_ref[half * CH : half * CH + CH] = rows.astype(BF16)


def filter_split_kernel(filter_ref, head_ref, tail_ref, lone_ref, wide_ref):
    for part in range(2):
        fill_wide(wide_ref, filter_ref[part])
        for i in range(4):
            tail_ref[i, part] = every_eighth(wide_ref, 4 + i).astype(BF16)
            head_ref[i, part] = every_eighth(wide_ref, i).astype(BF16)
        lone_ref[part] = head_ref[0, part]


def put_spectrum(target_ref, part, column, block):
    rows = slice(column * 32, column * 32 + 32)
    for k2 in range(SLAB):
        piece = block[k2 * 32 : k2 * 32 + 32]
        target_ref[part, rows, k2 * 128 : k2 * 128 + 128] = piece[:, :128]
        at = WIDE + 64 * k2
        target_ref[part, rows, at : at + 64] = piece[:, 128:]


def filter_kernel(
    place_ref, head_ref, tail_ref, pair_ref, lone_ref, straight_ref, mirrored_ref, main_ref, cross_ref
):
    device = place_ref[0]
    low, special = device < 16, device == 16
    scale = 0.5 / POINTS
    for part in range(2):
        sign = 1.0 if part == 0 else -1.0
        for j in range(3):
            straight = nt(straight_ref[...], head_ref[1 + j, part])
            mirrored = nt(mirrored_ref[...], pair_ref[3 - j, part])
            put_spectrum(main_ref, part, j, (straight + sign * mirrored) * scale)
        own = jnp.where(low, tail_ref[0, part], head_ref[0, part])
        other = jnp.where(low, pair_ref[0, part], lone_ref[part])
        o, q = nt(straight_ref[...], own), nt(straight_ref[...], other)
        o_back = nt(mirrored_ref[...], own) * sign
        q_back = nt(mirrored_ref[...], other) * sign
        usual = (o + q_back) * scale
        put_spectrum(
            main_ref, part, 3, jnp.where(special, (o + o_back + q + q_back) * (0.5 * scale), usual)
        )
        put_spectrum(
            cross_ref,
            part,
            0,
            jnp.where(special, (q + q_back - o - o_back) * (0.5 * scale), 0.0 * usual),
        )


def eighth_turn(value, step, sign):
    re, im = value
    if step == 0:
        return value
    if step == 1:
        return (re + sign * im) * root_half, (im - sign * re) * root_half
    if step == 2:
        return sign * im, -sign * re
    return (sign * im - re) * root_half, (-sign * re - im) * root_half


def add(a, b):
    return a[0] + b[0], a[1] + b[1]


def sub(a, b):
    return a[0] - b[0], a[1] - b[1]


def four_points(x, sign):
    s, d = add(x[0], x[2]), sub(x[0], x[2])
    t, u = add(x[1], x[3]), eighth_turn(sub(x[1], x[3]), 2, sign)
    return [add(s, t), add(d, u), sub(s, t), sub(d, u)]


def eight_points(x, sign):
    even = four_points([add(x[m], x[m + 4]) for m in range(4)], sign)
    odd = four_points([eighth_turn(sub(x[m], x[m + 4]), m, sign) for m in range(4)], sign)
    return [part[q] for q in range(4) for part in (even, odd)]


def upper_lanes(like):
    return lax.broadcasted_iota(jnp.int32, like.shape, 1) >= 64


def halves(value):
    upper = upper_lanes(value)
    return pltpu.roll(value, 64, axis=1) + jnp.where(upper, -value, value)


def upper_turn(value, step, sign):
    upper = upper_lanes(value[0])
    return tuple(jnp.where(upper, b, a) for a, b in zip(value, eighth_turn(value, step, sign)))


def narrow_forward(x, sign):
    turned = [upper_turn((halves(re), halves(im)), m, sign) for m, (re, im) in enumerate(x)]
    return four_points(turned, sign)


def narrow_inverse(x, sign):
    turned = [upper_turn(v, m, sign) for m, v in enumerate(four_points(x, sign))]
    return [(halves(re), halves(im)) for re, im in turned]


def lane_blocks(re, im):
    return [(re[:, at : at + 128], im[:, at : at + 128]) for at in range(0, LANES, 128)]


def to_frequencies(re, im, cos, sin):
    x = lane_blocks(re * cos + im * sin, im * cos - re * sin)
    return eight_points(x[:SLAB], 1.0) + narrow_forward(x[SLAB:], 1.0)


def to_tokens_rows(blocks, cos, sin):
    y = eight_points(blocks[:SLAB], -1.0) + narrow_inverse(blocks[SLAB:], -1.0)
    re = jnp.concatenate([v[0] for v in y], axis=1)
    im = jnp.concatenate([v[1] for v in y], axis=1)
    return re * cos - im * sin, im * cos + re * sin


def moved_rows(block, step):
    empty = jnp.zeros((SLAB, block.shape[1]), block.dtype)
    if step > 0:
        return jnp.concatenate([empty, block[:-SLAB]], axis=0)
    return jnp.concatenate([block[SLAB:], empty], axis=0)


def row_body(saves, refs):
    place_ref, received_ref, fwd_ref, inv_ref, cos_ref, sin_ref, main_ref, cross_ref = refs[:8]
    if saves:
        message_ref, seen_ref, mixed_ref, ready_ref = refs[8:]
    else:
        seen_ref, message_ref, product_ref, mixed_ref, ready_ref = refs[8:]

    def joined(at, width, edge, step):
        rows = received_ref[:, at : at + width].astype(F32)
        moved = moved_rows(received_ref[:, edge : edge + width].astype(F32), step)
        return nn(fwd_ref[...], (rows + moved).astype(BF16))

    for at in range(0, LANES, 512):
        mixed_ref[:, at : at + 512] = nn(fwd_ref[...], received_ref[:, at : at + 512])
    if not saves:
        for h, edge, step in ((0, SLAB, 1), (SLAB - 1, -1, -1)):
            at = wide_at(h)
            mixed_ref[:, at : at + 128] = joined(at, 128, wide_at(edge), step)
            at = narrow_at(h)
            mixed_ref[:, at : at + 64] = joined(at, 64, narrow_at(edge), step)

    def spectrum(group):
        at = pl.multiple_of(group * 16, 16)
        table = pl.ds(pl.multiple_of(lax.rem(group, 2) * 16, 16), 16)
        return to_frequencies(
            mixed_ref[pl.ds(at, 16), :],
            mixed_ref[pl.ds(160 + at, 16), :],
            cos_ref[table, :],
            sin_ref[table, :],
        )

    def save(group, blocks):
        at = pl.ds(pl.multiple_of(group * 16, 16), 16)
        for n, value in enumerate(blocks):
            for part in range(2):
                seen_ref[part, at, n * 128 : n * 128 + 128] = value[part].astype(BF16)

    def times(value, n, source_ref, at):
        k_re = source_ref[0, at, n * 128 : n * 128 + 128]
        k_im = source_ref[1, at, n * 128 : n * 128 + 128]
        re, im = value
        if saves:
            return re * k_re - im * k_im, im * k_re + re * k_im
        return re * k_re + im * k_im, im * k_re - re * k_im

    def store_back(group, blocks):
        table = pl.ds(pl.multiple_of(lax.rem(group, 2) * 16, 16), 16)
        re, im = to_tokens_rows(blocks, cos_ref[table, :], sin_ref[table, :])
        at = pl.multiple_of(group * 16, 16)
        ready_ref[pl.ds(at, 16), :] = re.astype(BF16)
        ready_ref[pl.ds(128 + at, 16), :] = im.astype(BF16)

    def seen(group, n):
        at = pl.ds(pl.multiple_of(group * 16, 16), 16)
        return tuple(seen_ref[part, at, n * 128 : n * 128 + 128].astype(F32) for part in range(2))

    def product(a, b, factor):
        re = (a[0] * b[0] + a[1] * b[1]) * factor
        return re, (b[1] * a[0] - b[0] * a[1]) * factor

    def put_product(group, n, value):
        at = pl.ds(pl.multiple_of(group * 16, 16), 16)
        for part in range(2):
            product_ref[part, at, n * 128 : n * 128 + 128] = value[part].astype(BF16)

    def plain(group, carry):
        at = pl.ds(pl.multiple_of(group * 16, 16), 16)
        values = spectrum(group)
        if saves:
            save(group, values)
        else:
            for n, value in enumerate(values):
                put_product(group, n, product(seen(group, n), value, 1.0 / POINTS))
        store_back(group, [times(v, n, main_ref, at) for n, v in enumerate(values)])
        return carry

    def packed(group, carry):
        at = pl.ds(pl.multiple_of(group * 16, 16), 16)
        cross_at = pl.ds(pl.multiple_of((group - 6) * 16, 16), 16)
        values, mirrors = spectrum(group), spectrum(group + 2)
        if saves:
            save(group, values)
            save(group + 2, mirrors)
        else:
            special = place_ref[0] == 16
            for n, (value, mirror) in enumerate(zip(values, mirrors)):
                first, first_mirror = seen(group, n), seen(group + 2, n)
                usual = product(first, value, 1.0 / POINTS)
                odd = product(sub(first, first_mirror), sub(value, mirror), 0.25 / POINTS)
                even = product(add(first, first_mirror), add(value, mirror), 0.25 / POINTS)
                put_product(group, n, [jnp.where(special, a, b) for a, b in zip(odd, usual)])
                put_product(group + 2, n, [jnp.where(special, a, b) for a, b in zip(even, usual)])
        store_back(
            group,
            [
                add(times(v, n, main_ref, at), times(m, n, cross_ref, cross_at))
                for n, (v, m) in enumerate(zip(values, mirrors))
            ],
        )
        return carry

    lax.fori_loop(0, 6, plain, 0)
    lax.fori_loop(6, 8, packed, 0)
    for at in range(0, LANES, 512):
        block = nn(inv_ref[...], ready_ref[:, at : at + 512])
        message_ref[:, at : at + 512] = block.astype(BF16)
        if saves:
            for h, edge, step in ((0, SLAB, -1), (SLAB - 1, -1, 1)):
                for place, width in ((wide_at, 128), (narrow_at, 64)):
                    start = place(h) - at
                    if 0 <= start < 512:
                        moved = moved_rows(block[:, start : start + width], step)
                        message_ref[:, place(edge) : place(edge) + width] = moved.astype(BF16)


def rows_forward_kernel(*refs):
    row_body(True, refs)


def rows_backward_kernel(*refs):
    row_body(False, refs)


def token_rows(received_ref, table_ref, place):
    for h in range(SLAB):
        place(h, 0, tn(received_ref[:, h * 128 : h * 128 + 128], table_ref[...]))
    for m in range(4):
        at = WIDE + 128 * m
        block = tn(received_ref[:, at : at + 128], table_ref[...])
        place(m, 128, block[:64])
        place(m + 4, 128, block[64:])


def convolve(load, rows, taps, put):
    lane = lax.broadcasted_iota(jnp.int32, (16, LEN), 1)
    window = [load(rows[0] - 1), load(rows[0])]
    for h in rows:
        window.append(load(h + 1))
        sums = []
        for b in range(3):
            terms = [taps[3 * a + b] * w for a, w in enumerate(window) if w is not None]
            sums.append(sum(terms[1:], terms[0]))
        left = jnp.where(lane == 0, 0.0, pltpu.roll(sums[0], 1, axis=1))
        right = jnp.where(lane == LEN - 1, 0.0, pltpu.roll(sums[2], LEN - 1, axis=1))
        put(h, sums[1] + left + right)
        window.pop(0)


def every_chunk(body):
    def wide(index, carry):
        at = pl.multiple_of(index * 16, 16)
        body(at, lambda h: pl.ds(pl.multiple_of(wide_at(h) + at, 16), 16))
        return carry

    def last(index, carry):
        at = pl.multiple_of(index * 16, 16)
        body(at + 128, lambda h: pl.ds(pl.multiple_of(narrow_at(h) + at, 16), 16))
        return carry

    lax.fori_loop(0, 8, wide, 0)
    lax.fori_loop(0, 4, last, 0)


def rows_at(h, start):
    return pl.ds(pl.multiple_of(h * CH + start, 16), 16)


def spread_taps(taps_ref, start, order):
    taps = taps_ref[pl.ds(pl.multiple_of(start, 16), 16), :]
    return [jnp.broadcast_to(taps[:, k : k + 1], (16, LEN)) for k in order]


def hidden_kernel(received_ref, table_ref, taps_ref, signal_ref, hidden_ref, filtered_ref):
    for at in range(0, SENT, 128):
        block = tn(received_ref[:, at : at + 128], table_ref[...])
        filtered_ref[at : at + 128] = block.astype(BF16)

    def chunk(start, place):
        def load(h):
            return filtered_ref[place(h), :].astype(F32)

        def put(h, convolved):
            at = rows_at(h, start)
            hidden_ref[at, :] = (signal_ref[at, :].astype(F32) + convolved).astype(BF16)

        convolve(load, range(SLAB), spread_taps(taps_ref, start, range(9)), put)

    every_chunk(chunk)


def gradient_columns_kernel(upstream_ref, mlp_ref, taps_ref, table_ref, message_ref, lanes_ref):
    def chunk(start, place):
        def load(h):
            if h < 0 or h >= SLAB:
                return None
            at = rows_at(h, start)
            return upstream_ref[at, :].astype(F32) + mlp_ref[at, :].astype(F32)

        def put(h, convolved):
            lanes_ref[place(h), :] = convolved.astype(BF16)

        convolve(
            load, range(-1, SLAB + 1), spread_taps(taps_ref, start, range(8, -1, -1)), put
        )

    every_chunk(chunk)
    send_columns(table_ref, lanes_ref, message_ref)


def gelu_parts(pre_act):
    cumulative = 0.5 * (1.0 + lax.erf(pre_act * root_half))
    bell = density * jnp.exp(-0.5 * pre_act * pre_act)
    return pre_act * cumulative, cumulative + pre_act * bell


def mlp_kernel(
    channel_ref,
    hidden_ref,
    own_dy_ref,
    dy_one_ref,
    dy_two_ref,
    dy_three_ref,
    gain_ref,
    unit_ref,
    mine_ref,
    other_ref,
    out_own_ref,
    out_one_ref,
    out_two_ref,
    out_three_ref,
    grad_ref,
    parts_ref,
    gathered_ref,
    scaled_ref,
    dy_ref,
    normed_ref,
    inv_ref,
    out_sum_ref,
    grad_sum_ref,
):
    step = pl.program_id(0)
    channel = channel_ref[0]

    def turn_in(half):
        for src in range(CH_DEVICES):
            at = src * 2 * CH + half * CH
            gathered_ref[src * CH : (src + 1) * CH] = hidden_ref[at : at + CH]
        return nt(unit_ref[...], gathered_ref[...])

    def turn_in_dy(half):
        for src in range(CH_DEVICES):
            gathered_ref[src * CH : (src + 1) * CH] = parts_ref[src, half * CH : half * CH + CH]
        return nt(unit_ref[...], gathered_ref[...])

    @pl.when(step == 0)
    def _():
        for turn, source_ref in enumerate((own_dy_ref, dy_one_ref, dy_two_ref, dy_three_ref)):
            parts_ref[lax.rem(channel + CH_DEVICES - turn, CH_DEVICES)] = source_ref[...]
        for half in range(2):
            rows = slice(half * LEN, half * LEN + LEN)
            values = turn_in(half)
            centred = values - jnp.mean(values, axis=1, keepdims=True)
            variance = jnp.mean(centred * centred, axis=1, keepdims=True)
            inv_std = lax.rsqrt(variance + norm_epsilon)
            normed = centred * inv_std
            normed_ref[rows] = normed
            inv_ref[rows] = jnp.broadcast_to(inv_std, (LEN, 128))
            scaled_ref[rows] = (normed * gain_ref[...]).astype(BF16)
            dy_ref[rows] = turn_in_dy(half).astype(BF16)
        out_sum_ref[...] = jnp.zeros_like(out_sum_ref)
        grad_sum_ref[...] = jnp.zeros_like(grad_sum_ref)

    for weights_ref in (mine_ref, other_ref):
        up, down = weights_ref[:, :ALL_CH], weights_ref[:, ALL_CH:]
        pre_act = nt(scaled_ref[...], up)
        grad_act = nt(dy_ref[...], down)
        activated, slope = gelu_parts(pre_act)
        out_sum_ref[...] += nn(activated.astype(BF16), down)
        grad_sum_ref[...] += nn((grad_act * slope).astype(BF16), up)

    def turn_out(values, half, put):
        for block in range(3):
            piece = nt(unit_ref[...], values[:, block * LEN : (block + 1) * LEN])
            gathered_ref[block * LEN : (block + 1) * LEN] = piece.astype(BF16)
        for dst in range(CH_DEVICES):
            put(dst, half, gathered_ref[dst * CH : (dst + 1) * CH])

    def put_grad(dst, half, rows):
        at = (dst * 2 + half) * CH
        grad_ref[at : at + CH] = rows

    def put_out(dst, half, rows):
        parts_ref[dst, half * CH : half * CH + CH] = rows

    @pl.when(step == pl.num_programs(0) - 1)
    def _():
        for half in range(2):
            rows = slice(half * LEN, half * LEN + LEN)
            weighted = grad_sum_ref[rows] * gain_ref[...]
            normed = normed_ref[rows]
            first = jnp.mean(weighted, axis=1, keepdims=True)
            second = jnp.mean(weighted * normed, axis=1, keepdims=True)
            term = inv_ref[rows, 0:1] * (weighted - first - normed * second)
            turn_out(term.astype(BF16), half, put_grad)
            turn_out(out_sum_ref[rows].astype(BF16), half, put_out)
        for turn, out_ref in enumerate((out_own_ref, out_one_ref, out_two_ref, out_three_ref)):
            out_ref[...] = parts_ref[lax.rem(channel + turn, CH_DEVICES)]


def mlp(channel, hidden, dy_parts, gain, weights, block=256):
    tokens, steps = 2 * LEN, UNITS // 2 // block
    part = whole_block((2 * CH, LEN))
    return pl.pallas_call(
        mlp_kernel,
        name="mlp",
        grid=(steps,),
        out_shape=(*(shape((2 * CH, LEN), BF16),) * CH_DEVICES, shape((LANES, LEN), BF16)),
        in_specs=[
            pl.BlockSpec(memory_space=pltpu.SMEM),
            whole_block((LANES, LEN)),
            part,
            part,
            part,
            part,
            whole_block((1, ALL_CH)),
            whole_block((LEN, LEN)),
            pl.BlockSpec((block, 2 * ALL_CH), lambda i: (i, 0)),
            pl.BlockSpec((block, 2 * ALL_CH), lambda i: (i + steps, 0)),
        ],
        out_specs=(part, part, part, part, whole_block((LANES, LEN))),
        scratch_shapes=[
            pltpu.VMEM((CH_DEVICES, 2 * CH, LEN), BF16),
            pltpu.VMEM((ALL_CH, LEN), BF16),
            pltpu.VMEM((tokens, ALL_CH), BF16),
            pltpu.VMEM((tokens, ALL_CH), BF16),
            pltpu.VMEM((tokens, ALL_CH), F32),
            pltpu.VMEM((tokens, 128), F32),
            pltpu.VMEM((tokens, ALL_CH), F32),
            pltpu.VMEM((tokens, ALL_CH), F32),
        ],
        cost_estimate=pl.CostEstimate(
            flops=8 * tokens * UNITS * ALL_CH,
            bytes_accessed=4 * UNITS * ALL_CH + 8 * LANES * LEN,
            transcendentals=2 * tokens * UNITS,
        ),
        compiler_params=pltpu.CompilerParams(vmem_limit_bytes=28 * MIB),
    )(channel, hidden, *dy_parts, gain, jnp.asarray(UNIT), weights, weights)


def block_out_kernel(channel_ref, hidden_ref, own_ref, one_ref, two_ref, three_ref, out_ref, wide_ref):
    for turn, sum_ref in enumerate((own_ref, one_ref, two_ref, three_ref)):
        src = lax.rem(channel_ref[0] + CH_DEVICES - turn, CH_DEVICES)
        for half in range(2):
            rows = pl.ds(pl.multiple_of((src * 2 + half) * CH, 64), CH)
            total = hidden_ref[rows, :].astype(F32)
            total += sum_ref[half * CH : half * CH + CH].astype(F32)
            put_eighth(wide_ref, src * 2 + half, total)
    out_ref[...] = take_wide(wide_ref).astype(BF16)


def image_kernel(received_ref, table_ref, upstream_ref, mlp_ref, out_ref, wide_ref):
    def place(h, channel, block):
        count = block.shape[0]
        rows = slice(h * CH + channel, h * CH + channel + count)
        total = block + upstream_ref[rows].astype(F32) + mlp_ref[rows].astype(F32)
        put_eighth(wide_ref, channel * SLAB + h, total)

    token_rows(received_ref, table_ref, place)
    out_ref[...] = take_wide(wide_ref)


def unturn_kernel(product_ref, straight_ref, mirrored_ref, own_ref, pair_ref, lone_ref, block_ref):
    def gather(part, column):
        rows = slice(column * 32, column * 32 + 32)
        for k2 in range(SLAB):
            to = slice(k2 * 32, k2 * 32 + 32)
            at = WIDE + 64 * k2
            block_ref[to, :128] = product_ref[part, rows, k2 * 128 : k2 * 128 + 128]
            block_ref[to, 128:] = product_ref[part, rows, at : at + 64]

    for part in range(2):
        sign = 1.0 if part == 0 else -1.0
        for j in range(4):
            gather(part, j)
            own_ref[j, part] = tn(block_ref[...], straight_ref[...]).astype(BF16)
            pair_ref[3 - j, part] = (tn(block_ref[...], mirrored_ref[...]) * sign).astype(BF16)
        gather(part, 4)
        lone_ref[part] = (tn(block_ref[...], mirrored_ref[...]) * sign).astype(BF16)


def grad_filter_kernel(place_ref, own_ref, pair_ref, lone_ref, out_ref, wide_ref):
    low = place_ref[0] < 16
    for part in range(2):
        parts = [jnp.where(low, lone_ref[part], own_ref[3, part])]
        parts += [own_ref[j, part] for j in range(3)]
        parts += [jnp.where(low, own_ref[3, part], pair_ref[0, part])]
        parts += [pair_ref[n, part] for n in range(1, 4)]
        for i, value in enumerate(parts):
            put_eighth(wide_ref, i, value.astype(F32))
        out_ref[part] = take_wide(wide_ref)


def to_peers(values, axis):
    return lax.all_to_all(values, axis, split_axis=0, concat_axis=0, tiled=True)


def turned_exchange(parts):
    received = [parts[0]]
    for turn in range(1, CH_DEVICES):
        pairs = [(i, (i + turn) % CH_DEVICES) for i in range(CH_DEVICES)]
        received.append(lax.ppermute(parts[turn], "ch", pairs))
    return received


def after(value, earlier):
    return lax.optimization_barrier((value, earlier))


def on_device(tile_image, spectral_filter, conv_taps, norm_gain, up_weight, down_weight, upstream):
    device = lax.axis_index(ROWS)
    place = device.reshape(1).astype(jnp.int32)
    channel = lax.axis_index("ch").reshape(1).astype(jnp.int32)
    flat = (LANES, LEN)
    tables = [jnp.asarray(t) for t in (FORWARD_ROWS, INVERSE_ROWS, TWIDDLE_COS, TWIDDLE_SIN)]
    forward_columns, inverse_columns = jnp.asarray(FORWARD_COLUMNS), jnp.asarray(INVERSE_COLUMNS)
    straight, mirrored = jnp.asarray(STRAIGHT), jnp.asarray(MIRRORED)

    wide = pltpu.VMEM((2, LANES, 128), F32)
    head, tail, lone = kernel_call(
        filter_split_kernel,
        "filter_split",
        [shape((4, 2, CH, LEN), BF16), shape((4, 2, CH, LEN), BF16), shape((2, CH, LEN), BF16)],
        [wide],
        [spectral_filter.reshape(2, LANES, LEN)],
        16,
    )
    opposite = [(i, ROWS_DEVICES - 1 - i) for i in range(ROWS_DEVICES)]
    lone_in = [(i, ROWS_DEVICES - i) for i in range(1, 16)] + [(0, 16)]
    pair_filter = lax.ppermute(tail, ROWS, opposite)
    lone_filter = lax.ppermute(lone, ROWS, lone_in)
    message, signal = kernel_call(
        columns_kernel,
        "columns",
        [shape((LEN, LANES), BF16), shape(flat, BF16)],
        [wide, pltpu.VMEM(flat, BF16)],
        [tile_image.reshape(flat), forward_columns],
        16,
        2 * LEN * LEN * LANES,
    )
    received = to_peers(message, ROWS)

    (up_own, down_own, upstream_rows), _ = after(
        (up_weight, down_weight, upstream.reshape(flat)), message
    )
    start = lax.axis_index("core") * HALF_UNITS
    own_up = lax.dynamic_slice_in_dim(up_own, start, HALF_UNITS, axis=1).T
    own_down = lax.dynamic_slice_in_dim(down_own, start, HALF_UNITS, axis=0)
    pack = jnp.concatenate([own_up, own_down], axis=1)
    weights = lax.all_gather(pack, ("core", "ch"), axis=0, tiled=True)
    dy, *dy_turned = kernel_call(
        unfold_kernel,
        "unfold",
        [shape(flat, BF16)] + [shape((2 * CH, LEN), BF16)] * CH_DEVICES,
        [wide],
        [channel, upstream_rows],
        16,
        smem=1,
        hint=6,
    )
    dy_parts = turned_exchange(dy_turned)
    main, cross = kernel_call(
        filter_kernel,
        "filter",
        [shape((2, 128, LANES), F32), shape((2, 32, LANES), F32)],
        [],
        [place, head, tail, pair_filter, lone_filter, straight, mirrored],
        16,
        2 * 14 * LEN * LEN * CH,
        smem=1,
        hint=6,
    )
    received, dy_parts = after(received, dy_parts)

    row_scratch = [pltpu.VMEM((320, LANES), F32), pltpu.VMEM((LEN, LANES), BF16)]
    message, seen = kernel_call(
        rows_forward_kernel,
        "rows_forward",
        [shape((LEN, SENT), BF16), shape((2, 160, LANES), BF16)],
        row_scratch,
        [place, received, *tables, main, cross],
        20,
        2 * 576 * LEN * LANES,
        smem=1,
    )
    received = to_peers(message, ROWS)
    (hidden,) = kernel_call(
        hidden_kernel,
        "hidden",
        [shape(flat, BF16)],
        [pltpu.VMEM((SENT, LEN), BF16)],
        [received, inverse_columns, conv_taps, signal],
        16,
        2 * LEN * LEN * SENT,
    )
    hidden_tokens = to_peers(hidden, "ch")
    *out_turned, grad_message = mlp(
        channel, hidden_tokens, dy_parts, norm_gain.reshape(1, ALL_CH), weights
    )
    grad_mlp = to_peers(grad_message, "ch")
    (message,) = kernel_call(
        gradient_columns_kernel,
        "gradient_columns",
        [shape((LEN, SENT), BF16)],
        [pltpu.VMEM((SENT, LEN), BF16)],
        [dy, grad_mlp, conv_taps, forward_columns],
        16,
        2 * LEN * LEN * SENT,
    )
    out_turned, message = after(out_turned, message)
    received = to_peers(message, ROWS)
    out_parts = turned_exchange(out_turned)
    (block_out,) = kernel_call(
        block_out_kernel, "block_out", [shape(flat, BF16)], [wide], [channel, hidden, *out_parts], 16, smem=1
    )
    message, products = kernel_call(
        rows_backward_kernel,
        "rows_backward",
        [shape((LEN, LANES), BF16), shape((2, 160, LANES), BF16)],
        row_scratch,
        [place, received, *tables, main, cross, seen],
        20,
        2 * 576 * LEN * LANES,
        smem=1,
    )
    received = to_peers(message, ROWS)
    own, pair, lone = kernel_call(
        unturn_kernel,
        "unturn",
        [shape((4, 2, CH, LEN), BF16), shape((4, 2, CH, LEN), BF16), shape((2, CH, LEN), BF16)],
        [pltpu.VMEM((LEN, CH), BF16)],
        [products, straight, mirrored],
        16,
        2 * 18 * LEN * LEN * CH,
        hint=12,
    )
    pair = lax.ppermute(pair, ROWS, opposite)
    lone = lax.ppermute(lone, ROWS, [(b, a) for a, b in lone_in])
    (grad_filter,) = kernel_call(
        grad_filter_kernel,
        "grad_filter",
        [shape((2, LANES, LEN), F32)],
        [wide],
        [place, own, pair, lone],
        16,
        smem=1,
    )
    (grad_image,) = kernel_call(
        image_kernel,
        "image",
        [shape(flat, F32)],
        [wide],
        [received, inverse_columns, dy, grad_mlp],
        16,
        2 * LEN * LEN * LANES,
    )
    slab = (CH, SLAB, LEN)
    return (
        block_out.reshape(slab),
        grad_image.reshape(slab),
        grad_filter.reshape(2, CH, SLAB, LEN),
    )


def solution(mesh):
    devices = mesh.devices.reshape(4, 4, 2, CH_DEVICES)
    token = P("ch", ROWS, None)
    frequency = P(None, "ch", ROWS, None)
    return jax.shard_map(
        on_device,
        mesh=jax.sharding.Mesh(devices, (*ROWS, "ch")),
        in_specs=(token, frequency, P("ch", None), P(), P(None, "ch"), P("ch", None), token),
        out_specs=(token, token, frequency),
        check_vma=False,
    )
```

```python
import jax
import jax.numpy as jnp
import ml_dtypes
import numpy as np
from jax import lax
from jax.experimental import pallas as pl
from jax.experimental.pallas import tpu as pltpu
from jax.sharding import PartitionSpec as P

norm_epsilon = 1e-05
root_half = 0.7071067811865476
density = 0.3989422804014327

ROWS_DEVICES = 32
CH_DEVICES = 4
LEN = 256
SLAB = 8
CH = 192
ALL_CH = 768
LANES = SLAB * CH
WIDE = SLAB * 128
POINTS = LEN * LEN
HALF_UNITS = 384
MESSAGE = 2 * LEN
UNITS = 3072
ROWS = ("y", "z", "core")
SENT = (SLAB + 2) * CH
F32 = jnp.float32
BF16 = jnp.bfloat16
MIB = 1 << 20


def wide_at(h):
    return {-1: LANES, SLAB: LANES + 128}.get(h, 128 * h)


def narrow_at(h):
    return {-1: LANES + 256, SLAB: LANES + 320}.get(h, WIDE + 64 * (2 * (h % 4) + h // 4))


def column_tables():
    w, kw = np.arange(LEN)[None, :], np.arange(LEN)[:, None]
    turn = (2 * np.pi * (kw * w % LEN) / LEN).reshape(ROWS_DEVICES, SLAB, LEN)
    both = np.stack([np.cos(turn), -np.sin(turn)], axis=1)
    return both.reshape(MESSAGE, LEN)


def row_tables():
    k1, src = np.arange(32)[:, None], np.arange(32)[None, :]
    turn = 2 * np.pi * (k1 * src % 32) / 32
    cos, sin = np.cos(turn), np.sin(turn)
    forward = np.zeros((2, SLAB, 32, 32, 2, SLAB))
    inverse = np.zeros((32, 2, SLAB, 2, SLAB, 32))
    for j in range(SLAB):
        forward[0, j, :, :, 0, j], forward[0, j, :, :, 1, j] = cos, sin
        forward[1, j, :, :, 0, j], forward[1, j, :, :, 1, j] = -sin, cos
        inverse[:, 0, j, 0, j, :], inverse[:, 0, j, 1, j, :] = cos.T, -sin.T
        inverse[:, 1, j, 0, j, :], inverse[:, 1, j, 1, j, :] = sin.T, cos.T
    return forward.reshape(MESSAGE, MESSAGE), inverse.reshape(MESSAGE, MESSAGE)


def twiddle_tables():
    token_row = np.zeros(LANES, np.int64)
    for h in range(SLAB):
        token_row[128 * h : 128 * h + 128] = h
        token_row[narrow_at(h) : narrow_at(h) + 64] = h
    turn = 2 * np.pi * (np.arange(32)[:, None] * token_row[None, :] % LEN) / LEN
    return np.cos(turn), np.sin(turn)


def turn_table():
    k2, k1 = np.divmod(np.arange(LEN), 32)
    straight = np.zeros((LEN, LEN))
    straight[np.arange(LEN), k1 + 32 * k2] = 1.0
    return straight


def narrow(table):
    return np.asarray(table, np.float64).astype(ml_dtypes.bfloat16)


COLUMNS = narrow(column_tables())
FORWARD_ROWS, INVERSE_ROWS = (narrow(t) for t in row_tables())
TWIDDLE_COS, TWIDDLE_SIN = (t.astype(np.float32) for t in twiddle_tables())
STRAIGHT = narrow(turn_table())
UNIT = narrow(np.eye(LEN))


def nn(a, b):
    return lax.dot_general(a, b, (((1,), (0,)), ((), ())), preferred_element_type=F32)


def nt(a, b):
    return lax.dot_general(a, b, (((1,), (1,)), ((), ())), preferred_element_type=F32)


def tn(a, b):
    return lax.dot_general(a, b, (((0,), (0,)), ((), ())), preferred_element_type=F32)


def whole_block(dims):
    return pl.BlockSpec(dims, lambda *_: (0,) * len(dims), pipeline_mode=pl.Buffered(1))


def kernel_call(body, name, outs, scratch, operands, vmem, flops=0, smem=0, hint=0):
    scalar = pl.BlockSpec(memory_space=pltpu.SMEM)
    moved = sum(a.size * a.dtype.itemsize for a in operands)
    moved += sum(o.size * np.dtype(o.dtype).itemsize for o in outs)
    return pl.pallas_call(
        body,
        name=name,
        grid=(1,),
        out_shape=tuple(outs),
        in_specs=[scalar] * smem + [whole_block(a.shape) for a in operands[smem:]],
        out_specs=tuple(whole_block(o.shape) for o in outs),
        scratch_shapes=scratch,
        cost_estimate=pl.CostEstimate(
            flops=flops + hint * 10**9, bytes_accessed=moved, transcendentals=0
        ),
        compiler_params=pltpu.CompilerParams(vmem_limit_bytes=vmem * MIB),
    )(*operands)


def shape(dims, dtype):
    return jax.ShapeDtypeStruct(dims, dtype)


def fill_wide(wide_ref, values):
    for side in range(2):
        wide_ref[side] = values[:, side * 128 : side * 128 + 128]


def every_eighth(wide_ref, h):
    return jnp.concatenate([wide_ref[side, pl.ds(h, CH, stride=SLAB), :] for side in range(2)], axis=1)


def put_eighth(wide_ref, first, values):
    for side in range(2):
        at = pl.ds(first, values.shape[0], stride=SLAB)
        wide_ref[side, at, :] = values[:, side * 128 : side * 128 + 128]


def take_wide(wide_ref):
    return jnp.concatenate([wide_ref[side] for side in range(2)], axis=1)


def unfold_rows(source_ref, wide_ref):
    fill_wide(wide_ref, source_ref[...].astype(F32))
    for h in range(SLAB):
        yield h, every_eighth(wide_ref, h).astype(BF16)


def columns_kernel(image_ref, table_ref, message_ref, kept_ref, wide_ref, lanes_ref):
    for h, rows in unfold_rows(image_ref, wide_ref):
        kept_ref[h * CH : (h + 1) * CH] = rows
        lanes_ref[h * 128 : h * 128 + 128] = rows[:128]
        lanes_ref[narrow_at(h) : narrow_at(h) + 64] = rows[128:]
    send_columns(table_ref, lanes_ref, message_ref)


def send_columns(table_ref, lanes_ref, message_ref):
    for at in range(0, lanes_ref.shape[0], 384):
        message_ref[:, at : at + 384] = nt(table_ref[...], lanes_ref[at : at + 384]).astype(BF16)


def unfold_kernel(channel_ref, source_ref, kept_ref, *refs):
    *turned_refs, wide_ref = refs
    for h, rows in unfold_rows(source_ref, wide_ref):
        kept_ref[h * CH : (h + 1) * CH] = rows
    for turn, turned_ref in enumerate(turned_refs):
        peer = lax.rem(channel_ref[0] + turn, CH_DEVICES)
        for half in range(2):
            rows = every_eighth(wide_ref, peer * 2 + half)
            turned_ref[half * CH : half * CH + CH] = rows.astype(BF16)


def put_spectrum(target_ref, part, column, block):
    rows = slice(column * 32, column * 32 + 32)
    for k2 in range(SLAB):
        piece = block[k2 * 32 : k2 * 32 + 32]
        target_ref[part, rows, k2 * 128 : k2 * 128 + 128] = piece[:, :128]
        at = WIDE + 64 * k2
        target_ref[part, rows, at : at + 64] = piece[:, 128:]


def filter_kernel(filter_ref, straight_ref, main_ref, wide_ref):
    for part in range(2):
        fill_wide(wide_ref, filter_ref[part])
        for j in range(SLAB):
            turned = nt(straight_ref[...], every_eighth(wide_ref, j).astype(BF16))
            put_spectrum(main_ref, part, j, (turned * (1.0 / POINTS)).astype(BF16))


def eighth_turn(value, step, sign):
    re, im = value
    if step == 0:
        return value
    if step == 1:
        return (re + sign * im) * root_half, (im - sign * re) * root_half
    if step == 2:
        return sign * im, -sign * re
    return (sign * im - re) * root_half, (-sign * re - im) * root_half


def add(a, b):
    return a[0] + b[0], a[1] + b[1]


def sub(a, b):
    return a[0] - b[0], a[1] - b[1]


def four_points(x, sign):
    s, d = add(x[0], x[2]), sub(x[0], x[2])
    t, u = add(x[1], x[3]), eighth_turn(sub(x[1], x[3]), 2, sign)
    return [add(s, t), add(d, u), sub(s, t), sub(d, u)]


def eight_points(x, sign):
    even = four_points([add(x[m], x[m + 4]) for m in range(4)], sign)
    odd = four_points([eighth_turn(sub(x[m], x[m + 4]), m, sign) for m in range(4)], sign)
    return [part[q] for q in range(4) for part in (even, odd)]


def upper_lanes(like):
    return lax.broadcasted_iota(jnp.int32, like.shape, 1) >= 64


def halves(value):
    upper = upper_lanes(value)
    return pltpu.roll(value, 64, axis=1) + jnp.where(upper, -value, value)


def upper_turn(value, step, sign):
    upper = upper_lanes(value[0])
    return tuple(jnp.where(upper, b, a) for a, b in zip(value, eighth_turn(value, step, sign)))


def narrow_forward(x, sign):
    turned = [upper_turn((halves(re), halves(im)), m, sign) for m, (re, im) in enumerate(x)]
    return four_points(turned, sign)


def narrow_inverse(x, sign):
    turned = [upper_turn(v, m, sign) for m, v in enumerate(four_points(x, sign))]
    return [(halves(re), halves(im)) for re, im in turned]


def lane_blocks(re, im):
    return [(re[:, at : at + 128], im[:, at : at + 128]) for at in range(0, LANES, 128)]


def to_frequencies(re, im, cos, sin):
    x = lane_blocks(re * cos + im * sin, im * cos - re * sin)
    return eight_points(x[:SLAB], 1.0) + narrow_forward(x[SLAB:], 1.0)


def to_tokens_rows(blocks, cos, sin):
    y = eight_points(blocks[:SLAB], -1.0) + narrow_inverse(blocks[SLAB:], -1.0)
    re = jnp.concatenate([v[0] for v in y], axis=1)
    im = jnp.concatenate([v[1] for v in y], axis=1)
    return re * cos - im * sin, im * cos + re * sin


def moved_rows(block, step):
    rows = 2 * SLAB
    empty = jnp.zeros((rows, block.shape[1]), block.dtype)
    if step > 0:
        return jnp.concatenate([empty, block[:-rows]], axis=0)
    return jnp.concatenate([block[rows:], empty], axis=0)


def row_body(saves, refs):
    received_ref, fwd_ref, inv_ref, cos_ref, sin_ref, main_ref = refs[:6]
    if saves:
        message_ref, seen_ref, mixed_ref, ready_ref = refs[6:]
    else:
        seen_ref, message_ref, product_ref, mixed_ref, ready_ref = refs[6:]

    def joined(at, width, edge, step):
        rows = received_ref[:, at : at + width].astype(F32)
        moved = moved_rows(received_ref[:, edge : edge + width].astype(F32), step)
        return nn(fwd_ref[...], (rows + moved).astype(BF16))

    for at in range(0, LANES, 512):
        mixed_ref[:, at : at + 512] = nn(fwd_ref[...], received_ref[:, at : at + 512])
    if not saves:
        for h, edge, step in ((0, SLAB, 1), (SLAB - 1, -1, -1)):
            at = wide_at(h)
            mixed_ref[:, at : at + 128] = joined(at, 128, wide_at(edge), step)
            at = narrow_at(h)
            mixed_ref[:, at : at + 64] = joined(at, 64, narrow_at(edge), step)

    def group(index, carry):
        at = pl.ds(pl.multiple_of(index * 16, 16), 16)
        at_im = pl.ds(pl.multiple_of(LEN + index * 16, 16), 16)
        table = pl.ds(pl.multiple_of(lax.rem(index, 2) * 16, 16), 16)
        cos, sin = cos_ref[table, :], sin_ref[table, :]
        values = to_frequencies(mixed_ref[at, :], mixed_ref[at_im, :], cos, sin)
        filtered = []
        for n, (re, im) in enumerate(values):
            lanes = slice(n * 128, n * 128 + 128)
            k_re, k_im = main_ref[0, at, lanes].astype(F32), main_ref[1, at, lanes].astype(F32)
            if saves:
                seen_ref[0, at, lanes], seen_ref[1, at, lanes] = re.astype(BF16), im.astype(BF16)
                filtered.append((re * k_re - im * k_im, im * k_re + re * k_im))
            else:
                x_re, x_im = seen_ref[0, at, lanes].astype(F32), seen_ref[1, at, lanes].astype(F32)
                product_re = (x_re * re + x_im * im) * (1.0 / POINTS)
                product_im = (im * x_re - re * x_im) * (1.0 / POINTS)
                product_ref[0, at, lanes] = product_re.astype(BF16)
                product_ref[1, at, lanes] = product_im.astype(BF16)
                filtered.append((re * k_re + im * k_im, im * k_re - re * k_im))
        re, im = to_tokens_rows(filtered, cos, sin)
        ready_ref[at, :] = re.astype(BF16)
        ready_ref[at_im, :] = im.astype(BF16)
        return carry

    lax.fori_loop(0, 16, group, 0)
    for at in range(0, LANES, 512):
        block = nn(inv_ref[...], ready_ref[:, at : at + 512])
        message_ref[:, at : at + 512] = block.astype(BF16)
        if saves:
            for h, edge, step in ((0, SLAB, -1), (SLAB - 1, -1, 1)):
                for place, width in ((wide_at, 128), (narrow_at, 64)):
                    start = place(h) - at
                    if 0 <= start < 512:
                        moved = moved_rows(block[:, start : start + width], step)
                        message_ref[:, place(edge) : place(edge) + width] = moved.astype(BF16)


def rows_forward_kernel(*refs):
    row_body(True, refs)


def rows_backward_kernel(*refs):
    row_body(False, refs)


def token_rows(received_ref, table_ref, place):
    for h in range(SLAB):
        place(h, 0, tn(received_ref[:, h * 128 : h * 128 + 128], table_ref[...]))
    for m in range(4):
        at = WIDE + 128 * m
        block = tn(received_ref[:, at : at + 128], table_ref[...])
        place(m, 128, block[:64])
        place(m + 4, 128, block[64:])


def convolve(load, rows, taps, put):
    lane = lax.broadcasted_iota(jnp.int32, (16, LEN), 1)
    window = [load(rows[0] - 1), load(rows[0])]
    for h in rows:
        window.append(load(h + 1))
        sums = []
        for b in range(3):
            terms = [taps[3 * a + b] * w for a, w in enumerate(window) if w is not None]
            sums.append(sum(terms[1:], terms[0]))
        left = jnp.where(lane == 0, 0.0, pltpu.roll(sums[0], 1, axis=1))
        right = jnp.where(lane == LEN - 1, 0.0, pltpu.roll(sums[2], LEN - 1, axis=1))
        put(h, sums[1] + left + right)
        window.pop(0)


def every_chunk(body):
    def wide(index, carry):
        at = pl.multiple_of(index * 16, 16)
        body(at, lambda h: pl.ds(pl.multiple_of(wide_at(h) + at, 16), 16))
        return carry

    def last(index, carry):
        at = pl.multiple_of(index * 16, 16)
        body(at + 128, lambda h: pl.ds(pl.multiple_of(narrow_at(h) + at, 16), 16))
        return carry

    lax.fori_loop(0, 8, wide, 0)
    lax.fori_loop(0, 4, last, 0)


def rows_at(h, start):
    return pl.ds(pl.multiple_of(h * CH + start, 16), 16)


def spread_taps(taps_ref, start, order):
    taps = taps_ref[pl.ds(pl.multiple_of(start, 16), 16), :]
    return [jnp.broadcast_to(taps[:, k : k + 1], (16, LEN)) for k in order]


def hidden_kernel(received_ref, table_ref, taps_ref, signal_ref, hidden_ref, filtered_ref):
    for at in range(0, SENT, 128):
        block = tn(received_ref[:, at : at + 128], table_ref[...])
        filtered_ref[at : at + 128] = block.astype(BF16)

    def chunk(start, place):
        def load(h):
            return filtered_ref[place(h), :].astype(F32)

        def put(h, convolved):
            at = rows_at(h, start)
            hidden_ref[at, :] = (signal_ref[at, :].astype(F32) + convolved).astype(BF16)

        convolve(load, range(SLAB), spread_taps(taps_ref, start, range(9)), put)

    every_chunk(chunk)


def gradient_columns_kernel(upstream_ref, mlp_ref, taps_ref, table_ref, message_ref, lanes_ref):
    def chunk(start, place):
        def load(h):
            if h < 0 or h >= SLAB:
                return None
            at = rows_at(h, start)
            return upstream_ref[at, :].astype(F32) + mlp_ref[at, :].astype(F32)

        def put(h, convolved):
            lanes_ref[place(h), :] = convolved.astype(BF16)

        convolve(
            load, range(-1, SLAB + 1), spread_taps(taps_ref, start, range(8, -1, -1)), put
        )

    every_chunk(chunk)
    send_columns(table_ref, lanes_ref, message_ref)


def gelu_parts(pre_act):
    cumulative = 0.5 * (1.0 + lax.erf(pre_act * root_half))
    bell = density * jnp.exp(-0.5 * pre_act * pre_act)
    return pre_act * cumulative, cumulative + pre_act * bell


def mlp_kernel(
    channel_ref,
    hidden_ref,
    own_dy_ref,
    dy_one_ref,
    dy_two_ref,
    dy_three_ref,
    gain_ref,
    unit_ref,
    mine_ref,
    other_ref,
    out_own_ref,
    out_one_ref,
    out_two_ref,
    out_three_ref,
    grad_ref,
    parts_ref,
    gathered_ref,
    scaled_ref,
    dy_ref,
    normed_ref,
    inv_ref,
    out_sum_ref,
    grad_sum_ref,
):
    step = pl.program_id(0)
    channel = channel_ref[0]

    def turn_in(half):
        for src in range(CH_DEVICES):
            at = src * 2 * CH + half * CH
            gathered_ref[src * CH : (src + 1) * CH] = hidden_ref[at : at + CH]
        return nt(unit_ref[...], gathered_ref[...])

    def turn_in_dy(half):
        for src in range(CH_DEVICES):
            gathered_ref[src * CH : (src + 1) * CH] = parts_ref[src, half * CH : half * CH + CH]
        return nt(unit_ref[...], gathered_ref[...])

    @pl.when(step == 0)
    def _():
        for turn, source_ref in enumerate((own_dy_ref, dy_one_ref, dy_two_ref, dy_three_ref)):
            parts_ref[lax.rem(channel + CH_DEVICES - turn, CH_DEVICES)] = source_ref[...]
        for half in range(2):
            rows = slice(half * LEN, half * LEN + LEN)
            values = turn_in(half)
            centred = values - jnp.mean(values, axis=1, keepdims=True)
            variance = jnp.mean(centred * centred, axis=1, keepdims=True)
            inv_std = lax.rsqrt(variance + norm_epsilon)
            normed = centred * inv_std
            normed_ref[rows] = normed
            inv_ref[rows] = jnp.broadcast_to(inv_std, (LEN, 128))
            scaled_ref[rows] = (normed * gain_ref[...]).astype(BF16)
            dy_ref[rows] = turn_in_dy(half).astype(BF16)
        out_sum_ref[...] = jnp.zeros_like(out_sum_ref)
        grad_sum_ref[...] = jnp.zeros_like(grad_sum_ref)

    for weights_ref in (mine_ref, other_ref):
        up, down = weights_ref[:, :ALL_CH], weights_ref[:, ALL_CH:]
        pre_act = nt(scaled_ref[...], up)
        grad_act = nt(dy_ref[...], down)
        activated, slope = gelu_parts(pre_act)
        out_sum_ref[...] += nn(activated.astype(BF16), down)
        grad_sum_ref[...] += nn((grad_act * slope).astype(BF16), up)

    def turn_out(values, half, put):
        for block in range(3):
            piece = nt(unit_ref[...], values[:, block * LEN : (block + 1) * LEN])
            gathered_ref[block * LEN : (block + 1) * LEN] = piece.astype(BF16)
        for dst in range(CH_DEVICES):
            put(dst, half, gathered_ref[dst * CH : (dst + 1) * CH])

    def put_grad(dst, half, rows):
        at = (dst * 2 + half) * CH
        grad_ref[at : at + CH] = rows

    def put_out(dst, half, rows):
        parts_ref[dst, half * CH : half * CH + CH] = rows

    @pl.when(step == pl.num_programs(0) - 1)
    def _():
        for half in range(2):
            rows = slice(half * LEN, half * LEN + LEN)
            weighted = grad_sum_ref[rows] * gain_ref[...]
            normed = normed_ref[rows]
            first = jnp.mean(weighted, axis=1, keepdims=True)
            second = jnp.mean(weighted * normed, axis=1, keepdims=True)
            term = inv_ref[rows, 0:1] * (weighted - first - normed * second)
            turn_out(term.astype(BF16), half, put_grad)
            turn_out(out_sum_ref[rows].astype(BF16), half, put_out)
        for turn, out_ref in enumerate((out_own_ref, out_one_ref, out_two_ref, out_three_ref)):
            out_ref[...] = parts_ref[lax.rem(channel + turn, CH_DEVICES)]


def mlp(channel, hidden, dy_parts, gain, weights, block=256):
    tokens, steps = 2 * LEN, UNITS // 2 // block
    part = whole_block((2 * CH, LEN))
    return pl.pallas_call(
        mlp_kernel,
        name="mlp",
        grid=(steps,),
        out_shape=(*(shape((2 * CH, LEN), BF16),) * CH_DEVICES, shape((LANES, LEN), BF16)),
        in_specs=[
            pl.BlockSpec(memory_space=pltpu.SMEM),
            whole_block((LANES, LEN)),
            part,
            part,
            part,
            part,
            whole_block((1, ALL_CH)),
            whole_block((LEN, LEN)),
            pl.BlockSpec((block, 2 * ALL_CH), lambda i: (i, 0)),
            pl.BlockSpec((block, 2 * ALL_CH), lambda i: (i + steps, 0)),
        ],
        out_specs=(part, part, part, part, whole_block((LANES, LEN))),
        scratch_shapes=[
            pltpu.VMEM((CH_DEVICES, 2 * CH, LEN), BF16),
            pltpu.VMEM((ALL_CH, LEN), BF16),
            pltpu.VMEM((tokens, ALL_CH), BF16),
            pltpu.VMEM((tokens, ALL_CH), BF16),
            pltpu.VMEM((tokens, ALL_CH), F32),
            pltpu.VMEM((tokens, 128), F32),
            pltpu.VMEM((tokens, ALL_CH), F32),
            pltpu.VMEM((tokens, ALL_CH), F32),
        ],
        cost_estimate=pl.CostEstimate(
            flops=8 * tokens * UNITS * ALL_CH,
            bytes_accessed=4 * UNITS * ALL_CH + 8 * LANES * LEN,
            transcendentals=2 * tokens * UNITS,
        ),
        compiler_params=pltpu.CompilerParams(vmem_limit_bytes=48 * MIB),
    )(channel, hidden, *dy_parts, gain, jnp.asarray(UNIT), weights, weights)


def block_out_kernel(channel_ref, hidden_ref, own_ref, one_ref, two_ref, three_ref, out_ref, wide_ref):
    for turn, sum_ref in enumerate((own_ref, one_ref, two_ref, three_ref)):
        src = lax.rem(channel_ref[0] + CH_DEVICES - turn, CH_DEVICES)
        for half in range(2):
            rows = pl.ds(pl.multiple_of((src * 2 + half) * CH, 64), CH)
            total = hidden_ref[rows, :].astype(F32)
            total += sum_ref[half * CH : half * CH + CH].astype(F32)
            put_eighth(wide_ref, src * 2 + half, total)
    out_ref[...] = take_wide(wide_ref).astype(BF16)


def image_kernel(received_ref, table_ref, upstream_ref, mlp_ref, out_ref, wide_ref):
    def place(h, channel, block):
        count = block.shape[0]
        rows = slice(h * CH + channel, h * CH + channel + count)
        total = block + upstream_ref[rows].astype(F32) + mlp_ref[rows].astype(F32)
        put_eighth(wide_ref, channel * SLAB + h, total)

    token_rows(received_ref, table_ref, place)
    out_ref[...] = take_wide(wide_ref)


def grad_filter_kernel(product_ref, straight_ref, out_ref, block_ref, wide_ref):
    for part in range(2):
        for j in range(SLAB):
            rows = slice(j * 32, j * 32 + 32)
            for k2 in range(SLAB):
                to = slice(k2 * 32, k2 * 32 + 32)
                at = WIDE + 64 * k2
                block_ref[to, :128] = product_ref[part, rows, k2 * 128 : k2 * 128 + 128]
                block_ref[to, 128:] = product_ref[part, rows, at : at + 64]
            put_eighth(wide_ref, j, tn(block_ref[...], straight_ref[...]))
        out_ref[part] = take_wide(wide_ref)


def to_peers(values, axis):
    return lax.all_to_all(values, axis, split_axis=0, concat_axis=0, tiled=True)


def turned_exchange(parts):
    received = [parts[0]]
    for turn in range(1, CH_DEVICES):
        pairs = [(i, (i + turn) % CH_DEVICES) for i in range(CH_DEVICES)]
        received.append(lax.ppermute(parts[turn], "ch", pairs))
    return received


def after(value, earlier):
    return lax.optimization_barrier((value, earlier))


def on_device(tile_image, spectral_filter, conv_taps, norm_gain, up_weight, down_weight, upstream):
    channel = lax.axis_index("ch").reshape(1).astype(jnp.int32)
    flat = (LANES, LEN)
    tables = [jnp.asarray(t) for t in (FORWARD_ROWS, INVERSE_ROWS, TWIDDLE_COS, TWIDDLE_SIN)]
    columns, straight = jnp.asarray(COLUMNS), jnp.asarray(STRAIGHT)
    wide = pltpu.VMEM((2, LANES, 128), F32)
    message, signal = kernel_call(
        columns_kernel,
        "columns",
        [shape((MESSAGE, LANES), BF16), shape(flat, BF16)],
        [wide, pltpu.VMEM(flat, BF16)],
        [tile_image.reshape(flat), columns],
        16,
        2 * MESSAGE * LEN * LANES,
    )
    received = to_peers(message, ROWS)

    (upstream_rows, filter_rows), _ = after(
        (upstream.reshape(flat), spectral_filter.reshape(2, LANES, LEN)), message
    )
    dy, *dy_turned = kernel_call(
        unfold_kernel,
        "unfold",
        [shape(flat, BF16)] + [shape((2 * CH, LEN), BF16)] * CH_DEVICES,
        [wide],
        [channel, upstream_rows],
        16,
        smem=1,
        hint=6,
    )
    (up_own, down_own), _ = after((up_weight, down_weight), dy_turned)
    start = lax.axis_index("core") * HALF_UNITS
    own_up = lax.dynamic_slice_in_dim(up_own, start, HALF_UNITS, axis=1).T
    own_down = lax.dynamic_slice_in_dim(down_own, start, HALF_UNITS, axis=0)
    pack = jnp.concatenate([own_up, own_down], axis=1)
    weights = lax.all_gather(pack, ("core", "ch"), axis=0, tiled=True)
    dy_parts = turned_exchange(dy_turned)
    (main,) = kernel_call(
        filter_kernel,
        "filter",
        [shape((2, LEN, LANES), BF16)],
        [wide],
        [filter_rows, straight],
        16,
        2 * 16 * LEN * LEN * CH,
        hint=6,
    )
    received, dy_parts, main = lax.optimization_barrier((received, dy_parts, main))
    row_scratch = [pltpu.VMEM((MESSAGE, LANES), F32), pltpu.VMEM((MESSAGE, LANES), BF16)]
    row_flops = 4 * MESSAGE * MESSAGE * LANES
    message, seen = kernel_call(
        rows_forward_kernel,
        "rows_forward",
        [shape((MESSAGE, SENT), BF16), shape((2, LEN, LANES), BF16)],
        row_scratch,
        [received, *tables, main],
        20,
        row_flops,
    )
    received = to_peers(message, ROWS)
    (hidden,) = kernel_call(
        hidden_kernel,
        "hidden",
        [shape(flat, BF16)],
        [pltpu.VMEM((SENT, LEN), BF16)],
        [received, columns, conv_taps, signal],
        16,
        2 * MESSAGE * LEN * SENT,
    )
    hidden_tokens = to_peers(hidden, "ch")
    *out_turned, grad_message = mlp(
        channel, hidden_tokens, dy_parts, norm_gain.reshape(1, ALL_CH), weights
    )
    grad_mlp = to_peers(grad_message, "ch")
    (message,) = kernel_call(
        gradient_columns_kernel,
        "gradient_columns",
        [shape((MESSAGE, SENT), BF16)],
        [pltpu.VMEM((SENT, LEN), BF16)],
        [dy, grad_mlp, conv_taps, columns],
        16,
        2 * MESSAGE * LEN * SENT,
    )
    out_turned, message = after(out_turned, message)
    received = to_peers(message, ROWS)
    message, products = kernel_call(
        rows_backward_kernel,
        "rows_backward",
        [shape((MESSAGE, LANES), BF16), shape((2, LEN, LANES), BF16)],
        row_scratch,
        [received, *tables, main, seen],
        20,
        row_flops,
    )
    received = to_peers(message, ROWS)
    out_parts = turned_exchange(out_turned)
    (block_out,) = kernel_call(
        block_out_kernel, "block_out", [shape(flat, BF16)], [wide], [channel, hidden, *out_parts], 16, smem=1, hint=6
    )
    (grad_filter,) = kernel_call(
        grad_filter_kernel,
        "grad_filter",
        [shape((2, LANES, LEN), F32)],
        [pltpu.VMEM((LEN, CH), BF16), wide],
        [products, straight],
        16,
        2 * 16 * LEN * LEN * CH,
        hint=12,
    )
    (grad_image,) = kernel_call(
        image_kernel,
        "image",
        [shape(flat, F32)],
        [wide],
        [received, columns, dy, grad_mlp],
        16,
        2 * MESSAGE * LEN * LANES,
    )
    slab = (CH, SLAB, LEN)
    return (
        block_out.reshape(slab),
        grad_image.reshape(slab),
        grad_filter.reshape(2, CH, SLAB, LEN),
    )


def solution(mesh):
    devices = mesh.devices.reshape(4, 4, 2, CH_DEVICES)
    token = P("ch", ROWS, None)
    frequency = P(None, "ch", ROWS, None)
    return jax.shard_map(
        on_device,
        mesh=jax.sharding.Mesh(devices, (*ROWS, "ch")),
        in_specs=(token, frequency, P("ch", None), P(), P(None, "ch"), P("ch", None), token),
        out_specs=(token, token, frequency),
        check_vma=False,
    )
```

```python
import jax
import jax.numpy as jnp
import ml_dtypes
import numpy as np
from jax import lax
from jax.experimental import pallas as pl
from jax.experimental.pallas import tpu as pltpu
from jax.sharding import PartitionSpec as P

norm_epsilon = 1e-05
root_half = 0.7071067811865476
density = 0.3989422804014327

ROWS_DEVICES = 32
CH_DEVICES = 4
LEN = 256
SLAB = 8
CH = 192
ALL_CH = 768
LANES = SLAB * CH
WIDE = SLAB * 128
POINTS = LEN * LEN
HALF_UNITS = 384
MESSAGE = 2 * LEN
UNITS = 3072
ROWS = ("y", "z", "core")
SENT = (SLAB + 2) * CH
F32 = jnp.float32
BF16 = jnp.bfloat16
MIB = 1 << 20


def wide_at(h):
    return {-1: LANES, SLAB: LANES + 128}.get(h, 128 * h)


def narrow_at(h):
    return {-1: LANES + 256, SLAB: LANES + 320}.get(h, WIDE + 64 * (2 * (h % 4) + h // 4))


def column_tables():
    w, kw = np.arange(LEN)[None, :], np.arange(LEN)[:, None]
    turn = (2 * np.pi * (kw * w % LEN) / LEN).reshape(ROWS_DEVICES, SLAB, LEN)
    both = np.stack([np.cos(turn), -np.sin(turn)], axis=1)
    return both.reshape(MESSAGE, LEN)


def row_tables():
    k1, src = np.arange(32)[:, None], np.arange(32)[None, :]
    turn = 2 * np.pi * (k1 * src % 32) / 32
    cos, sin = np.cos(turn), np.sin(turn)
    forward = np.zeros((2, SLAB, 32, 32, 2, SLAB))
    inverse = np.zeros((32, 2, SLAB, 2, SLAB, 32))
    for j in range(SLAB):
        forward[0, j, :, :, 0, j], forward[0, j, :, :, 1, j] = cos, sin
        forward[1, j, :, :, 0, j], forward[1, j, :, :, 1, j] = -sin, cos
        inverse[:, 0, j, 0, j, :], inverse[:, 0, j, 1, j, :] = cos.T, -sin.T
        inverse[:, 1, j, 0, j, :], inverse[:, 1, j, 1, j, :] = sin.T, cos.T
    return forward.reshape(MESSAGE, MESSAGE), inverse.reshape(MESSAGE, MESSAGE)


def twiddle_tables():
    token_row = np.zeros(LANES, np.int64)
    for h in range(SLAB):
        token_row[128 * h : 128 * h + 128] = h
        token_row[narrow_at(h) : narrow_at(h) + 64] = h
    turn = 2 * np.pi * (np.arange(32)[:, None] * token_row[None, :] % LEN) / LEN
    return np.cos(turn), np.sin(turn)


def turn_table():
    k2, k1 = np.divmod(np.arange(LEN), 32)
    straight = np.zeros((LEN, LEN))
    straight[np.arange(LEN), k1 + 32 * k2] = 1.0
    return straight


def narrow(table):
    return np.asarray(table, np.float64).astype(ml_dtypes.bfloat16)


COLUMNS = narrow(column_tables())
FORWARD_ROWS, INVERSE_ROWS = (narrow(t) for t in row_tables())
TWIDDLE_COS, TWIDDLE_SIN = (t.astype(np.float32) for t in twiddle_tables())
STRAIGHT = narrow(turn_table())
UNIT = narrow(np.eye(LEN))


def nn(a, b):
    return lax.dot_general(a, b, (((1,), (0,)), ((), ())), preferred_element_type=F32)


def nt(a, b):
    return lax.dot_general(a, b, (((1,), (1,)), ((), ())), preferred_element_type=F32)


def tn(a, b):
    return lax.dot_general(a, b, (((0,), (0,)), ((), ())), preferred_element_type=F32)


def whole_block(dims):
    return pl.BlockSpec(dims, lambda *_: (0,) * len(dims), pipeline_mode=pl.Buffered(1))


def kernel_call(body, name, outs, scratch, operands, vmem, flops=0, smem=0, beside=False):
    scalar = pl.BlockSpec(memory_space=pltpu.SMEM)
    moved = sum(a.size * a.dtype.itemsize for a in operands)
    moved += sum(o.size * np.dtype(o.dtype).itemsize for o in outs)
    return pl.pallas_call(
        body,
        name=name,
        grid=(1,),
        out_shape=tuple(outs),
        in_specs=[scalar] * smem + [whole_block(a.shape) for a in operands[smem:]],
        out_specs=tuple(whole_block(o.shape) for o in outs),
        scratch_shapes=scratch,
        cost_estimate=pl.CostEstimate(
            flops=0 if beside else flops,
            bytes_accessed=1024 if beside else moved,
            transcendentals=0,
        ),
        compiler_params=pltpu.CompilerParams(vmem_limit_bytes=vmem * MIB),
    )(*operands)


def shape(dims, dtype):
    return jax.ShapeDtypeStruct(dims, dtype)


def fill_wide(wide_ref, values):
    for side in range(2):
        wide_ref[side] = values[:, side * 128 : side * 128 + 128]


def every_eighth(wide_ref, h):
    return jnp.concatenate([wide_ref[side, pl.ds(h, CH, stride=SLAB), :] for side in range(2)], axis=1)


def put_eighth(wide_ref, first, values):
    for side in range(2):
        at = pl.ds(first, values.shape[0], stride=SLAB)
        wide_ref[side, at, :] = values[:, side * 128 : side * 128 + 128]


def take_wide(wide_ref):
    return jnp.concatenate([wide_ref[side] for side in range(2)], axis=1)


def unfold_rows(source_ref, wide_ref):
    fill_wide(wide_ref, source_ref[...].astype(F32))
    for h in range(SLAB):
        yield h, every_eighth(wide_ref, h).astype(BF16)


def columns_kernel(image_ref, table_ref, message_ref, kept_ref, wide_ref, lanes_ref):
    for h, rows in unfold_rows(image_ref, wide_ref):
        kept_ref[h * CH : (h + 1) * CH] = rows
        lanes_ref[h * 128 : h * 128 + 128] = rows[:128]
        lanes_ref[narrow_at(h) : narrow_at(h) + 64] = rows[128:]
    send_columns(table_ref, lanes_ref, message_ref)


def send_columns(table_ref, lanes_ref, message_ref):
    for at in range(0, lanes_ref.shape[0], 384):
        message_ref[:, at : at + 384] = nt(table_ref[...], lanes_ref[at : at + 384]).astype(BF16)


def unfold_kernel(channel_ref, source_ref, kept_ref, *refs):
    *turned_refs, wide_ref = refs
    for h, rows in unfold_rows(source_ref, wide_ref):
        kept_ref[h * CH : (h + 1) * CH] = rows
    for turn, turned_ref in enumerate(turned_refs):
        peer = lax.rem(channel_ref[0] + turn, CH_DEVICES)
        for half in range(2):
            rows = every_eighth(wide_ref, peer * 2 + half)
            turned_ref[half * CH : half * CH + CH] = rows.astype(BF16)


def put_spectrum(target_ref, part, column, block):
    rows = slice(column * 32, column * 32 + 32)
    for k2 in range(SLAB):
        piece = block[k2 * 32 : k2 * 32 + 32]
        target_ref[part, rows, k2 * 128 : k2 * 128 + 128] = piece[:, :128]
        at = WIDE + 64 * k2
        target_ref[part, rows, at : at + 64] = piece[:, 128:]


def filter_kernel(filter_ref, straight_ref, main_ref, wide_ref):
    for part in range(2):
        fill_wide(wide_ref, filter_ref[part])
        for j in range(SLAB):
            turned = nt(straight_ref[...], every_eighth(wide_ref, j).astype(BF16))
            put_spectrum(main_ref, part, j, (turned * (1.0 / POINTS)).astype(BF16))


def eighth_turn(value, step, sign):
    re, im = value
    if step == 0:
        return value
    if step == 1:
        return (re + sign * im) * root_half, (im - sign * re) * root_half
    if step == 2:
        return sign * im, -sign * re
    return (sign * im - re) * root_half, (-sign * re - im) * root_half


def add(a, b):
    return a[0] + b[0], a[1] + b[1]


def sub(a, b):
    return a[0] - b[0], a[1] - b[1]


def four_points(x, sign):
    s, d = add(x[0], x[2]), sub(x[0], x[2])
    t, u = add(x[1], x[3]), eighth_turn(sub(x[1], x[3]), 2, sign)
    return [add(s, t), add(d, u), sub(s, t), sub(d, u)]


def eight_points(x, sign):
    even = four_points([add(x[m], x[m + 4]) for m in range(4)], sign)
    odd = four_points([eighth_turn(sub(x[m], x[m + 4]), m, sign) for m in range(4)], sign)
    return [part[q] for q in range(4) for part in (even, odd)]


def upper_lanes(like):
    return lax.broadcasted_iota(jnp.int32, like.shape, 1) >= 64


def halves(value):
    upper = upper_lanes(value)
    return pltpu.roll(value, 64, axis=1) + jnp.where(upper, -value, value)


def upper_turn(value, step, sign):
    upper = upper_lanes(value[0])
    return tuple(jnp.where(upper, b, a) for a, b in zip(value, eighth_turn(value, step, sign)))


def narrow_forward(x, sign):
    turned = [upper_turn((halves(re), halves(im)), m, sign) for m, (re, im) in enumerate(x)]
    return four_points(turned, sign)


def narrow_inverse(x, sign):
    turned = [upper_turn(v, m, sign) for m, v in enumerate(four_points(x, sign))]
    return [(halves(re), halves(im)) for re, im in turned]


def lane_blocks(re, im):
    return [(re[:, at : at + 128], im[:, at : at + 128]) for at in range(0, LANES, 128)]


def to_frequencies(re, im, cos, sin):
    x = lane_blocks(re * cos + im * sin, im * cos - re * sin)
    return eight_points(x[:SLAB], 1.0) + narrow_forward(x[SLAB:], 1.0)


def to_tokens_rows(blocks, cos, sin):
    y = eight_points(blocks[:SLAB], -1.0) + narrow_inverse(blocks[SLAB:], -1.0)
    re = jnp.concatenate([v[0] for v in y], axis=1)
    im = jnp.concatenate([v[1] for v in y], axis=1)
    return re * cos - im * sin, im * cos + re * sin


def moved_rows(block, step):
    rows = 2 * SLAB
    empty = jnp.zeros((rows, block.shape[1]), block.dtype)
    if step > 0:
        return jnp.concatenate([empty, block[:-rows]], axis=0)
    return jnp.concatenate([block[rows:], empty], axis=0)


def row_body(saves, refs):
    received_ref, fwd_ref, inv_ref, cos_ref, sin_ref, main_ref = refs[:6]
    if saves:
        message_ref, seen_ref, mixed_ref, ready_ref = refs[6:]
    else:
        seen_ref, message_ref, product_ref, mixed_ref, ready_ref = refs[6:]

    def joined(at, width, edge, step):
        rows = received_ref[:, at : at + width].astype(F32)
        moved = moved_rows(received_ref[:, edge : edge + width].astype(F32), step)
        return nn(fwd_ref[...], (rows + moved).astype(BF16))

    for at in range(0, LANES, 512):
        mixed_ref[:, at : at + 512] = nn(fwd_ref[...], received_ref[:, at : at + 512])
    if not saves:
        for h, edge, step in ((0, SLAB, 1), (SLAB - 1, -1, -1)):
            at = wide_at(h)
            mixed_ref[:, at : at + 128] = joined(at, 128, wide_at(edge), step)
            at = narrow_at(h)
            mixed_ref[:, at : at + 64] = joined(at, 64, narrow_at(edge), step)

    def group(index, carry):
        at = pl.ds(pl.multiple_of(index * 16, 16), 16)
        at_im = pl.ds(pl.multiple_of(LEN + index * 16, 16), 16)
        table = pl.ds(pl.multiple_of(lax.rem(index, 2) * 16, 16), 16)
        cos, sin = cos_ref[table, :], sin_ref[table, :]
        values = to_frequencies(mixed_ref[at, :], mixed_ref[at_im, :], cos, sin)
        filtered = []
        for n, (re, im) in enumerate(values):
            lanes = slice(n * 128, n * 128 + 128)
            k_re, k_im = main_ref[0, at, lanes].astype(F32), main_ref[1, at, lanes].astype(F32)
            if saves:
                seen_ref[0, at, lanes], seen_ref[1, at, lanes] = re.astype(BF16), im.astype(BF16)
                filtered.append((re * k_re - im * k_im, im * k_re + re * k_im))
            else:
                x_re, x_im = seen_ref[0, at, lanes].astype(F32), seen_ref[1, at, lanes].astype(F32)
                product_re = (x_re * re + x_im * im) * (1.0 / POINTS)
                product_im = (im * x_re - re * x_im) * (1.0 / POINTS)
                product_ref[0, at, lanes] = product_re.astype(BF16)
                product_ref[1, at, lanes] = product_im.astype(BF16)
                filtered.append((re * k_re + im * k_im, im * k_re - re * k_im))
        re, im = to_tokens_rows(filtered, cos, sin)
        ready_ref[at, :] = re.astype(BF16)
        ready_ref[at_im, :] = im.astype(BF16)
        return carry

    lax.fori_loop(0, 16, group, 0)
    for at in range(0, LANES, 512):
        block = nn(inv_ref[...], ready_ref[:, at : at + 512])
        message_ref[:, at : at + 512] = block.astype(BF16)
        if saves:
            for h, edge, step in ((0, SLAB, -1), (SLAB - 1, -1, 1)):
                for place, width in ((wide_at, 128), (narrow_at, 64)):
                    start = place(h) - at
                    if 0 <= start < 512:
                        moved = moved_rows(block[:, start : start + width], step)
                        message_ref[:, place(edge) : place(edge) + width] = moved.astype(BF16)


def rows_forward_kernel(*refs):
    row_body(True, refs)


def rows_backward_kernel(*refs):
    row_body(False, refs)


def token_rows(received_ref, table_ref, place):
    for h in range(SLAB):
        place(h, 0, tn(received_ref[:, h * 128 : h * 128 + 128], table_ref[...]))
    for m in range(4):
        at = WIDE + 128 * m
        block = tn(received_ref[:, at : at + 128], table_ref[...])
        place(m, 128, block[:64])
        place(m + 4, 128, block[64:])


def convolve(load, rows, taps, put):
    lane = lax.broadcasted_iota(jnp.int32, (16, LEN), 1)
    window = [load(rows[0] - 1), load(rows[0])]
    for h in rows:
        window.append(load(h + 1))
        sums = []
        for b in range(3):
            terms = [taps[3 * a + b] * w for a, w in enumerate(window) if w is not None]
            sums.append(sum(terms[1:], terms[0]))
        left = jnp.where(lane == 0, 0.0, pltpu.roll(sums[0], 1, axis=1))
        right = jnp.where(lane == LEN - 1, 0.0, pltpu.roll(sums[2], LEN - 1, axis=1))
        put(h, sums[1] + left + right)
        window.pop(0)


def every_chunk(body):
    def wide(index, carry):
        at = pl.multiple_of(index * 16, 16)
        body(at, lambda h: pl.ds(pl.multiple_of(wide_at(h) + at, 16), 16))
        return carry

    def last(index, carry):
        at = pl.multiple_of(index * 16, 16)
        body(at + 128, lambda h: pl.ds(pl.multiple_of(narrow_at(h) + at, 16), 16))
        return carry

    lax.fori_loop(0, 8, wide, 0)
    lax.fori_loop(0, 4, last, 0)


def rows_at(h, start):
    return pl.ds(pl.multiple_of(h * CH + start, 16), 16)


def spread_taps(taps_ref, start, order):
    taps = taps_ref[pl.ds(pl.multiple_of(start, 16), 16), :]
    return [jnp.broadcast_to(taps[:, k : k + 1], (16, LEN)) for k in order]


def hidden_kernel(received_ref, table_ref, taps_ref, signal_ref, hidden_ref, filtered_ref):
    for at in range(0, SENT, 128):
        block = tn(received_ref[:, at : at + 128], table_ref[...])
        filtered_ref[at : at + 128] = block.astype(BF16)

    def chunk(start, place):
        def load(h):
            return filtered_ref[place(h), :].astype(F32)

        def put(h, convolved):
            at = rows_at(h, start)
            hidden_ref[at, :] = (signal_ref[at, :].astype(F32) + convolved).astype(BF16)

        convolve(load, range(SLAB), spread_taps(taps_ref, start, range(9)), put)

    every_chunk(chunk)


def gradient_columns_kernel(upstream_ref, mlp_ref, taps_ref, table_ref, message_ref, lanes_ref):
    def chunk(start, place):
        def load(h):
            if h < 0 or h >= SLAB:
                return None
            at = rows_at(h, start)
            return upstream_ref[at, :].astype(F32) + mlp_ref[at, :].astype(F32)

        def put(h, convolved):
            lanes_ref[place(h), :] = convolved.astype(BF16)

        convolve(
            load, range(-1, SLAB + 1), spread_taps(taps_ref, start, range(8, -1, -1)), put
        )

    every_chunk(chunk)
    send_columns(table_ref, lanes_ref, message_ref)


def gelu_parts(pre_act):
    cumulative = 0.5 * (1.0 + lax.erf(pre_act * root_half))
    bell = density * jnp.exp(-0.5 * pre_act * pre_act)
    return pre_act * cumulative, cumulative + pre_act * bell


def mlp_kernel(
    channel_ref,
    hidden_ref,
    own_dy_ref,
    dy_one_ref,
    dy_two_ref,
    dy_three_ref,
    gain_ref,
    unit_ref,
    mine_ref,
    other_ref,
    out_own_ref,
    out_one_ref,
    out_two_ref,
    out_three_ref,
    grad_ref,
    parts_ref,
    gathered_ref,
    scaled_ref,
    dy_ref,
    normed_ref,
    inv_ref,
    out_sum_ref,
    grad_sum_ref,
):
    step = pl.program_id(0)
    channel = channel_ref[0]

    def turn_in(half):
        for src in range(CH_DEVICES):
            at = src * 2 * CH + half * CH
            gathered_ref[src * CH : (src + 1) * CH] = hidden_ref[at : at + CH]
        return nt(unit_ref[...], gathered_ref[...])

    def turn_in_dy(half):
        for src in range(CH_DEVICES):
            gathered_ref[src * CH : (src + 1) * CH] = parts_ref[src, half * CH : half * CH + CH]
        return nt(unit_ref[...], gathered_ref[...])

    @pl.when(step == 0)
    def _():
        for turn, source_ref in enumerate((own_dy_ref, dy_one_ref, dy_two_ref, dy_three_ref)):
            parts_ref[lax.rem(channel + CH_DEVICES - turn, CH_DEVICES)] = source_ref[...]
        for half in range(2):
            rows = slice(half * LEN, half * LEN + LEN)
            values = turn_in(half)
            centred = values - jnp.mean(values, axis=1, keepdims=True)
            variance = jnp.mean(centred * centred, axis=1, keepdims=True)
            inv_std = lax.rsqrt(variance + norm_epsilon)
            normed = centred * inv_std
            normed_ref[rows] = normed
            inv_ref[rows] = jnp.broadcast_to(inv_std, (LEN, 128))
            scaled_ref[rows] = (normed * gain_ref[...]).astype(BF16)
            dy_ref[rows] = turn_in_dy(half).astype(BF16)
        out_sum_ref[...] = jnp.zeros_like(out_sum_ref)
        grad_sum_ref[...] = jnp.zeros_like(grad_sum_ref)

    for weights_ref in (mine_ref, other_ref):
        up, down = weights_ref[:, :ALL_CH], weights_ref[:, ALL_CH:]
        pre_act = nt(scaled_ref[...], up)
        grad_act = nt(dy_ref[...], down)
        activated, slope = gelu_parts(pre_act)
        out_sum_ref[...] += nn(activated.astype(BF16), down)
        grad_sum_ref[...] += nn((grad_act * slope).astype(BF16), up)

    def turn_out(values, half, put):
        for block in range(3):
            piece = nt(unit_ref[...], values[:, block * LEN : (block + 1) * LEN])
            gathered_ref[block * LEN : (block + 1) * LEN] = piece.astype(BF16)
        for dst in range(CH_DEVICES):
            put(dst, half, gathered_ref[dst * CH : (dst + 1) * CH])

    def put_grad(dst, half, rows):
        at = (dst * 2 + half) * CH
        grad_ref[at : at + CH] = rows

    def put_out(dst, half, rows):
        parts_ref[dst, half * CH : half * CH + CH] = rows

    @pl.when(step == pl.num_programs(0) - 1)
    def _():
        for half in range(2):
            rows = slice(half * LEN, half * LEN + LEN)
            weighted = grad_sum_ref[rows] * gain_ref[...]
            normed = normed_ref[rows]
            first = jnp.mean(weighted, axis=1, keepdims=True)
            second = jnp.mean(weighted * normed, axis=1, keepdims=True)
            term = inv_ref[rows, 0:1] * (weighted - first - normed * second)
            turn_out(term.astype(BF16), half, put_grad)
            turn_out(out_sum_ref[rows].astype(BF16), half, put_out)
        for turn, out_ref in enumerate((out_own_ref, out_one_ref, out_two_ref, out_three_ref)):
            out_ref[...] = parts_ref[lax.rem(channel + turn, CH_DEVICES)]


def mlp(channel, hidden, dy_parts, gain, weights, block=256):
    tokens, steps = 2 * LEN, UNITS // 2 // block
    part = whole_block((2 * CH, LEN))
    return pl.pallas_call(
        mlp_kernel,
        name="mlp",
        grid=(steps,),
        out_shape=(*(shape((2 * CH, LEN), BF16),) * CH_DEVICES, shape((LANES, LEN), BF16)),
        in_specs=[
            pl.BlockSpec(memory_space=pltpu.SMEM),
            whole_block((LANES, LEN)),
            part,
            part,
            part,
            part,
            whole_block((1, ALL_CH)),
            whole_block((LEN, LEN)),
            pl.BlockSpec((block, 2 * ALL_CH), lambda i: (i, 0)),
            pl.BlockSpec((block, 2 * ALL_CH), lambda i: (i + steps, 0)),
        ],
        out_specs=(part, part, part, part, whole_block((LANES, LEN))),
        scratch_shapes=[
            pltpu.VMEM((CH_DEVICES, 2 * CH, LEN), BF16),
            pltpu.VMEM((ALL_CH, LEN), BF16),
            pltpu.VMEM((tokens, ALL_CH), BF16),
            pltpu.VMEM((tokens, ALL_CH), BF16),
            pltpu.VMEM((tokens, ALL_CH), F32),
            pltpu.VMEM((tokens, 128), F32),
            pltpu.VMEM((tokens, ALL_CH), F32),
            pltpu.VMEM((tokens, ALL_CH), F32),
        ],
        cost_estimate=pl.CostEstimate(
            flops=8 * tokens * UNITS * ALL_CH,
            bytes_accessed=4 * UNITS * ALL_CH + 8 * LANES * LEN,
            transcendentals=2 * tokens * UNITS,
        ),
        compiler_params=pltpu.CompilerParams(vmem_limit_bytes=48 * MIB),
    )(channel, hidden, *dy_parts, gain, jnp.asarray(UNIT), weights, weights)


def block_out_kernel(channel_ref, hidden_ref, own_ref, one_ref, two_ref, three_ref, out_ref, wide_ref):
    for turn, sum_ref in enumerate((own_ref, one_ref, two_ref, three_ref)):
        src = lax.rem(channel_ref[0] + CH_DEVICES - turn, CH_DEVICES)
        for half in range(2):
            rows = pl.ds(pl.multiple_of((src * 2 + half) * CH, 64), CH)
            total = hidden_ref[rows, :].astype(F32)
            total += sum_ref[half * CH : half * CH + CH].astype(F32)
            put_eighth(wide_ref, src * 2 + half, total)
    out_ref[...] = take_wide(wide_ref).astype(BF16)


def image_kernel(received_ref, table_ref, upstream_ref, mlp_ref, out_ref, wide_ref):
    def place(h, channel, block):
        count = block.shape[0]
        rows = slice(h * CH + channel, h * CH + channel + count)
        total = block + upstream_ref[rows].astype(F32) + mlp_ref[rows].astype(F32)
        put_eighth(wide_ref, channel * SLAB + h, total)

    token_rows(received_ref, table_ref, place)
    out_ref[...] = take_wide(wide_ref)


def grad_filter_kernel(product_ref, straight_ref, out_ref, block_ref, wide_ref):
    for part in range(2):
        for j in range(SLAB):
            rows = slice(j * 32, j * 32 + 32)
            for k2 in range(SLAB):
                to = slice(k2 * 32, k2 * 32 + 32)
                at = WIDE + 64 * k2
                block_ref[to, :128] = product_ref[part, rows, k2 * 128 : k2 * 128 + 128]
                block_ref[to, 128:] = product_ref[part, rows, at : at + 64]
            put_eighth(wide_ref, j, tn(block_ref[...], straight_ref[...]))
        out_ref[part] = take_wide(wide_ref)


def to_peers(values, axis):
    return lax.all_to_all(values, axis, split_axis=0, concat_axis=0, tiled=True)


def turned_exchange(parts):
    received = [parts[0]]
    for turn in range(1, CH_DEVICES):
        pairs = [(i, (i + turn) % CH_DEVICES) for i in range(CH_DEVICES)]
        received.append(lax.ppermute(parts[turn], "ch", pairs))
    return received


def after(value, earlier):
    return lax.optimization_barrier((value, earlier))


def fenced(values, axis, live):
    values, live = lax.optimization_barrier((values, live))
    return lax.optimization_barrier((to_peers(values, axis), live))


def on_device(tile_image, spectral_filter, conv_taps, norm_gain, up_weight, down_weight, upstream):
    channel = lax.axis_index("ch").reshape(1).astype(jnp.int32)
    flat = (LANES, LEN)
    tables = [jnp.asarray(t) for t in (FORWARD_ROWS, INVERSE_ROWS, TWIDDLE_COS, TWIDDLE_SIN)]
    columns, straight = jnp.asarray(COLUMNS), jnp.asarray(STRAIGHT)
    wide = pltpu.VMEM((2, LANES, 128), F32)
    message, signal = kernel_call(
        columns_kernel,
        "columns",
        [shape((MESSAGE, LANES), BF16), shape(flat, BF16)],
        [wide, pltpu.VMEM(flat, BF16)],
        [tile_image.reshape(flat), columns],
        16,
        2 * MESSAGE * LEN * LANES,
    )
    received = to_peers(message, ROWS)

    (upstream_rows, filter_rows), _ = after(
        (upstream.reshape(flat), spectral_filter.reshape(2, LANES, LEN)), message
    )
    dy, *dy_turned = kernel_call(
        unfold_kernel,
        "unfold",
        [shape(flat, BF16)] + [shape((2 * CH, LEN), BF16)] * CH_DEVICES,
        [wide],
        [channel, upstream_rows],
        16,
        smem=1,
        beside=True,
    )
    (up_own, down_own), _ = after((up_weight, down_weight), dy_turned)
    start = lax.axis_index("core") * HALF_UNITS
    own_up = lax.dynamic_slice_in_dim(up_own, start, HALF_UNITS, axis=1).T
    own_down = lax.dynamic_slice_in_dim(down_own, start, HALF_UNITS, axis=0)
    pack = jnp.concatenate([own_up, own_down], axis=1)
    weights = lax.all_gather(pack, ("core", "ch"), axis=0, tiled=True)
    dy_parts = turned_exchange(dy_turned)
    (main,) = kernel_call(
        filter_kernel,
        "filter",
        [shape((2, LEN, LANES), BF16)],
        [wide],
        [filter_rows, straight],
        16,
        2 * 16 * LEN * LEN * CH,
        beside=True,
    )
    received, dy_parts, main = lax.optimization_barrier((received, dy_parts, main))
    row_scratch = [pltpu.VMEM((MESSAGE, LANES), F32), pltpu.VMEM((MESSAGE, LANES), BF16)]
    row_flops = 4 * MESSAGE * MESSAGE * LANES
    message, seen = kernel_call(
        rows_forward_kernel,
        "rows_forward",
        [shape((MESSAGE, SENT), BF16), shape((2, LEN, LANES), BF16)],
        row_scratch,
        [received, *tables, main],
        20,
        row_flops,
    )
    live = (seen, main, signal, dy, dy_parts, conv_taps, norm_gain)
    received, live = fenced(message, ROWS, live)
    seen, main, signal, dy, dy_parts, conv_taps, norm_gain = live
    (hidden,) = kernel_call(
        hidden_kernel,
        "hidden",
        [shape(flat, BF16)],
        [pltpu.VMEM((SENT, LEN), BF16)],
        [received, columns, conv_taps, signal],
        16,
        2 * MESSAGE * LEN * SENT,
    )
    live = (seen, main, dy, dy_parts, conv_taps, norm_gain.reshape(1, ALL_CH), hidden)
    hidden_tokens, live = fenced(hidden, "ch", live)
    seen, main, dy, dy_parts, conv_taps, gain_row, hidden = live
    *out_turned, grad_message = mlp(channel, hidden_tokens, dy_parts, gain_row, weights)
    grad_mlp, live = fenced(grad_message, "ch", (seen, main, dy, out_turned, conv_taps, hidden))
    seen, main, dy, out_turned, conv_taps, hidden = live
    (message,) = kernel_call(
        gradient_columns_kernel,
        "gradient_columns",
        [shape((MESSAGE, SENT), BF16)],
        [pltpu.VMEM((SENT, LEN), BF16)],
        [dy, grad_mlp, conv_taps, columns],
        16,
        2 * MESSAGE * LEN * SENT,
    )
    live = (seen, main, dy, out_turned, grad_mlp, hidden)
    received, live = fenced(message, ROWS, live)
    seen, main, dy, out_turned, grad_mlp, hidden = live
    message, products = kernel_call(
        rows_backward_kernel,
        "rows_backward",
        [shape((MESSAGE, LANES), BF16), shape((2, LEN, LANES), BF16)],
        row_scratch,
        [received, *tables, main, seen],
        20,
        row_flops,
    )
    (dy, out_turned, grad_mlp, hidden, products), message = after(
        (dy, out_turned, grad_mlp, hidden, products), message
    )
    received = to_peers(message, ROWS)
    out_parts = turned_exchange(out_turned)
    (block_out,) = kernel_call(
        block_out_kernel, "block_out", [shape(flat, BF16)], [wide], [channel, hidden, *out_parts], 16, smem=1, beside=True
    )
    (grad_filter,) = kernel_call(
        grad_filter_kernel,
        "grad_filter",
        [shape((2, LANES, LEN), F32)],
        [pltpu.VMEM((LEN, CH), BF16), wide],
        [products, straight],
        16,
        2 * 16 * LEN * LEN * CH,
        beside=True,
    )
    (grad_image,) = kernel_call(
        image_kernel,
        "image",
        [shape(flat, F32)],
        [wide],
        [received, columns, dy, grad_mlp],
        16,
        2 * MESSAGE * LEN * LANES,
    )
    slab = (CH, SLAB, LEN)
    return (
        block_out.reshape(slab),
        grad_image.reshape(slab),
        grad_filter.reshape(2, CH, SLAB, LEN),
    )


def solution(mesh):
    devices = mesh.devices.reshape(4, 4, 2, CH_DEVICES)
    token = P("ch", ROWS, None)
    frequency = P(None, "ch", ROWS, None)
    return jax.shard_map(
        on_device,
        mesh=jax.sharding.Mesh(devices, (*ROWS, "ch")),
        in_specs=(token, frequency, P("ch", None), P(), P(None, "ch"), P("ch", None), token),
        out_specs=(token, token, frequency),
        check_vma=False,
    )
```

```python
import functools

import jax
import jax.numpy as jnp
import ml_dtypes
import numpy as np
from jax import lax
from jax.experimental import pallas as pl
from jax.experimental.pallas import tpu as pltpu
from jax.sharding import PartitionSpec as P

norm_epsilon = 1e-05
root_half = 0.7071067811865476
density = 0.3989422804014327

ROWS_DEVICES = 32
CH_DEVICES = 4
LEN = 256
SLAB = 8
CH = 192
ALL_CH = 768
LANES = SLAB * CH
WIDE = SLAB * 128
POINTS = LEN * LEN
HALF_UNITS = 384
UNITS = 3072
ROWS = ("y", "z", "core")
SENT = (SLAB + 2) * CH
F32 = jnp.float32
BF16 = jnp.bfloat16
MIB = 1 << 20


def wide_at(h):
    return {-1: LANES, SLAB: LANES + 128}.get(h, 128 * h)


def narrow_at(h):
    return {-1: LANES + 256, SLAB: LANES + 320}.get(h, WIDE + 64 * (2 * (h % 4) + h // 4))


def columns_of(device):
    base = SLAB * device
    return [base + 1, base + 2, base + 3, base + 4 if device < 16 else base]


def column_tables():
    w = np.arange(LEN)
    forward, inverse = np.zeros((LEN, LEN)), np.zeros((LEN, LEN))
    for device in range(ROWS_DEVICES):
        for j, kw in enumerate(columns_of(device)):
            turn = 2 * np.pi * (kw * w % LEN) / LEN
            re, im = SLAB * device + j, SLAB * device + 4 + j
            if device == 16 and j == 3:
                forward[re] = inverse[re] = 1.0
                forward[im] = inverse[im] = np.where(w % 2 == 0, 1.0, -1.0)
            else:
                forward[re], forward[im] = np.cos(turn), -np.sin(turn)
                inverse[re], inverse[im] = 2 * np.cos(turn), -2 * np.sin(turn)
    return forward, inverse


def row_tables():
    k1, src = np.arange(32)[:, None], np.arange(32)[None, :]
    turn = 2 * np.pi * (k1 * src % 32) / 32
    cos, sin = np.cos(turn), np.sin(turn)
    forward = np.zeros((2, 5, 32, 32, 2, 4))
    inverse = np.zeros((32, 2, 4, 2, 4, 32))
    for j in range(4):
        forward[0, j, :, :, 0, j], forward[0, j, :, :, 1, j] = cos, sin
        forward[1, j, :, :, 0, j], forward[1, j, :, :, 1, j] = -sin, cos
        inverse[:, 0, j, 0, j, :], inverse[:, 0, j, 1, j, :] = cos.T, -sin.T
        inverse[:, 1, j, 0, j, :], inverse[:, 1, j, 1, j, :] = sin.T, cos.T
    forward[0, 4, :, :, 0, 3], forward[0, 4, :, :, 1, 3] = cos, -sin
    forward[1, 4, :, :, 0, 3], forward[1, 4, :, :, 1, 3] = -sin, -cos
    return forward.reshape(320, 256), inverse.reshape(256, 256)


def twiddle_tables():
    token_row = np.zeros(LANES, np.int64)
    for h in range(SLAB):
        token_row[128 * h : 128 * h + 128] = h
        token_row[narrow_at(h) : narrow_at(h) + 64] = h
    turn = 2 * np.pi * (np.arange(32)[:, None] * token_row[None, :] % LEN) / LEN
    return np.cos(turn), np.sin(turn)


def turn_tables():
    k2, k1 = np.divmod(np.arange(LEN), 32)
    kh = k1 + 32 * k2
    straight, mirrored = np.zeros((LEN, LEN)), np.zeros((LEN, LEN))
    straight[np.arange(LEN), kh] = 1.0
    mirrored[np.arange(LEN), -kh % LEN] = 1.0
    return straight, mirrored


def narrow(table):
    return np.asarray(table, np.float64).astype(ml_dtypes.bfloat16)


FORWARD_COLUMNS, INVERSE_COLUMNS = (narrow(t) for t in column_tables())
FORWARD_ROWS, INVERSE_ROWS = (narrow(t) for t in row_tables())
TWIDDLE_COS, TWIDDLE_SIN = (t.astype(np.float32) for t in twiddle_tables())
STRAIGHT, MIRRORED = (narrow(t) for t in turn_tables())
UNIT = narrow(np.eye(LEN))


def nn(a, b):
    return lax.dot_general(a, b, (((1,), (0,)), ((), ())), preferred_element_type=F32)


def nt(a, b):
    return lax.dot_general(a, b, (((1,), (1,)), ((), ())), preferred_element_type=F32)


def tn(a, b):
    return lax.dot_general(a, b, (((0,), (0,)), ((), ())), preferred_element_type=F32)


def whole_block(dims):
    return pl.BlockSpec(dims, lambda *_: (0,) * len(dims), pipeline_mode=pl.Buffered(1))


def kernel_call(body, name, outs, scratch, operands, vmem, flops=0, smem=0, beside=False, hint=0):
    scalar = pl.BlockSpec(memory_space=pltpu.SMEM)
    moved = sum(a.size * a.dtype.itemsize for a in operands)
    moved += sum(o.size * np.dtype(o.dtype).itemsize for o in outs)
    return pl.pallas_call(
        body,
        name=name,
        grid=(1,),
        out_shape=tuple(outs),
        in_specs=[scalar] * smem + [whole_block(a.shape) for a in operands[smem:]],
        out_specs=tuple(whole_block(o.shape) for o in outs),
        scratch_shapes=scratch,
        cost_estimate=pl.CostEstimate(
            flops=0 if beside else flops + hint * 10**9,
            bytes_accessed=1024 if beside else moved,
            transcendentals=0,
        ),
        compiler_params=pltpu.CompilerParams(vmem_limit_bytes=vmem * MIB),
    )(*operands)


def shape(dims, dtype):
    return jax.ShapeDtypeStruct(dims, dtype)


def fill_wide(wide_ref, values):
    for side in range(2):
        wide_ref[side] = values[:, side * 128 : side * 128 + 128]


def every_eighth(wide_ref, h):
    return jnp.concatenate([wide_ref[side, pl.ds(h, CH, stride=SLAB), :] for side in range(2)], axis=1)


def put_eighth(wide_ref, first, values):
    for side in range(2):
        at = pl.ds(first, values.shape[0], stride=SLAB)
        wide_ref[side, at, :] = values[:, side * 128 : side * 128 + 128]


def take_wide(wide_ref):
    return jnp.concatenate([wide_ref[side] for side in range(2)], axis=1)


def unfold_rows(source_ref, wide_ref):
    fill_wide(wide_ref, source_ref[...].astype(F32))
    for h in range(SLAB):
        yield h, every_eighth(wide_ref, h).astype(BF16)


def columns_kernel(image_ref, table_ref, message_ref, kept_ref, wide_ref, lanes_ref):
    for h, rows in unfold_rows(image_ref, wide_ref):
        kept_ref[h * CH : (h + 1) * CH] = rows
        lanes_ref[h * 128 : h * 128 + 128] = rows[:128]
        lanes_ref[narrow_at(h) : narrow_at(h) + 64] = rows[128:]
    send_columns(table_ref, lanes_ref, message_ref)


def send_columns(table_ref, lanes_ref, message_ref):
    for at in range(0, lanes_ref.shape[0], 384):
        message_ref[:, at : at + 384] = nt(table_ref[...], lanes_ref[at : at + 384]).astype(BF16)


def unfold_kernel(channel_ref, source_ref, kept_ref, *refs):
    *turned_refs, wide_ref = refs
    for h, rows in unfold_rows(source_ref, wide_ref):
        kept_ref[h * CH : (h + 1) * CH] = rows
    for turn, turned_ref in enumerate(turned_refs):
        peer = lax.rem(channel_ref[0] + turn, CH_DEVICES)
        for half in range(2):
            rows = every_eighth(wide_ref, peer * 2 + half)
            turned_ref[half * CH : half * CH + CH] = rows.astype(BF16)


def filter_split_kernel(filter_ref, head_ref, tail_ref, lone_ref, wide_ref):
    for part in range(2):
        fill_wide(wide_ref, filter_ref[part])
        for i in range(4):
            tail_ref[i, part] = every_eighth(wide_ref, 4 + i).astype(BF16)
            head_ref[i, part] = every_eighth(wide_ref, i).astype(BF16)
        lone_ref[part] = head_ref[0, part]


def put_spectrum(target_ref, part, column, block):
    rows = slice(column * 32, column * 32 + 32)
    for k2 in range(SLAB):
        piece = block[k2 * 32 : k2 * 32 + 32]
        target_ref[part, rows, k2 * 128 : k2 * 128 + 128] = piece[:, :128]
        at = WIDE + 64 * k2
        target_ref[part, rows, at : at + 64] = piece[:, 128:]


def filter_kernel(
    place_ref, head_ref, tail_ref, pair_ref, lone_ref, straight_ref, mirrored_ref, main_ref, cross_ref
):
    device = place_ref[0]
    low, special = device < 16, device == 16
    scale = 0.5 / POINTS
    for part in range(2):
        sign = 1.0 if part == 0 else -1.0
        for j in range(3):
            straight = nt(straight_ref[...], head_ref[1 + j, part])
            mirrored = nt(mirrored_ref[...], pair_ref[3 - j, part])
            put_spectrum(main_ref, part, j, (straight + sign * mirrored) * scale)
        own = jnp.where(low, tail_ref[0, part], head_ref[0, part])
        other = jnp.where(low, pair_ref[0, part], lone_ref[part])
        o, q = nt(straight_ref[...], own), nt(straight_ref[...], other)
        o_back = nt(mirrored_ref[...], own) * sign
        q_back = nt(mirrored_ref[...], other) * sign
        usual = (o + q_back) * scale
        put_spectrum(
            main_ref, part, 3, jnp.where(special, (o + o_back + q + q_back) * (0.5 * scale), usual)
        )
        put_spectrum(
            cross_ref,
            part,
            0,
            jnp.where(special, (q + q_back - o - o_back) * (0.5 * scale), 0.0 * usual),
        )


def eighth_turn(value, step, sign):
    re, im = value
    if step == 0:
        return value
    if step == 1:
        return (re + sign * im) * root_half, (im - sign * re) * root_half
    if step == 2:
        return sign * im, -sign * re
    return (sign * im - re) * root_half, (-sign * re - im) * root_half


def add(a, b):
    return a[0] + b[0], a[1] + b[1]


def sub(a, b):
    return a[0] - b[0], a[1] - b[1]


def four_points(x, sign):
    s, d = add(x[0], x[2]), sub(x[0], x[2])
    t, u = add(x[1], x[3]), eighth_turn(sub(x[1], x[3]), 2, sign)
    return [add(s, t), add(d, u), sub(s, t), sub(d, u)]


def eight_points(x, sign):
    even = four_points([add(x[m], x[m + 4]) for m in range(4)], sign)
    odd = four_points([eighth_turn(sub(x[m], x[m + 4]), m, sign) for m in range(4)], sign)
    return [part[q] for q in range(4) for part in (even, odd)]


def upper_lanes(like):
    return lax.broadcasted_iota(jnp.int32, like.shape, 1) >= 64


def halves(value):
    upper = upper_lanes(value)
    return pltpu.roll(value, 64, axis=1) + jnp.where(upper, -value, value)


def upper_turn(value, step, sign):
    upper = upper_lanes(value[0])
    return tuple(jnp.where(upper, b, a) for a, b in zip(value, eighth_turn(value, step, sign)))


def narrow_forward(x, sign):
    turned = [upper_turn((halves(re), halves(im)), m, sign) for m, (re, im) in enumerate(x)]
    return four_points(turned, sign)


def narrow_inverse(x, sign):
    turned = [upper_turn(v, m, sign) for m, v in enumerate(four_points(x, sign))]
    return [(halves(re), halves(im)) for re, im in turned]


def lane_blocks(re, im):
    return [(re[:, at : at + 128], im[:, at : at + 128]) for at in range(0, LANES, 128)]


def to_frequencies(re, im, cos, sin):
    x = lane_blocks(re * cos + im * sin, im * cos - re * sin)
    return eight_points(x[:SLAB], 1.0) + narrow_forward(x[SLAB:], 1.0)


def to_tokens_rows(blocks, cos, sin):
    y = eight_points(blocks[:SLAB], -1.0) + narrow_inverse(blocks[SLAB:], -1.0)
    re = jnp.concatenate([v[0] for v in y], axis=1)
    im = jnp.concatenate([v[1] for v in y], axis=1)
    return re * cos - im * sin, im * cos + re * sin


def moved_rows(block, step):
    empty = jnp.zeros((SLAB, block.shape[1]), block.dtype)
    if step > 0:
        return jnp.concatenate([empty, block[:-SLAB]], axis=0)
    return jnp.concatenate([block[SLAB:], empty], axis=0)


def row_body(saves, refs):
    place_ref, received_ref, fwd_ref, inv_ref, cos_ref, sin_ref, main_ref, cross_ref = refs[:8]
    if saves:
        message_ref, seen_ref, mixed_ref, ready_ref = refs[8:]
    else:
        seen_ref, message_ref, product_ref, mixed_ref, ready_ref = refs[8:]

    def joined(at, width, edge, step):
        rows = received_ref[:, at : at + width].astype(F32)
        moved = moved_rows(received_ref[:, edge : edge + width].astype(F32), step)
        return nn(fwd_ref[...], (rows + moved).astype(BF16))

    for at in range(0, LANES, 512):
        mixed_ref[:, at : at + 512] = nn(fwd_ref[...], received_ref[:, at : at + 512])
    if not saves:
        for h, edge, step in ((0, SLAB, 1), (SLAB - 1, -1, -1)):
            at = wide_at(h)
            mixed_ref[:, at : at + 128] = joined(at, 128, wide_at(edge), step)
            at = narrow_at(h)
            mixed_ref[:, at : at + 64] = joined(at, 64, narrow_at(edge), step)

    def spectrum(group):
        at = pl.multiple_of(group * 16, 16)
        table = pl.ds(pl.multiple_of(lax.rem(group, 2) * 16, 16), 16)
        return to_frequencies(
            mixed_ref[pl.ds(at, 16), :],
            mixed_ref[pl.ds(160 + at, 16), :],
            cos_ref[table, :],
            sin_ref[table, :],
        )

    def save(group, blocks):
        at = pl.ds(pl.multiple_of(group * 16, 16), 16)
        for n, value in enumerate(blocks):
            for part in range(2):
                seen_ref[part, at, n * 128 : n * 128 + 128] = value[part].astype(BF16)

    def times(value, n, source_ref, at):
        k_re = source_ref[0, at, n * 128 : n * 128 + 128]
        k_im = source_ref[1, at, n * 128 : n * 128 + 128]
        re, im = value
        if saves:
            return re * k_re - im * k_im, im * k_re + re * k_im
        return re * k_re + im * k_im, im * k_re - re * k_im

    def store_back(group, blocks):
        table = pl.ds(pl.multiple_of(lax.rem(group, 2) * 16, 16), 16)
        re, im = to_tokens_rows(blocks, cos_ref[table, :], sin_ref[table, :])
        at = pl.multiple_of(group * 16, 16)
        ready_ref[pl.ds(at, 16), :] = re.astype(BF16)
        ready_ref[pl.ds(128 + at, 16), :] = im.astype(BF16)

    def seen(group, n):
        at = pl.ds(pl.multiple_of(group * 16, 16), 16)
        return tuple(seen_ref[part, at, n * 128 : n * 128 + 128].astype(F32) for part in range(2))

    def product(a, b, factor):
        re = (a[0] * b[0] + a[1] * b[1]) * factor
        return re, (b[1] * a[0] - b[0] * a[1]) * factor

    def put_product(group, n, value):
        at = pl.ds(pl.multiple_of(group * 16, 16), 16)
        for part in range(2):
            product_ref[part, at, n * 128 : n * 128 + 128] = value[part].astype(BF16)

    def plain(group, carry):
        at = pl.ds(pl.multiple_of(group * 16, 16), 16)
        values = spectrum(group)
        if saves:
            save(group, values)
        else:
            for n, value in enumerate(values):
                put_product(group, n, product(seen(group, n), value, 1.0 / POINTS))
        store_back(group, [times(v, n, main_ref, at) for n, v in enumerate(values)])
        return carry

    def packed(group, carry):
        at = pl.ds(pl.multiple_of(group * 16, 16), 16)
        cross_at = pl.ds(pl.multiple_of((group - 6) * 16, 16), 16)
        values, mirrors = spectrum(group), spectrum(group + 2)
        if saves:
            save(group, values)
            save(group + 2, mirrors)
        else:
            special = place_ref[0] == 16
            for n, (value, mirror) in enumerate(zip(values, mirrors)):
                first, first_mirror = seen(group, n), seen(group + 2, n)
                usual = product(first, value, 1.0 / POINTS)
                odd = product(sub(first, first_mirror), sub(value, mirror), 0.25 / POINTS)
                even = product(add(first, first_mirror), add(value, mirror), 0.25 / POINTS)
                put_product(group, n, [jnp.where(special, a, b) for a, b in zip(odd, usual)])
                put_product(group + 2, n, [jnp.where(special, a, b) for a, b in zip(even, usual)])
        store_back(
            group,
            [
                add(times(v, n, main_ref, at), times(m, n, cross_ref, cross_at))
                for n, (v, m) in enumerate(zip(values, mirrors))
            ],
        )
        return carry

    lax.fori_loop(0, 6, plain, 0)
    lax.fori_loop(6, 8, packed, 0)
    for at in range(0, LANES, 512):
        block = nn(inv_ref[...], ready_ref[:, at : at + 512])
        message_ref[:, at : at + 512] = block.astype(BF16)
        if saves:
            for h, edge, step in ((0, SLAB, -1), (SLAB - 1, -1, 1)):
                for place, width in ((wide_at, 128), (narrow_at, 64)):
                    start = place(h) - at
                    if 0 <= start < 512:
                        moved = moved_rows(block[:, start : start + width], step)
                        message_ref[:, place(edge) : place(edge) + width] = moved.astype(BF16)


def rows_forward_kernel(*refs):
    row_body(True, refs)


def rows_backward_kernel(*refs):
    row_body(False, refs)


def token_rows(received_ref, table_ref, place):
    for h in range(SLAB):
        place(h, 0, tn(received_ref[:, h * 128 : h * 128 + 128], table_ref[...]))
    for m in range(4):
        at = WIDE + 128 * m
        block = tn(received_ref[:, at : at + 128], table_ref[...])
        place(m, 128, block[:64])
        place(m + 4, 128, block[64:])


def convolve(load, rows, taps, put):
    lane = lax.broadcasted_iota(jnp.int32, (16, LEN), 1)
    window = [load(rows[0] - 1), load(rows[0])]
    for h in rows:
        window.append(load(h + 1))
        sums = []
        for b in range(3):
            terms = [taps[3 * a + b] * w for a, w in enumerate(window) if w is not None]
            sums.append(sum(terms[1:], terms[0]))
        left = jnp.where(lane == 0, 0.0, pltpu.roll(sums[0], 1, axis=1))
        right = jnp.where(lane == LEN - 1, 0.0, pltpu.roll(sums[2], LEN - 1, axis=1))
        put(h, sums[1] + left + right)
        window.pop(0)


def every_chunk(body):
    def wide(index, carry):
        at = pl.multiple_of(index * 16, 16)
        body(at, lambda h: pl.ds(pl.multiple_of(wide_at(h) + at, 16), 16))
        return carry

    def last(index, carry):
        at = pl.multiple_of(index * 16, 16)
        body(at + 128, lambda h: pl.ds(pl.multiple_of(narrow_at(h) + at, 16), 16))
        return carry

    lax.fori_loop(0, 8, wide, 0)
    lax.fori_loop(0, 4, last, 0)


def rows_at(h, start):
    return pl.ds(pl.multiple_of(h * CH + start, 16), 16)


def spread_taps(taps_ref, start, order):
    taps = taps_ref[pl.ds(pl.multiple_of(start, 16), 16), :]
    return [jnp.broadcast_to(taps[:, k : k + 1], (16, LEN)) for k in order]


def hidden_kernel(received_ref, table_ref, taps_ref, signal_ref, hidden_ref, filtered_ref):
    for at in range(0, SENT, 128):
        block = tn(received_ref[:, at : at + 128], table_ref[...])
        filtered_ref[at : at + 128] = block.astype(BF16)

    def chunk(start, place):
        def load(h):
            return filtered_ref[place(h), :].astype(F32)

        def put(h, convolved):
            at = rows_at(h, start)
            hidden_ref[at, :] = (signal_ref[at, :].astype(F32) + convolved).astype(BF16)

        convolve(load, range(SLAB), spread_taps(taps_ref, start, range(9)), put)

    every_chunk(chunk)


def gradient_columns_kernel(upstream_ref, mlp_ref, taps_ref, table_ref, message_ref, lanes_ref):
    def chunk(start, place):
        def load(h):
            if h < 0 or h >= SLAB:
                return None
            at = rows_at(h, start)
            return upstream_ref[at, :].astype(F32) + mlp_ref[at, :].astype(F32)

        def put(h, convolved):
            lanes_ref[place(h), :] = convolved.astype(BF16)

        convolve(
            load, range(-1, SLAB + 1), spread_taps(taps_ref, start, range(8, -1, -1)), put
        )

    every_chunk(chunk)
    send_columns(table_ref, lanes_ref, message_ref)


def gelu_parts(pre_act):
    cumulative = 0.5 * (1.0 + lax.erf(pre_act * root_half))
    bell = density * jnp.exp(-0.5 * pre_act * pre_act)
    return pre_act * cumulative, cumulative + pre_act * bell


def mlp_kernel(
    channel_ref,
    hidden_ref,
    own_dy_ref,
    dy_one_ref,
    dy_two_ref,
    dy_three_ref,
    gain_ref,
    unit_ref,
    mine_ref,
    other_ref,
    out_own_ref,
    out_one_ref,
    out_two_ref,
    out_three_ref,
    grad_ref,
    parts_ref,
    gathered_ref,
    scaled_ref,
    dy_ref,
    normed_ref,
    inv_ref,
    out_sum_ref,
    grad_sum_ref,
):
    step = pl.program_id(0)
    channel = channel_ref[0]

    def turn_in(half):
        for src in range(CH_DEVICES):
            at = src * 2 * CH + half * CH
            gathered_ref[src * CH : (src + 1) * CH] = hidden_ref[at : at + CH]
        return nt(unit_ref[...], gathered_ref[...])

    def turn_in_dy(half):
        for src in range(CH_DEVICES):
            gathered_ref[src * CH : (src + 1) * CH] = parts_ref[src, half * CH : half * CH + CH]
        return nt(unit_ref[...], gathered_ref[...])

    @pl.when(step == 0)
    def _():
        for turn, source_ref in enumerate((own_dy_ref, dy_one_ref, dy_two_ref, dy_three_ref)):
            parts_ref[lax.rem(channel + CH_DEVICES - turn, CH_DEVICES)] = source_ref[...]
        for half in range(2):
            rows = slice(half * LEN, half * LEN + LEN)
            values = turn_in(half)
            centred = values - jnp.mean(values, axis=1, keepdims=True)
            variance = jnp.mean(centred * centred, axis=1, keepdims=True)
            inv_std = lax.rsqrt(variance + norm_epsilon)
            normed = centred * inv_std
            normed_ref[rows] = normed
            inv_ref[rows] = jnp.broadcast_to(inv_std, (LEN, 128))
            scaled_ref[rows] = (normed * gain_ref[...]).astype(BF16)
            dy_ref[rows] = turn_in_dy(half).astype(BF16)
        out_sum_ref[...] = jnp.zeros_like(out_sum_ref)
        grad_sum_ref[...] = jnp.zeros_like(grad_sum_ref)

    for weights_ref in (mine_ref, other_ref):
        up, down = weights_ref[:, :ALL_CH], weights_ref[:, ALL_CH:]
        pre_act = nt(scaled_ref[...], up)
        grad_act = nt(dy_ref[...], down)
        activated, slope = gelu_parts(pre_act)
        out_sum_ref[...] += nn(activated.astype(BF16), down)
        grad_sum_ref[...] += nn((grad_act * slope).astype(BF16), up)

    def turn_out(values, half, put):
        for block in range(3):
            piece = nt(unit_ref[...], values[:, block * LEN : (block + 1) * LEN])
            gathered_ref[block * LEN : (block + 1) * LEN] = piece.astype(BF16)
        for dst in range(CH_DEVICES):
            put(dst, half, gathered_ref[dst * CH : (dst + 1) * CH])

    def put_grad(dst, half, rows):
        at = (dst * 2 + half) * CH
        grad_ref[at : at + CH] = rows

    def put_out(dst, half, rows):
        parts_ref[dst, half * CH : half * CH + CH] = rows

    @pl.when(step == pl.num_programs(0) - 1)
    def _():
        for half in range(2):
            rows = slice(half * LEN, half * LEN + LEN)
            weighted = grad_sum_ref[rows] * gain_ref[...]
            normed = normed_ref[rows]
            first = jnp.mean(weighted, axis=1, keepdims=True)
            second = jnp.mean(weighted * normed, axis=1, keepdims=True)
            term = inv_ref[rows, 0:1] * (weighted - first - normed * second)
            turn_out(term.astype(BF16), half, put_grad)
            turn_out(out_sum_ref[rows].astype(BF16), half, put_out)
        for turn, out_ref in enumerate((out_own_ref, out_one_ref, out_two_ref, out_three_ref)):
            out_ref[...] = parts_ref[lax.rem(channel + turn, CH_DEVICES)]


def mlp(channel, hidden, dy_parts, gain, weights, block=256):
    tokens, steps = 2 * LEN, UNITS // 2 // block
    part = whole_block((2 * CH, LEN))
    return pl.pallas_call(
        mlp_kernel,
        name="mlp",
        grid=(steps,),
        out_shape=(*(shape((2 * CH, LEN), BF16),) * CH_DEVICES, shape((LANES, LEN), BF16)),
        in_specs=[
            pl.BlockSpec(memory_space=pltpu.SMEM),
            whole_block((LANES, LEN)),
            part,
            part,
            part,
            part,
            whole_block((1, ALL_CH)),
            whole_block((LEN, LEN)),
            pl.BlockSpec((block, 2 * ALL_CH), lambda i: (i, 0)),
            pl.BlockSpec((block, 2 * ALL_CH), lambda i: (i + steps, 0)),
        ],
        out_specs=(part, part, part, part, whole_block((LANES, LEN))),
        scratch_shapes=[
            pltpu.VMEM((CH_DEVICES, 2 * CH, LEN), BF16),
            pltpu.VMEM((ALL_CH, LEN), BF16),
            pltpu.VMEM((tokens, ALL_CH), BF16),
            pltpu.VMEM((tokens, ALL_CH), BF16),
            pltpu.VMEM((tokens, ALL_CH), F32),
            pltpu.VMEM((tokens, 128), F32),
            pltpu.VMEM((tokens, ALL_CH), F32),
            pltpu.VMEM((tokens, ALL_CH), F32),
        ],
        cost_estimate=pl.CostEstimate(
            flops=8 * tokens * UNITS * ALL_CH,
            bytes_accessed=4 * UNITS * ALL_CH + 8 * LANES * LEN,
            transcendentals=2 * tokens * UNITS,
        ),
        compiler_params=pltpu.CompilerParams(vmem_limit_bytes=48 * MIB),
    )(channel, hidden, *dy_parts, gain, jnp.asarray(UNIT), weights, weights)


def block_out_kernel(channel_ref, hidden_ref, own_ref, one_ref, two_ref, three_ref, out_ref, wide_ref):
    for turn, sum_ref in enumerate((own_ref, one_ref, two_ref, three_ref)):
        src = lax.rem(channel_ref[0] + CH_DEVICES - turn, CH_DEVICES)
        for half in range(2):
            rows = pl.ds(pl.multiple_of((src * 2 + half) * CH, 64), CH)
            total = hidden_ref[rows, :].astype(F32)
            total += sum_ref[half * CH : half * CH + CH].astype(F32)
            put_eighth(wide_ref, src * 2 + half, total)
    out_ref[...] = take_wide(wide_ref).astype(BF16)


def image_kernel(received_ref, table_ref, upstream_ref, mlp_ref, out_ref, wide_ref):
    def place(h, channel, block):
        count = block.shape[0]
        rows = slice(h * CH + channel, h * CH + channel + count)
        total = block + upstream_ref[rows].astype(F32) + mlp_ref[rows].astype(F32)
        put_eighth(wide_ref, channel * SLAB + h, total)

    token_rows(received_ref, table_ref, place)
    out_ref[...] = take_wide(wide_ref)


def unturn_kernel(product_ref, straight_ref, mirrored_ref, own_ref, pair_ref, lone_ref, block_ref):
    def gather(part, column):
        rows = slice(column * 32, column * 32 + 32)
        for k2 in range(SLAB):
            to = slice(k2 * 32, k2 * 32 + 32)
            at = WIDE + 64 * k2
            block_ref[to, :128] = product_ref[part, rows, k2 * 128 : k2 * 128 + 128]
            block_ref[to, 128:] = product_ref[part, rows, at : at + 64]

    for part in range(2):
        sign = 1.0 if part == 0 else -1.0
        for j in range(4):
            gather(part, j)
            own_ref[j, part] = tn(block_ref[...], straight_ref[...]).astype(BF16)
            pair_ref[3 - j, part] = (tn(block_ref[...], mirrored_ref[...]) * sign).astype(BF16)
        gather(part, 4)
        lone_ref[part] = (tn(block_ref[...], mirrored_ref[...]) * sign).astype(BF16)


def grad_filter_kernel(place_ref, own_ref, pair_ref, lone_ref, out_ref, wide_ref):
    low = place_ref[0] < 16
    for part in range(2):
        parts = [jnp.where(low, lone_ref[part], own_ref[3, part])]
        parts += [own_ref[j, part] for j in range(3)]
        parts += [jnp.where(low, own_ref[3, part], pair_ref[0, part])]
        parts += [pair_ref[n, part] for n in range(1, 4)]
        for i, value in enumerate(parts):
            put_eighth(wide_ref, i, value.astype(F32))
        out_ref[part] = take_wide(wide_ref)


def to_peers(values, axis):
    return lax.all_to_all(values, axis, split_axis=0, concat_axis=0, tiled=True)


def turned_exchange(parts):
    received = [parts[0]]
    for turn in range(1, CH_DEVICES):
        pairs = [(i, (i + turn) % CH_DEVICES) for i in range(CH_DEVICES)]
        received.append(lax.ppermute(parts[turn], "ch", pairs))
    return received


def after(value, earlier):
    return lax.optimization_barrier((value, earlier))


def fenced(values, axis, live):
    values, live = lax.optimization_barrier((values, live))
    return lax.optimization_barrier((to_peers(values, axis), live))


def on_device(tile_image, spectral_filter, conv_taps, norm_gain, up_weight, down_weight, upstream):
    device = lax.axis_index(ROWS)
    place = device.reshape(1).astype(jnp.int32)
    channel = lax.axis_index("ch").reshape(1).astype(jnp.int32)
    flat = (LANES, LEN)
    tables = [jnp.asarray(t) for t in (FORWARD_ROWS, INVERSE_ROWS, TWIDDLE_COS, TWIDDLE_SIN)]
    forward_columns, inverse_columns = jnp.asarray(FORWARD_COLUMNS), jnp.asarray(INVERSE_COLUMNS)
    straight, mirrored = jnp.asarray(STRAIGHT), jnp.asarray(MIRRORED)

    wide = pltpu.VMEM((2, LANES, 128), F32)
    head, tail, lone = kernel_call(
        filter_split_kernel,
        "filter_split",
        [shape((4, 2, CH, LEN), BF16), shape((4, 2, CH, LEN), BF16), shape((2, CH, LEN), BF16)],
        [wide],
        [spectral_filter.reshape(2, LANES, LEN)],
        16,
    )
    opposite = [(i, ROWS_DEVICES - 1 - i) for i in range(ROWS_DEVICES)]
    lone_in = [(i, ROWS_DEVICES - i) for i in range(1, 16)] + [(0, 16)]
    pair_filter = lax.ppermute(tail, ROWS, opposite)
    lone_filter = lax.ppermute(lone, ROWS, lone_in)
    image_rows, _ = after(tile_image.reshape(flat), (tail, lone))
    message, signal = kernel_call(
        columns_kernel,
        "columns",
        [shape((LEN, LANES), BF16), shape(flat, BF16)],
        [wide, pltpu.VMEM(flat, BF16)],
        [image_rows, forward_columns],
        16,
        2 * LEN * LEN * LANES,
    )
    received = to_peers(message, ROWS)
    upstream_rows, _ = after(upstream.reshape(flat), message)
    dy, *dy_turned = kernel_call(
        unfold_kernel,
        "unfold",
        [shape(flat, BF16)] + [shape((2 * CH, LEN), BF16)] * CH_DEVICES,
        [wide],
        [channel, upstream_rows],
        16,
        smem=1,
        hint=6,
    )

    (up_here, down_here), _ = after((up_weight, down_weight), dy_turned)
    start = lax.axis_index("core") * HALF_UNITS
    own_up = lax.dynamic_slice_in_dim(up_here, start, HALF_UNITS, axis=1).T
    own_down = lax.dynamic_slice_in_dim(down_here, start, HALF_UNITS, axis=0)
    pack = jnp.concatenate([own_up, own_down], axis=1)
    weights = lax.all_gather(pack, ("core", "ch"), axis=0, tiled=True)
    dy_parts = turned_exchange(dy_turned)
    main, cross = kernel_call(
        filter_kernel,
        "filter",
        [shape((2, 128, LANES), F32), shape((2, 32, LANES), F32)],
        [],
        [place, head, tail, pair_filter, lone_filter, straight, mirrored],
        16,
        2 * 14 * LEN * LEN * CH,
        smem=1,
        hint=6,
    )

    row_scratch = [pltpu.VMEM((320, LANES), F32), pltpu.VMEM((LEN, LANES), BF16)]
    message, seen = kernel_call(
        rows_forward_kernel,
        "rows_forward",
        [shape((LEN, SENT), BF16), shape((2, 160, LANES), BF16)],
        row_scratch,
        [place, received, *tables, main, cross],
        20,
        2 * 576 * LEN * LANES,
        smem=1,
    )
    received, live = fenced(message, ROWS, (seen, main, cross, signal, dy))
    seen, main, cross, signal, dy = live
    (hidden,) = kernel_call(
        hidden_kernel,
        "hidden",
        [shape(flat, BF16)],
        [pltpu.VMEM((SENT, LEN), BF16)],
        [received, inverse_columns, conv_taps, signal],
        16,
        2 * LEN * LEN * SENT,
    )
    hidden_tokens, live = fenced(hidden, "ch", (seen, main, cross, dy, hidden))
    seen, main, cross, dy, hidden = live
    *out_turned, grad_message = mlp(
        channel, hidden_tokens, dy_parts, norm_gain.reshape(1, ALL_CH), weights
    )
    live = (seen, main, cross, dy, out_turned, hidden)
    grad_mlp, live = fenced(grad_message, "ch", live)
    seen, main, cross, dy, out_turned, hidden = live
    (message,) = kernel_call(
        gradient_columns_kernel,
        "gradient_columns",
        [shape((LEN, SENT), BF16)],
        [pltpu.VMEM((SENT, LEN), BF16)],
        [dy, grad_mlp, conv_taps, forward_columns],
        16,
        2 * LEN * LEN * SENT,
    )
    live = (seen, main, cross, dy, out_turned, grad_mlp, hidden)
    received, live = fenced(message, ROWS, live)
    seen, main, cross, dy, out_turned, grad_mlp, hidden = live
    message, products = kernel_call(
        rows_backward_kernel,
        "rows_backward",
        [shape((LEN, LANES), BF16), shape((2, 160, LANES), BF16)],
        row_scratch,
        [place, received, *tables, main, cross, seen],
        20,
        2 * 576 * LEN * LANES,
        smem=1,
    )
    (dy, out_turned, grad_mlp, hidden), (message, products) = after(
        (dy, out_turned, grad_mlp, hidden), (message, products)
    )
    received = to_peers(message, ROWS)
    own, pair, lone = kernel_call(
        unturn_kernel,
        "unturn",
        [shape((4, 2, CH, LEN), BF16), shape((4, 2, CH, LEN), BF16), shape((2, CH, LEN), BF16)],
        [pltpu.VMEM((LEN, CH), BF16)],
        [products, straight, mirrored],
        16,
        2 * 18 * LEN * LEN * CH,
        beside=True,
    )
    out_parts = turned_exchange(out_turned)
    (block_out,) = kernel_call(
        block_out_kernel,
        "block_out",
        [shape(flat, BF16)],
        [wide],
        [channel, hidden, *out_parts],
        16,
        smem=1,
        beside=True,
    )
    pair = lax.ppermute(pair, ROWS, opposite)
    lone = lax.ppermute(lone, ROWS, [(b, a) for a, b in lone_in])
    (grad_filter,) = kernel_call(
        grad_filter_kernel,
        "grad_filter",
        [shape((2, LANES, LEN), F32)],
        [wide],
        [place, own, pair, lone],
        16,
        smem=1,
    )
    (grad_image,) = kernel_call(
        image_kernel,
        "image",
        [shape(flat, F32)],
        [wide],
        [received, inverse_columns, dy, grad_mlp],
        16,
        2 * LEN * LEN * LANES,
    )
    slab = (CH, SLAB, LEN)
    return (
        block_out.reshape(slab),
        grad_image.reshape(slab),
        grad_filter.reshape(2, CH, SLAB, LEN),
    )


def solution(mesh):
    devices = mesh.devices.reshape(4, 4, 2, CH_DEVICES)
    token = P("ch", ROWS, None)
    frequency = P(None, "ch", ROWS, None)
    return jax.shard_map(
        on_device,
        mesh=jax.sharding.Mesh(devices, (*ROWS, "ch")),
        in_specs=(token, frequency, P("ch", None), P(), P(None, "ch"), P("ch", None), token),
        out_specs=(token, token, frequency),
        check_vma=False,
    )
```

```python
import jax
import jax.numpy as jnp
import ml_dtypes
import numpy as np
from jax import lax
from jax.experimental import pallas as pl
from jax.experimental.pallas import tpu as pltpu
from jax.sharding import PartitionSpec as P

norm_epsilon = 1e-05
root_half = 0.7071067811865476
density = 0.3989422804014327

ROWS_DEVICES = 32
CH_DEVICES = 4
LEN = 256
SLAB = 8
CH = 192
ALL_CH = 768
LANES = SLAB * CH
WIDE = SLAB * 128
POINTS = LEN * LEN
HALF_UNITS = 384
MESSAGE = 2 * LEN
UNITS = 3072
ROWS = ("y", "z", "core")
SENT = (SLAB + 2) * CH
F32 = jnp.float32
BF16 = jnp.bfloat16
MIB = 1 << 20


def wide_at(h):
    return {-1: LANES, SLAB: LANES + 128}.get(h, 128 * h)


def narrow_at(h):
    return {-1: LANES + 256, SLAB: LANES + 320}.get(h, WIDE + 64 * (2 * (h % 4) + h // 4))


def column_tables():
    w, kw = np.arange(LEN)[None, :], np.arange(LEN)[:, None]
    turn = (2 * np.pi * (kw * w % LEN) / LEN).reshape(ROWS_DEVICES, SLAB, LEN)
    both = np.stack([np.cos(turn), -np.sin(turn)], axis=1)
    return both.reshape(MESSAGE, LEN)


def row_tables():
    k1, src = np.arange(32)[:, None], np.arange(32)[None, :]
    turn = 2 * np.pi * (k1 * src % 32) / 32
    cos, sin = np.cos(turn), np.sin(turn)
    forward = np.zeros((2, SLAB, 32, 32, 2, SLAB))
    inverse = np.zeros((32, 2, SLAB, 2, SLAB, 32))
    for j in range(SLAB):
        forward[0, j, :, :, 0, j], forward[0, j, :, :, 1, j] = cos, sin
        forward[1, j, :, :, 0, j], forward[1, j, :, :, 1, j] = -sin, cos
        inverse[:, 0, j, 0, j, :], inverse[:, 0, j, 1, j, :] = cos.T, -sin.T
        inverse[:, 1, j, 0, j, :], inverse[:, 1, j, 1, j, :] = sin.T, cos.T
    return forward.reshape(MESSAGE, MESSAGE), inverse.reshape(MESSAGE, MESSAGE)


def twiddle_tables():
    token_row = np.zeros(LANES, np.int64)
    for h in range(SLAB):
        token_row[128 * h : 128 * h + 128] = h
        token_row[narrow_at(h) : narrow_at(h) + 64] = h
    turn = 2 * np.pi * (np.arange(32)[:, None] * token_row[None, :] % LEN) / LEN
    return np.cos(turn), np.sin(turn)


def turn_table():
    k2, k1 = np.divmod(np.arange(LEN), 32)
    straight = np.zeros((LEN, LEN))
    straight[np.arange(LEN), k1 + 32 * k2] = 1.0
    return straight


def narrow(table):
    return np.asarray(table, np.float64).astype(ml_dtypes.bfloat16)


COLUMNS = narrow(column_tables())
ROW_TABLES = narrow(np.stack(row_tables()))
TWIDDLES = np.stack(twiddle_tables()).astype(np.float32)
STRAIGHT = narrow(turn_table())
UNIT = narrow(np.eye(LEN))


def nn(a, b):
    return lax.dot_general(a, b, (((1,), (0,)), ((), ())), preferred_element_type=F32)


def nt(a, b):
    return lax.dot_general(a, b, (((1,), (1,)), ((), ())), preferred_element_type=F32)


def tn(a, b):
    return lax.dot_general(a, b, (((0,), (0,)), ((), ())), preferred_element_type=F32)


def whole_block(dims):
    return pl.BlockSpec(dims, lambda *_: (0,) * len(dims), pipeline_mode=pl.Buffered(1))


def kernel_call(body, name, outs, scratch, operands, vmem, flops=0, smem=0, beside=False):
    scalar = pl.BlockSpec(memory_space=pltpu.SMEM)
    moved = sum(a.size * a.dtype.itemsize for a in operands)
    moved += sum(o.size * np.dtype(o.dtype).itemsize for o in outs)
    return pl.pallas_call(
        body,
        name=name,
        grid=(1,),
        out_shape=tuple(outs),
        in_specs=[scalar] * smem + [whole_block(a.shape) for a in operands[smem:]],
        out_specs=tuple(whole_block(o.shape) for o in outs),
        scratch_shapes=scratch,
        cost_estimate=pl.CostEstimate(
            flops=0 if beside else flops,
            bytes_accessed=1024 if beside else moved,
            transcendentals=0,
        ),
        compiler_params=pltpu.CompilerParams(vmem_limit_bytes=vmem * MIB),
    )(*operands)


def shape(dims, dtype):
    return jax.ShapeDtypeStruct(dims, dtype)


def fill_wide(wide_ref, values):
    for side in range(2):
        wide_ref[side] = values[:, side * 128 : side * 128 + 128]


def every_eighth(wide_ref, h):
    return jnp.concatenate([wide_ref[side, pl.ds(h, CH, stride=SLAB), :] for side in range(2)], axis=1)


def put_eighth(wide_ref, first, values):
    for side in range(2):
        at = pl.ds(first, values.shape[0], stride=SLAB)
        wide_ref[side, at, :] = values[:, side * 128 : side * 128 + 128]


def take_wide(wide_ref):
    return jnp.concatenate([wide_ref[side] for side in range(2)], axis=1)


def unfold_rows(source_ref, wide_ref):
    fill_wide(wide_ref, source_ref[...].astype(F32))
    for h in range(SLAB):
        yield h, every_eighth(wide_ref, h).astype(BF16)


def columns_kernel(image_ref, table_ref, message_ref, kept_ref, wide_ref, lanes_ref):
    for h, rows in unfold_rows(image_ref, wide_ref):
        kept_ref[h * CH : (h + 1) * CH] = rows
        lanes_ref[h * 128 : h * 128 + 128] = rows[:128]
        lanes_ref[narrow_at(h) : narrow_at(h) + 64] = rows[128:]
    send_columns(table_ref, lanes_ref, message_ref)


def send_columns(table_ref, lanes_ref, message_ref):
    for at in range(0, lanes_ref.shape[0], 384):
        message_ref[:, at : at + 384] = nt(table_ref[...], lanes_ref[at : at + 384]).astype(BF16)


def unfold_kernel(channel_ref, source_ref, kept_ref, *refs):
    *turned_refs, wide_ref = refs
    for h, rows in unfold_rows(source_ref, wide_ref):
        kept_ref[h * CH : (h + 1) * CH] = rows
    for turn, turned_ref in enumerate(turned_refs):
        peer = lax.rem(channel_ref[0] + turn, CH_DEVICES)
        for half in range(2):
            rows = every_eighth(wide_ref, peer * 2 + half)
            turned_ref[half * CH : half * CH + CH] = rows.astype(BF16)


def put_spectrum(target_ref, part, column, block):
    rows = slice(column * 32, column * 32 + 32)
    for k2 in range(SLAB):
        piece = block[k2 * 32 : k2 * 32 + 32]
        target_ref[part, rows, k2 * 128 : k2 * 128 + 128] = piece[:, :128]
        at = WIDE + 64 * k2
        target_ref[part, rows, at : at + 64] = piece[:, 128:]


def filter_kernel(filter_ref, straight_ref, main_ref, wide_ref):
    for part in range(2):
        fill_wide(wide_ref, filter_ref[part])
        for j in range(SLAB):
            turned = nt(straight_ref[...], every_eighth(wide_ref, j).astype(BF16))
            put_spectrum(main_ref, part, j, (turned * (1.0 / POINTS)).astype(BF16))


def eighth_turn(value, step, sign):
    re, im = value
    if step == 0:
        return value
    if step == 1:
        return (re + sign * im) * root_half, (im - sign * re) * root_half
    if step == 2:
        return sign * im, -sign * re
    return (sign * im - re) * root_half, (-sign * re - im) * root_half


def add(a, b):
    return a[0] + b[0], a[1] + b[1]


def sub(a, b):
    return a[0] - b[0], a[1] - b[1]


def four_points(x, sign):
    s, d = add(x[0], x[2]), sub(x[0], x[2])
    t, u = add(x[1], x[3]), eighth_turn(sub(x[1], x[3]), 2, sign)
    return [add(s, t), add(d, u), sub(s, t), sub(d, u)]


def eight_points(x, sign):
    even = four_points([add(x[m], x[m + 4]) for m in range(4)], sign)
    odd = four_points([eighth_turn(sub(x[m], x[m + 4]), m, sign) for m in range(4)], sign)
    return [part[q] for q in range(4) for part in (even, odd)]


def upper_lanes(like):
    return lax.broadcasted_iota(jnp.int32, like.shape, 1) >= 64


def halves(value):
    upper = upper_lanes(value)
    return pltpu.roll(value, 64, axis=1) + jnp.where(upper, -value, value)


def upper_turn(value, step, sign):
    upper = upper_lanes(value[0])
    return tuple(jnp.where(upper, b, a) for a, b in zip(value, eighth_turn(value, step, sign)))


def narrow_forward(x, sign):
    turned = [upper_turn((halves(re), halves(im)), m, sign) for m, (re, im) in enumerate(x)]
    return four_points(turned, sign)


def narrow_inverse(x, sign):
    turned = [upper_turn(v, m, sign) for m, v in enumerate(four_points(x, sign))]
    return [(halves(re), halves(im)) for re, im in turned]


def lane_blocks(re, im):
    return [(re[:, at : at + 128], im[:, at : at + 128]) for at in range(0, LANES, 128)]


def to_frequencies(re, im, cos, sin):
    x = lane_blocks(re * cos + im * sin, im * cos - re * sin)
    return eight_points(x[:SLAB], 1.0) + narrow_forward(x[SLAB:], 1.0)


def to_tokens_rows(blocks, cos, sin):
    y = eight_points(blocks[:SLAB], -1.0) + narrow_inverse(blocks[SLAB:], -1.0)
    re = jnp.concatenate([v[0] for v in y], axis=1)
    im = jnp.concatenate([v[1] for v in y], axis=1)
    return re * cos - im * sin, im * cos + re * sin


def moved_rows(block, step):
    rows = 2 * SLAB
    empty = jnp.zeros((rows, block.shape[1]), block.dtype)
    if step > 0:
        return jnp.concatenate([empty, block[:-rows]], axis=0)
    return jnp.concatenate([block[rows:], empty], axis=0)


def row_body(saves, refs):
    received_ref, tables_ref, twiddles_ref, main_ref = refs[:4]
    if saves:
        message_ref, seen_ref, mixed_ref, ready_ref = refs[4:]
    else:
        seen_ref, message_ref, product_ref, mixed_ref, ready_ref = refs[4:]

    def joined(at, width, edge, step):
        rows = received_ref[:, at : at + width].astype(F32)
        moved = moved_rows(received_ref[:, edge : edge + width].astype(F32), step)
        return nn(tables_ref[0], (rows + moved).astype(BF16))

    for at in range(0, LANES, 512):
        mixed_ref[:, at : at + 512] = nn(tables_ref[0], received_ref[:, at : at + 512])
    if not saves:
        for h, edge, step in ((0, SLAB, 1), (SLAB - 1, -1, -1)):
            at = wide_at(h)
            mixed_ref[:, at : at + 128] = joined(at, 128, wide_at(edge), step)
            at = narrow_at(h)
            mixed_ref[:, at : at + 64] = joined(at, 64, narrow_at(edge), step)

    def group(index, carry):
        at = pl.ds(pl.multiple_of(index * 16, 16), 16)
        at_im = pl.ds(pl.multiple_of(LEN + index * 16, 16), 16)
        table = pl.ds(pl.multiple_of(lax.rem(index, 2) * 16, 16), 16)
        cos, sin = twiddles_ref[0, table, :], twiddles_ref[1, table, :]
        values = to_frequencies(mixed_ref[at, :], mixed_ref[at_im, :], cos, sin)
        filtered = []
        for n, (re, im) in enumerate(values):
            lanes = slice(n * 128, n * 128 + 128)
            k_re, k_im = main_ref[0, at, lanes].astype(F32), main_ref[1, at, lanes].astype(F32)
            if saves:
                seen_ref[0, at, lanes], seen_ref[1, at, lanes] = re.astype(BF16), im.astype(BF16)
                filtered.append((re * k_re - im * k_im, im * k_re + re * k_im))
            else:
                x_re, x_im = seen_ref[0, at, lanes].astype(F32), seen_ref[1, at, lanes].astype(F32)
                product_re = (x_re * re + x_im * im) * (1.0 / POINTS)
                product_im = (im * x_re - re * x_im) * (1.0 / POINTS)
                product_ref[0, at, lanes] = product_re.astype(BF16)
                product_ref[1, at, lanes] = product_im.astype(BF16)
                filtered.append((re * k_re + im * k_im, im * k_re - re * k_im))
        re, im = to_tokens_rows(filtered, cos, sin)
        ready_ref[at, :] = re.astype(BF16)
        ready_ref[at_im, :] = im.astype(BF16)
        return carry

    lax.fori_loop(0, 16, group, 0)
    for at in range(0, LANES, 512):
        block = nn(tables_ref[1], ready_ref[:, at : at + 512])
        message_ref[:, at : at + 512] = block.astype(BF16)
        if saves:
            for h, edge, step in ((0, SLAB, -1), (SLAB - 1, -1, 1)):
                for place, width in ((wide_at, 128), (narrow_at, 64)):
                    start = place(h) - at
                    if 0 <= start < 512:
                        moved = moved_rows(block[:, start : start + width], step)
                        message_ref[:, place(edge) : place(edge) + width] = moved.astype(BF16)


def rows_forward_kernel(*refs):
    row_body(True, refs)


def rows_backward_kernel(*refs):
    row_body(False, refs)


def token_rows(received_ref, table_ref, place):
    for h in range(SLAB):
        place(h, 0, tn(received_ref[:, h * 128 : h * 128 + 128], table_ref[...]))
    for m in range(4):
        at = WIDE + 128 * m
        block = tn(received_ref[:, at : at + 128], table_ref[...])
        place(m, 128, block[:64])
        place(m + 4, 128, block[64:])


def convolve(load, rows, taps, put):
    lane = lax.broadcasted_iota(jnp.int32, (16, LEN), 1)
    window = [load(rows[0] - 1), load(rows[0])]
    for h in rows:
        window.append(load(h + 1))
        sums = []
        for b in range(3):
            terms = [taps[3 * a + b] * w for a, w in enumerate(window) if w is not None]
            sums.append(sum(terms[1:], terms[0]))
        left = jnp.where(lane == 0, 0.0, pltpu.roll(sums[0], 1, axis=1))
        right = jnp.where(lane == LEN - 1, 0.0, pltpu.roll(sums[2], LEN - 1, axis=1))
        put(h, sums[1] + left + right)
        window.pop(0)


def every_chunk(body):
    def wide(index, carry):
        at = pl.multiple_of(index * 16, 16)
        body(at, lambda h: pl.ds(pl.multiple_of(wide_at(h) + at, 16), 16))
        return carry

    def last(index, carry):
        at = pl.multiple_of(index * 16, 16)
        body(at + 128, lambda h: pl.ds(pl.multiple_of(narrow_at(h) + at, 16), 16))
        return carry

    lax.fori_loop(0, 8, wide, 0)
    lax.fori_loop(0, 4, last, 0)


def rows_at(h, start):
    return pl.ds(pl.multiple_of(h * CH + start, 16), 16)


def spread_taps(taps_ref, start, order):
    taps = taps_ref[pl.ds(pl.multiple_of(start, 16), 16), :]
    return [jnp.broadcast_to(taps[:, k : k + 1], (16, LEN)) for k in order]


def hidden_kernel(received_ref, table_ref, taps_ref, signal_ref, hidden_ref, filtered_ref):
    for at in range(0, SENT, 128):
        block = tn(received_ref[:, at : at + 128], table_ref[...])
        filtered_ref[at : at + 128] = block.astype(BF16)

    def chunk(start, place):
        def load(h):
            return filtered_ref[place(h), :].astype(F32)

        def put(h, convolved):
            at = rows_at(h, start)
            hidden_ref[at, :] = (signal_ref[at, :].astype(F32) + convolved).astype(BF16)

        convolve(load, range(SLAB), spread_taps(taps_ref, start, range(9)), put)

    every_chunk(chunk)


def gradient_columns_kernel(upstream_ref, mlp_ref, taps_ref, table_ref, message_ref, lanes_ref):
    def chunk(start, place):
        def load(h):
            if h < 0 or h >= SLAB:
                return None
            at = rows_at(h, start)
            return upstream_ref[at, :].astype(F32) + mlp_ref[at, :].astype(F32)

        def put(h, convolved):
            lanes_ref[place(h), :] = convolved.astype(BF16)

        convolve(
            load, range(-1, SLAB + 1), spread_taps(taps_ref, start, range(8, -1, -1)), put
        )

    every_chunk(chunk)
    send_columns(table_ref, lanes_ref, message_ref)


def gelu_parts(pre_act):
    cumulative = 0.5 * (1.0 + lax.erf(pre_act * root_half))
    bell = density * jnp.exp(-0.5 * pre_act * pre_act)
    return pre_act * cumulative, cumulative + pre_act * bell


def mlp_kernel(
    channel_ref,
    hidden_ref,
    own_dy_ref,
    dy_one_ref,
    dy_two_ref,
    dy_three_ref,
    gain_ref,
    unit_ref,
    mine_ref,
    other_ref,
    out_own_ref,
    out_one_ref,
    out_two_ref,
    out_three_ref,
    grad_ref,
    parts_ref,
    gathered_ref,
    scaled_ref,
    dy_ref,
    normed_ref,
    inv_ref,
    out_sum_ref,
    grad_sum_ref,
):
    step = pl.program_id(0)
    channel = channel_ref[0]

    def turn_in(half):
        for src in range(CH_DEVICES):
            at = src * 2 * CH + half * CH
            gathered_ref[src * CH : (src + 1) * CH] = hidden_ref[at : at + CH]
        return nt(unit_ref[...], gathered_ref[...])

    def turn_in_dy(half):
        for src in range(CH_DEVICES):
            gathered_ref[src * CH : (src + 1) * CH] = parts_ref[src, half * CH : half * CH + CH]
        return nt(unit_ref[...], gathered_ref[...])

    @pl.when(step == 0)
    def _():
        for turn, source_ref in enumerate((own_dy_ref, dy_one_ref, dy_two_ref, dy_three_ref)):
            parts_ref[lax.rem(channel + CH_DEVICES - turn, CH_DEVICES)] = source_ref[...]
        for half in range(2):
            rows = slice(half * LEN, half * LEN + LEN)
            values = turn_in(half)
            centred = values - jnp.mean(values, axis=1, keepdims=True)
            variance = jnp.mean(centred * centred, axis=1, keepdims=True)
            inv_std = lax.rsqrt(variance + norm_epsilon)
            normed = centred * inv_std
            normed_ref[rows] = normed
            inv_ref[rows] = jnp.broadcast_to(inv_std, (LEN, 128))
            scaled_ref[rows] = (normed * gain_ref[...]).astype(BF16)
            dy_ref[rows] = turn_in_dy(half).astype(BF16)
        out_sum_ref[...] = jnp.zeros_like(out_sum_ref)
        grad_sum_ref[...] = jnp.zeros_like(grad_sum_ref)

    for weights_ref in (mine_ref, other_ref):
        up, down = weights_ref[:, :ALL_CH], weights_ref[:, ALL_CH:]
        pre_act = nt(scaled_ref[...], up)
        grad_act = nt(dy_ref[...], down)
        activated, slope = gelu_parts(pre_act)
        out_sum_ref[...] += nn(activated.astype(BF16), down)
        grad_sum_ref[...] += nn((grad_act * slope).astype(BF16), up)

    def turn_out(values, half, put):
        for block in range(3):
            piece = nt(unit_ref[...], values[:, block * LEN : (block + 1) * LEN])
            gathered_ref[block * LEN : (block + 1) * LEN] = piece.astype(BF16)
        for dst in range(CH_DEVICES):
            put(dst, half, gathered_ref[dst * CH : (dst + 1) * CH])

    def put_grad(dst, half, rows):
        at = (dst * 2 + half) * CH
        grad_ref[at : at + CH] = rows

    def put_out(dst, half, rows):
        parts_ref[dst, half * CH : half * CH + CH] = rows

    @pl.when(step == pl.num_programs(0) - 1)
    def _():
        for half in range(2):
            rows = slice(half * LEN, half * LEN + LEN)
            weighted = grad_sum_ref[rows] * gain_ref[...]
            normed = normed_ref[rows]
            first = jnp.mean(weighted, axis=1, keepdims=True)
            second = jnp.mean(weighted * normed, axis=1, keepdims=True)
            term = inv_ref[rows, 0:1] * (weighted - first - normed * second)
            turn_out(term.astype(BF16), half, put_grad)
            turn_out(out_sum_ref[rows].astype(BF16), half, put_out)
        for turn, out_ref in enumerate((out_own_ref, out_one_ref, out_two_ref, out_three_ref)):
            out_ref[...] = parts_ref[lax.rem(channel + turn, CH_DEVICES)]


def mlp(channel, hidden, dy_parts, gain, weights, block=512):
    tokens, steps = 2 * LEN, UNITS // 2 // block
    part = whole_block((2 * CH, LEN))
    return pl.pallas_call(
        mlp_kernel,
        name="mlp",
        grid=(steps,),
        out_shape=(*(shape((2 * CH, LEN), BF16),) * CH_DEVICES, shape((LANES, LEN), BF16)),
        in_specs=[
            pl.BlockSpec(memory_space=pltpu.SMEM),
            whole_block((LANES, LEN)),
            part,
            part,
            part,
            part,
            whole_block((1, ALL_CH)),
            whole_block((LEN, LEN)),
            pl.BlockSpec((block, 2 * ALL_CH), lambda i: (i, 0)),
            pl.BlockSpec((block, 2 * ALL_CH), lambda i: (i + steps, 0)),
        ],
        out_specs=(part, part, part, part, whole_block((LANES, LEN))),
        scratch_shapes=[
            pltpu.VMEM((CH_DEVICES, 2 * CH, LEN), BF16),
            pltpu.VMEM((ALL_CH, LEN), BF16),
            pltpu.VMEM((tokens, ALL_CH), BF16),
            pltpu.VMEM((tokens, ALL_CH), BF16),
            pltpu.VMEM((tokens, ALL_CH), F32),
            pltpu.VMEM((tokens, 128), F32),
            pltpu.VMEM((tokens, ALL_CH), F32),
            pltpu.VMEM((tokens, ALL_CH), F32),
        ],
        cost_estimate=pl.CostEstimate(
            flops=8 * tokens * UNITS * ALL_CH,
            bytes_accessed=4 * UNITS * ALL_CH + 8 * LANES * LEN,
            transcendentals=2 * tokens * UNITS,
        ),
        compiler_params=pltpu.CompilerParams(vmem_limit_bytes=48 * MIB),
    )(channel, hidden, *dy_parts, gain, jnp.asarray(UNIT), weights, weights)


def block_out_kernel(channel_ref, hidden_ref, own_ref, one_ref, two_ref, three_ref, out_ref, wide_ref):
    for turn, sum_ref in enumerate((own_ref, one_ref, two_ref, three_ref)):
        src = lax.rem(channel_ref[0] + CH_DEVICES - turn, CH_DEVICES)
        for half in range(2):
            rows = pl.ds(pl.multiple_of((src * 2 + half) * CH, 64), CH)
            total = hidden_ref[rows, :].astype(F32)
            total += sum_ref[half * CH : half * CH + CH].astype(F32)
            put_eighth(wide_ref, src * 2 + half, total)
    out_ref[...] = take_wide(wide_ref).astype(BF16)


def image_kernel(received_ref, table_ref, upstream_ref, mlp_ref, out_ref, wide_ref):
    def place(h, channel, block):
        count = block.shape[0]
        rows = slice(h * CH + channel, h * CH + channel + count)
        total = block + upstream_ref[rows].astype(F32) + mlp_ref[rows].astype(F32)
        put_eighth(wide_ref, channel * SLAB + h, total)

    token_rows(received_ref, table_ref, place)
    out_ref[...] = take_wide(wide_ref)


def grad_filter_kernel(product_ref, straight_ref, out_ref, block_ref, wide_ref):
    for part in range(2):
        for j in range(SLAB):
            rows = slice(j * 32, j * 32 + 32)
            for k2 in range(SLAB):
                to = slice(k2 * 32, k2 * 32 + 32)
                at = WIDE + 64 * k2
                block_ref[to, :128] = product_ref[part, rows, k2 * 128 : k2 * 128 + 128]
                block_ref[to, 128:] = product_ref[part, rows, at : at + 64]
            put_eighth(wide_ref, j, tn(block_ref[...], straight_ref[...]))
        out_ref[part] = take_wide(wide_ref)


def to_peers(values, axis):
    return lax.all_to_all(values, axis, split_axis=0, concat_axis=0, tiled=True)


def turned_exchange(parts):
    received = [parts[0]]
    for turn in range(1, CH_DEVICES):
        pairs = [(i, (i + turn) % CH_DEVICES) for i in range(CH_DEVICES)]
        received.append(lax.ppermute(parts[turn], "ch", pairs))
    return received


def after(value, earlier):
    return lax.optimization_barrier((value, earlier))


def fenced(values, axis, live):
    values, live = lax.optimization_barrier((values, live))
    return lax.optimization_barrier((to_peers(values, axis), live))


def on_device(tile_image, spectral_filter, conv_taps, norm_gain, up_weight, down_weight, upstream):
    channel = lax.axis_index("ch").reshape(1).astype(jnp.int32)
    flat = (LANES, LEN)
    tables = [jnp.asarray(ROW_TABLES), jnp.asarray(TWIDDLES)]
    columns, straight = jnp.asarray(COLUMNS), jnp.asarray(STRAIGHT)
    wide = pltpu.VMEM((2, LANES, 128), F32)
    message, signal = kernel_call(
        columns_kernel,
        "columns",
        [shape((MESSAGE, LANES), BF16), shape(flat, BF16)],
        [wide, pltpu.VMEM(flat, BF16)],
        [tile_image.reshape(flat), columns],
        16,
        2 * MESSAGE * LEN * LANES,
    )
    received = to_peers(message, ROWS)

    (upstream_rows, filter_rows), _ = after(
        (upstream.reshape(flat), spectral_filter.reshape(2, LANES, LEN)), message
    )
    dy, *dy_turned = kernel_call(
        unfold_kernel,
        "unfold",
        [shape(flat, BF16)] + [shape((2 * CH, LEN), BF16)] * CH_DEVICES,
        [wide],
        [channel, upstream_rows],
        16,
        smem=1,
        beside=True,
    )
    (up_own, down_own), _ = after((up_weight, down_weight), dy_turned)
    start = lax.axis_index("core") * HALF_UNITS
    own_up = lax.dynamic_slice_in_dim(up_own, start, HALF_UNITS, axis=1).T
    own_down = lax.dynamic_slice_in_dim(down_own, start, HALF_UNITS, axis=0)
    pack = jnp.concatenate([own_up, own_down], axis=1)
    weights = lax.all_gather(pack, ("core", "ch"), axis=0, tiled=True)
    dy_parts = turned_exchange(dy_turned)
    (main,) = kernel_call(
        filter_kernel,
        "filter",
        [shape((2, LEN, LANES), BF16)],
        [wide],
        [filter_rows, straight],
        16,
        2 * 16 * LEN * LEN * CH,
        beside=True,
    )
    received, main = lax.optimization_barrier((received, main))
    row_scratch = [pltpu.VMEM((MESSAGE, LANES), F32), pltpu.VMEM((MESSAGE, LANES), BF16)]
    row_flops = 4 * MESSAGE * MESSAGE * LANES
    message, seen = kernel_call(
        rows_forward_kernel,
        "rows_forward",
        [shape((MESSAGE, SENT), BF16), shape((2, LEN, LANES), BF16)],
        row_scratch,
        [received, *tables, main],
        20,
        row_flops,
    )
    live = (seen, main, signal, dy)
    received, live = fenced(message, ROWS, live)
    seen, main, signal, dy = live
    (hidden,) = kernel_call(
        hidden_kernel,
        "hidden",
        [shape(flat, BF16)],
        [pltpu.VMEM((SENT, LEN), BF16)],
        [received, columns, conv_taps, signal],
        16,
        2 * MESSAGE * LEN * SENT,
    )
    live = (seen, main, dy, hidden)
    hidden_tokens, live = fenced(hidden, "ch", live)
    seen, main, dy, hidden = live
    gain_row = norm_gain.reshape(1, ALL_CH)
    *out_turned, grad_message = mlp(channel, hidden_tokens, dy_parts, gain_row, weights)
    grad_mlp, live = fenced(grad_message, "ch", (seen, main, dy, out_turned, hidden))
    seen, main, dy, out_turned, hidden = live
    (message,) = kernel_call(
        gradient_columns_kernel,
        "gradient_columns",
        [shape((MESSAGE, SENT), BF16)],
        [pltpu.VMEM((SENT, LEN), BF16)],
        [dy, grad_mlp, conv_taps, columns],
        16,
        2 * MESSAGE * LEN * SENT,
    )
    live = (seen, main, dy, out_turned, grad_mlp, hidden)
    received, live = fenced(message, ROWS, live)
    seen, main, dy, out_turned, grad_mlp, hidden = live
    message, products = kernel_call(
        rows_backward_kernel,
        "rows_backward",
        [shape((MESSAGE, LANES), BF16), shape((2, LEN, LANES), BF16)],
        row_scratch,
        [received, *tables, main, seen],
        20,
        row_flops,
    )
    (dy, out_turned, grad_mlp, hidden, products), message = after(
        (dy, out_turned, grad_mlp, hidden, products), message
    )
    received = to_peers(message, ROWS)
    out_parts = turned_exchange(out_turned)
    (block_out,) = kernel_call(
        block_out_kernel, "block_out", [shape(flat, BF16)], [wide], [channel, hidden, *out_parts], 16, smem=1, beside=True
    )
    (grad_filter,) = kernel_call(
        grad_filter_kernel,
        "grad_filter",
        [shape((2, LANES, LEN), F32)],
        [pltpu.VMEM((LEN, CH), BF16), wide],
        [products, straight],
        16,
        2 * 16 * LEN * LEN * CH,
        beside=True,
    )
    (grad_image,) = kernel_call(
        image_kernel,
        "image",
        [shape(flat, F32)],
        [wide],
        [received, columns, dy, grad_mlp],
        16,
        2 * MESSAGE * LEN * LANES,
    )
    slab = (CH, SLAB, LEN)
    return (
        block_out.reshape(slab),
        grad_image.reshape(slab),
        grad_filter.reshape(2, CH, SLAB, LEN),
    )


def solution(mesh):
    devices = mesh.devices.reshape(4, 4, 2, CH_DEVICES)
    token = P("ch", ROWS, None)
    frequency = P(None, "ch", ROWS, None)
    return jax.shard_map(
        on_device,
        mesh=jax.sharding.Mesh(devices, (*ROWS, "ch")),
        in_specs=(token, frequency, P("ch", None), P(), P(None, "ch"), P("ch", None), token),
        out_specs=(token, token, frequency),
        check_vma=False,
    )
```

```python
import jax
import jax.numpy as jnp
import ml_dtypes
import numpy as np
from jax import lax
from jax.experimental import pallas as pl
from jax.experimental.pallas import tpu as pltpu
from jax.sharding import PartitionSpec as P

norm_epsilon = 1e-05
root_half = 0.7071067811865476
density = 0.3989422804014327

ROWS_DEVICES = 32
CH_DEVICES = 4
LEN = 256
SLAB = 8
CH = 192
ALL_CH = 768
LANES = SLAB * CH
WIDE = SLAB * 128
POINTS = LEN * LEN
HALF_UNITS = 384
MESSAGE = 2 * LEN
UNITS = 3072
ROWS = ("y", "z", "core")
SENT = (SLAB + 2) * CH
F32 = jnp.float32
BF16 = jnp.bfloat16
MIB = 1 << 20


def wide_at(h):
    return {-1: LANES, SLAB: LANES + 128}.get(h, 128 * h)


def narrow_at(h):
    return {-1: LANES + 256, SLAB: LANES + 320}.get(h, WIDE + 64 * (2 * (h % 4) + h // 4))


def column_tables():
    w, kw = np.arange(LEN)[None, :], np.arange(LEN)[:, None]
    turn = (2 * np.pi * (kw * w % LEN) / LEN).reshape(ROWS_DEVICES, SLAB, LEN)
    both = np.stack([np.cos(turn), -np.sin(turn)], axis=1)
    return both.reshape(MESSAGE, LEN)


def row_tables():
    k1, src = np.arange(32)[:, None], np.arange(32)[None, :]
    turn = 2 * np.pi * (k1 * src % 32) / 32
    cos, sin = np.cos(turn), np.sin(turn)
    forward = np.zeros((2, SLAB, 32, 32, 2, SLAB))
    inverse = np.zeros((32, 2, SLAB, 2, SLAB, 32))
    for j in range(SLAB):
        forward[0, j, :, :, 0, j], forward[0, j, :, :, 1, j] = cos, sin
        forward[1, j, :, :, 0, j], forward[1, j, :, :, 1, j] = -sin, cos
        inverse[:, 0, j, 0, j, :], inverse[:, 0, j, 1, j, :] = cos.T, -sin.T
        inverse[:, 1, j, 0, j, :], inverse[:, 1, j, 1, j, :] = sin.T, cos.T
    return forward.reshape(MESSAGE, MESSAGE), inverse.reshape(MESSAGE, MESSAGE)


def twiddle_tables():
    token_row = np.zeros(LANES, np.int64)
    for h in range(SLAB):
        token_row[128 * h : 128 * h + 128] = h
        token_row[narrow_at(h) : narrow_at(h) + 64] = h
    turn = 2 * np.pi * (np.arange(32)[:, None] * token_row[None, :] % LEN) / LEN
    return np.cos(turn), np.sin(turn)


def turn_table():
    k2, k1 = np.divmod(np.arange(LEN), 32)
    straight = np.zeros((LEN, LEN))
    straight[np.arange(LEN), k1 + 32 * k2] = 1.0
    return straight


def narrow(table):
    return np.asarray(table, np.float64).astype(ml_dtypes.bfloat16)


COLUMNS = narrow(column_tables())
ROW_TABLES = narrow(np.stack(row_tables()))
TWIDDLES = np.stack(twiddle_tables()).astype(np.float32)
STRAIGHT = narrow(turn_table())
UNIT = narrow(np.eye(LEN))


def nn(a, b):
    return lax.dot_general(a, b, (((1,), (0,)), ((), ())), preferred_element_type=F32)


def nt(a, b):
    return lax.dot_general(a, b, (((1,), (1,)), ((), ())), preferred_element_type=F32)


def tn(a, b):
    return lax.dot_general(a, b, (((0,), (0,)), ((), ())), preferred_element_type=F32)


def whole_block(dims):
    return pl.BlockSpec(dims, lambda *_: (0,) * len(dims), pipeline_mode=pl.Buffered(1))


def kernel_call(body, name, outs, scratch, operands, vmem, flops=0, smem=0, beside=False):
    scalar = pl.BlockSpec(memory_space=pltpu.SMEM)
    moved = sum(a.size * a.dtype.itemsize for a in operands)
    moved += sum(o.size * np.dtype(o.dtype).itemsize for o in outs)
    return pl.pallas_call(
        body,
        name=name,
        grid=(1,),
        out_shape=tuple(outs),
        in_specs=[scalar] * smem + [whole_block(a.shape) for a in operands[smem:]],
        out_specs=tuple(whole_block(o.shape) for o in outs),
        scratch_shapes=scratch,
        cost_estimate=pl.CostEstimate(
            flops=0 if beside else flops,
            bytes_accessed=1024 if beside else moved,
            transcendentals=0,
        ),
        compiler_params=pltpu.CompilerParams(vmem_limit_bytes=vmem * MIB),
    )(*operands)


def shape(dims, dtype):
    return jax.ShapeDtypeStruct(dims, dtype)


def fill_wide(wide_ref, values):
    for side in range(2):
        wide_ref[side] = values[:, side * 128 : side * 128 + 128]


def every_eighth(wide_ref, h):
    return jnp.concatenate([wide_ref[side, pl.ds(h, CH, stride=SLAB), :] for side in range(2)], axis=1)


def put_eighth(wide_ref, first, values):
    for side in range(2):
        at = pl.ds(first, values.shape[0], stride=SLAB)
        wide_ref[side, at, :] = values[:, side * 128 : side * 128 + 128]


def take_wide(wide_ref):
    return jnp.concatenate([wide_ref[side] for side in range(2)], axis=1)


def unfold_rows(source_ref, wide_ref):
    fill_wide(wide_ref, source_ref[...].astype(F32))
    for h in range(SLAB):
        yield h, every_eighth(wide_ref, h).astype(BF16)


def columns_kernel(image_ref, table_ref, message_ref, kept_ref, wide_ref, lanes_ref):
    for h, rows in unfold_rows(image_ref, wide_ref):
        kept_ref[h * CH : (h + 1) * CH] = rows
        lanes_ref[h * 128 : h * 128 + 128] = rows[:128]
        lanes_ref[narrow_at(h) : narrow_at(h) + 64] = rows[128:]
    send_columns(table_ref, lanes_ref, message_ref)


def send_columns(table_ref, lanes_ref, message_ref):
    for at in range(0, lanes_ref.shape[0], 384):
        message_ref[:, at : at + 384] = nt(table_ref[...], lanes_ref[at : at + 384]).astype(BF16)


def unfold_kernel(channel_ref, source_ref, kept_ref, *refs):
    *turned_refs, wide_ref = refs
    for h, rows in unfold_rows(source_ref, wide_ref):
        kept_ref[h * CH : (h + 1) * CH] = rows
    for turn, turned_ref in enumerate(turned_refs):
        peer = lax.rem(channel_ref[0] + turn, CH_DEVICES)
        for half in range(2):
            rows = every_eighth(wide_ref, peer * 2 + half)
            turned_ref[half * CH : half * CH + CH] = rows.astype(BF16)


def put_spectrum(target_ref, part, column, block):
    rows = slice(column * 32, column * 32 + 32)
    for k2 in range(SLAB):
        piece = block[k2 * 32 : k2 * 32 + 32]
        target_ref[part, rows, k2 * 128 : k2 * 128 + 128] = piece[:, :128]
        at = WIDE + 64 * k2
        target_ref[part, rows, at : at + 64] = piece[:, 128:]


def filter_kernel(filter_ref, straight_ref, main_ref, wide_ref):
    for part in range(2):
        fill_wide(wide_ref, filter_ref[part])
        for j in range(SLAB):
            turned = nt(straight_ref[...], every_eighth(wide_ref, j).astype(BF16))
            put_spectrum(main_ref, part, j, (turned * (1.0 / POINTS)).astype(BF16))


def eighth_turn(value, step, sign):
    re, im = value
    if step == 0:
        return value
    if step == 1:
        return (re + sign * im) * root_half, (im - sign * re) * root_half
    if step == 2:
        return sign * im, -sign * re
    return (sign * im - re) * root_half, (-sign * re - im) * root_half


def add(a, b):
    return a[0] + b[0], a[1] + b[1]


def sub(a, b):
    return a[0] - b[0], a[1] - b[1]


def four_points(x, sign):
    s, d = add(x[0], x[2]), sub(x[0], x[2])
    t, u = add(x[1], x[3]), eighth_turn(sub(x[1], x[3]), 2, sign)
    return [add(s, t), add(d, u), sub(s, t), sub(d, u)]


def eight_points(x, sign):
    even = four_points([add(x[m], x[m + 4]) for m in range(4)], sign)
    odd = four_points([eighth_turn(sub(x[m], x[m + 4]), m, sign) for m in range(4)], sign)
    return [part[q] for q in range(4) for part in (even, odd)]


def upper_lanes(like):
    return lax.broadcasted_iota(jnp.int32, like.shape, 1) >= 64


def halves(value):
    upper = upper_lanes(value)
    return pltpu.roll(value, 64, axis=1) + jnp.where(upper, -value, value)


def upper_turn(value, step, sign):
    upper = upper_lanes(value[0])
    return tuple(jnp.where(upper, b, a) for a, b in zip(value, eighth_turn(value, step, sign)))


def narrow_forward(x, sign):
    turned = [upper_turn((halves(re), halves(im)), m, sign) for m, (re, im) in enumerate(x)]
    return four_points(turned, sign)


def narrow_inverse(x, sign):
    turned = [upper_turn(v, m, sign) for m, v in enumerate(four_points(x, sign))]
    return [(halves(re), halves(im)) for re, im in turned]


def lane_blocks(re, im):
    return [(re[:, at : at + 128], im[:, at : at + 128]) for at in range(0, LANES, 128)]


def to_frequencies(re, im, cos, sin):
    x = lane_blocks(re * cos + im * sin, im * cos - re * sin)
    return eight_points(x[:SLAB], 1.0) + narrow_forward(x[SLAB:], 1.0)


def to_tokens_rows(blocks, cos, sin):
    y = eight_points(blocks[:SLAB], -1.0) + narrow_inverse(blocks[SLAB:], -1.0)
    re = jnp.concatenate([v[0] for v in y], axis=1)
    im = jnp.concatenate([v[1] for v in y], axis=1)
    return re * cos - im * sin, im * cos + re * sin


def moved_rows(block, step):
    rows = 2 * SLAB
    empty = jnp.zeros((rows, block.shape[1]), block.dtype)
    if step > 0:
        return jnp.concatenate([empty, block[:-rows]], axis=0)
    return jnp.concatenate([block[rows:], empty], axis=0)


def row_body(saves, refs):
    received_ref, tables_ref, twiddles_ref, main_ref = refs[:4]
    if saves:
        message_ref, seen_ref, mixed_ref, ready_ref = refs[4:]
    else:
        seen_ref, message_ref, product_ref, mixed_ref, ready_ref = refs[4:]

    def joined(at, width, edge, step):
        rows = received_ref[:, at : at + width].astype(F32)
        moved = moved_rows(received_ref[:, edge : edge + width].astype(F32), step)
        return nn(tables_ref[0], (rows + moved).astype(BF16))

    for at in range(0, LANES, 512):
        mixed_ref[:, at : at + 512] = nn(tables_ref[0], received_ref[:, at : at + 512])
    if not saves:
        for h, edge, step in ((0, SLAB, 1), (SLAB - 1, -1, -1)):
            at = wide_at(h)
            mixed_ref[:, at : at + 128] = joined(at, 128, wide_at(edge), step)
            at = narrow_at(h)
            mixed_ref[:, at : at + 64] = joined(at, 64, narrow_at(edge), step)

    def group(index, carry):
        at = pl.ds(pl.multiple_of(index * 16, 16), 16)
        at_im = pl.ds(pl.multiple_of(LEN + index * 16, 16), 16)
        table = pl.ds(pl.multiple_of(lax.rem(index, 2) * 16, 16), 16)
        cos, sin = twiddles_ref[0, table, :], twiddles_ref[1, table, :]
        values = to_frequencies(mixed_ref[at, :], mixed_ref[at_im, :], cos, sin)
        filtered = []
        for n, (re, im) in enumerate(values):
            lanes = slice(n * 128, n * 128 + 128)
            k_re, k_im = main_ref[0, at, lanes].astype(F32), main_ref[1, at, lanes].astype(F32)
            if saves:
                seen_ref[0, at, lanes], seen_ref[1, at, lanes] = re.astype(BF16), im.astype(BF16)
                filtered.append((re * k_re - im * k_im, im * k_re + re * k_im))
            else:
                x_re, x_im = seen_ref[0, at, lanes].astype(F32), seen_ref[1, at, lanes].astype(F32)
                product_re = (x_re * re + x_im * im) * (1.0 / POINTS)
                product_im = (im * x_re - re * x_im) * (1.0 / POINTS)
                product_ref[0, at, lanes] = product_re.astype(BF16)
                product_ref[1, at, lanes] = product_im.astype(BF16)
                filtered.append((re * k_re + im * k_im, im * k_re - re * k_im))
        re, im = to_tokens_rows(filtered, cos, sin)
        ready_ref[at, :] = re.astype(BF16)
        ready_ref[at_im, :] = im.astype(BF16)
        return carry

    lax.fori_loop(0, 16, group, 0)
    for at in range(0, LANES, 512):
        block = nn(tables_ref[1], ready_ref[:, at : at + 512])
        message_ref[:, at : at + 512] = block.astype(BF16)
        if saves:
            for h, edge, step in ((0, SLAB, -1), (SLAB - 1, -1, 1)):
                for place, width in ((wide_at, 128), (narrow_at, 64)):
                    start = place(h) - at
                    if 0 <= start < 512:
                        moved = moved_rows(block[:, start : start + width], step)
                        message_ref[:, place(edge) : place(edge) + width] = moved.astype(BF16)


def rows_forward_kernel(*refs):
    row_body(True, refs)


def rows_backward_kernel(*refs):
    row_body(False, refs)


def token_rows(received_ref, table_ref, place):
    for h in range(SLAB):
        place(h, 0, tn(received_ref[:, h * 128 : h * 128 + 128], table_ref[...]))
    for m in range(4):
        at = WIDE + 128 * m
        block = tn(received_ref[:, at : at + 128], table_ref[...])
        place(m, 128, block[:64])
        place(m + 4, 128, block[64:])


def convolve(load, rows, taps, put):
    lane = lax.broadcasted_iota(jnp.int32, (16, LEN), 1)
    window = [load(rows[0] - 1), load(rows[0])]
    for h in rows:
        window.append(load(h + 1))
        sums = []
        for b in range(3):
            terms = [taps[3 * a + b] * w for a, w in enumerate(window) if w is not None]
            sums.append(sum(terms[1:], terms[0]))
        left = jnp.where(lane == 0, 0.0, pltpu.roll(sums[0], 1, axis=1))
        right = jnp.where(lane == LEN - 1, 0.0, pltpu.roll(sums[2], LEN - 1, axis=1))
        put(h, sums[1] + left + right)
        window.pop(0)


def every_chunk(body):
    def wide(index, carry):
        at = pl.multiple_of(index * 16, 16)
        body(at, lambda h: pl.ds(pl.multiple_of(wide_at(h) + at, 16), 16))
        return carry

    def last(index, carry):
        at = pl.multiple_of(index * 16, 16)
        body(at + 128, lambda h: pl.ds(pl.multiple_of(narrow_at(h) + at, 16), 16))
        return carry

    lax.fori_loop(0, 8, wide, 0)
    lax.fori_loop(0, 4, last, 0)


def rows_at(h, start):
    return pl.ds(pl.multiple_of(h * CH + start, 16), 16)


def spread_taps(taps_ref, start, order):
    taps = taps_ref[pl.ds(pl.multiple_of(start, 16), 16), :]
    return [jnp.broadcast_to(taps[:, k : k + 1], (16, LEN)) for k in order]


def hidden_kernel(received_ref, table_ref, taps_ref, signal_ref, hidden_ref, filtered_ref):
    for at in range(0, SENT, 128):
        block = tn(received_ref[:, at : at + 128], table_ref[...])
        filtered_ref[at : at + 128] = block.astype(BF16)

    def chunk(start, place):
        def load(h):
            return filtered_ref[place(h), :].astype(F32)

        def put(h, convolved):
            at = rows_at(h, start)
            hidden_ref[at, :] = (signal_ref[at, :].astype(F32) + convolved).astype(BF16)

        convolve(load, range(SLAB), spread_taps(taps_ref, start, range(9)), put)

    every_chunk(chunk)


def gradient_columns_kernel(upstream_ref, mlp_ref, taps_ref, table_ref, message_ref, lanes_ref):
    def chunk(start, place):
        def load(h):
            if h < 0 or h >= SLAB:
                return None
            at = rows_at(h, start)
            return upstream_ref[at, :].astype(F32) + mlp_ref[at, :].astype(F32)

        def put(h, convolved):
            lanes_ref[place(h), :] = convolved.astype(BF16)

        convolve(
            load, range(-1, SLAB + 1), spread_taps(taps_ref, start, range(8, -1, -1)), put
        )

    every_chunk(chunk)
    send_columns(table_ref, lanes_ref, message_ref)


def gelu_parts(pre_act):
    cumulative = 0.5 * (1.0 + lax.erf(pre_act * root_half))
    bell = density * jnp.exp(-0.5 * pre_act * pre_act)
    return pre_act * cumulative, cumulative + pre_act * bell


def mlp_kernel(
    channel_ref,
    hidden_ref,
    own_dy_ref,
    dy_one_ref,
    dy_two_ref,
    dy_three_ref,
    gain_ref,
    unit_ref,
    mine_ref,
    other_ref,
    out_own_ref,
    out_one_ref,
    out_two_ref,
    out_three_ref,
    grad_ref,
    parts_ref,
    gathered_ref,
    scaled_ref,
    dy_ref,
    normed_ref,
    inv_ref,
    out_sum_ref,
    grad_sum_ref,
):
    step = pl.program_id(0)
    channel = channel_ref[0]

    def turn_in(half):
        for src in range(CH_DEVICES):
            at = src * 2 * CH + half * CH
            gathered_ref[src * CH : (src + 1) * CH] = hidden_ref[at : at + CH]
        return nt(unit_ref[...], gathered_ref[...])

    def turn_in_dy(half):
        for src in range(CH_DEVICES):
            gathered_ref[src * CH : (src + 1) * CH] = parts_ref[src, half * CH : half * CH + CH]
        return nt(unit_ref[...], gathered_ref[...])

    @pl.when(step == 0)
    def _():
        for turn, source_ref in enumerate((own_dy_ref, dy_one_ref, dy_two_ref, dy_three_ref)):
            parts_ref[lax.rem(channel + CH_DEVICES - turn, CH_DEVICES)] = source_ref[...]
        for half in range(2):
            rows = slice(half * LEN, half * LEN + LEN)
            values = turn_in(half)
            centred = values - jnp.mean(values, axis=1, keepdims=True)
            variance = jnp.mean(centred * centred, axis=1, keepdims=True)
            inv_std = lax.rsqrt(variance + norm_epsilon)
            normed = centred * inv_std
            normed_ref[rows] = normed
            inv_ref[rows] = jnp.broadcast_to(inv_std, (LEN, 128))
            scaled_ref[rows] = (normed * gain_ref[...]).astype(BF16)
            dy_ref[rows] = turn_in_dy(half).astype(BF16)
        out_sum_ref[...] = jnp.zeros_like(out_sum_ref)
        grad_sum_ref[...] = jnp.zeros_like(grad_sum_ref)

    for weights_ref in (mine_ref, other_ref):
        up, down = weights_ref[:, :ALL_CH], weights_ref[:, ALL_CH:]
        pre_act = nt(scaled_ref[...], up)
        grad_act = nt(dy_ref[...], down)
        activated, slope = gelu_parts(pre_act)
        out_sum_ref[...] += nn(activated.astype(BF16), down)
        grad_sum_ref[...] += nn((grad_act * slope).astype(BF16), up)

    def turn_out(values, half, put):
        for block in range(3):
            piece = nt(unit_ref[...], values[:, block * LEN : (block + 1) * LEN])
            gathered_ref[block * LEN : (block + 1) * LEN] = piece.astype(BF16)
        for dst in range(CH_DEVICES):
            put(dst, half, gathered_ref[dst * CH : (dst + 1) * CH])

    def put_grad(dst, half, rows):
        at = (dst * 2 + half) * CH
        grad_ref[at : at + CH] = rows

    def put_out(dst, half, rows):
        parts_ref[dst, half * CH : half * CH + CH] = rows

    @pl.when(step == pl.num_programs(0) - 1)
    def _():
        for half in range(2):
            rows = slice(half * LEN, half * LEN + LEN)
            weighted = grad_sum_ref[rows] * gain_ref[...]
            normed = normed_ref[rows]
            first = jnp.mean(weighted, axis=1, keepdims=True)
            second = jnp.mean(weighted * normed, axis=1, keepdims=True)
            term = inv_ref[rows, 0:1] * (weighted - first - normed * second)
            turn_out(term.astype(BF16), half, put_grad)
            turn_out(out_sum_ref[rows].astype(BF16), half, put_out)
        for turn, out_ref in enumerate((out_own_ref, out_one_ref, out_two_ref, out_three_ref)):
            out_ref[...] = parts_ref[lax.rem(channel + turn, CH_DEVICES)]


def mlp(channel, hidden, dy_parts, gain, weights, block=512):
    tokens, steps = 2 * LEN, UNITS // 2 // block
    part = whole_block((2 * CH, LEN))
    return pl.pallas_call(
        mlp_kernel,
        name="mlp",
        grid=(steps,),
        out_shape=(*(shape((2 * CH, LEN), BF16),) * CH_DEVICES, shape((LANES, LEN), BF16)),
        in_specs=[
            pl.BlockSpec(memory_space=pltpu.SMEM),
            whole_block((LANES, LEN)),
            part,
            part,
            part,
            part,
            whole_block((1, ALL_CH)),
            whole_block((LEN, LEN)),
            pl.BlockSpec((block, 2 * ALL_CH), lambda i: (i, 0)),
            pl.BlockSpec((block, 2 * ALL_CH), lambda i: (i + steps, 0)),
        ],
        out_specs=(part, part, part, part, whole_block((LANES, LEN))),
        scratch_shapes=[
            pltpu.VMEM((CH_DEVICES, 2 * CH, LEN), BF16),
            pltpu.VMEM((ALL_CH, LEN), BF16),
            pltpu.VMEM((tokens, ALL_CH), BF16),
            pltpu.VMEM((tokens, ALL_CH), BF16),
            pltpu.VMEM((tokens, ALL_CH), F32),
            pltpu.VMEM((tokens, 128), F32),
            pltpu.VMEM((tokens, ALL_CH), F32),
            pltpu.VMEM((tokens, ALL_CH), F32),
        ],
        cost_estimate=pl.CostEstimate(
            flops=8 * tokens * UNITS * ALL_CH,
            bytes_accessed=4 * UNITS * ALL_CH + 8 * LANES * LEN,
            transcendentals=2 * tokens * UNITS,
        ),
        compiler_params=pltpu.CompilerParams(vmem_limit_bytes=48 * MIB),
    )(channel, hidden, *dy_parts, gain, jnp.asarray(UNIT), weights, weights)


def block_out_kernel(channel_ref, hidden_ref, own_ref, one_ref, two_ref, three_ref, out_ref, wide_ref):
    for turn, sum_ref in enumerate((own_ref, one_ref, two_ref, three_ref)):
        src = lax.rem(channel_ref[0] + CH_DEVICES - turn, CH_DEVICES)
        for half in range(2):
            rows = pl.ds(pl.multiple_of((src * 2 + half) * CH, 64), CH)
            total = hidden_ref[rows, :].astype(F32)
            total += sum_ref[half * CH : half * CH + CH].astype(F32)
            put_eighth(wide_ref, src * 2 + half, total)
    out_ref[...] = take_wide(wide_ref).astype(BF16)


def image_kernel(received_ref, table_ref, upstream_ref, mlp_ref, out_ref, wide_ref):
    def place(h, channel, block):
        count = block.shape[0]
        rows = slice(h * CH + channel, h * CH + channel + count)
        total = block + upstream_ref[rows].astype(F32) + mlp_ref[rows].astype(F32)
        put_eighth(wide_ref, channel * SLAB + h, total)

    token_rows(received_ref, table_ref, place)
    out_ref[...] = take_wide(wide_ref)


def grad_filter_kernel(product_ref, straight_ref, out_ref, block_ref, wide_ref):
    for part in range(2):
        for j in range(SLAB):
            rows = slice(j * 32, j * 32 + 32)
            for k2 in range(SLAB):
                to = slice(k2 * 32, k2 * 32 + 32)
                at = WIDE + 64 * k2
                block_ref[to, :128] = product_ref[part, rows, k2 * 128 : k2 * 128 + 128]
                block_ref[to, 128:] = product_ref[part, rows, at : at + 64]
            put_eighth(wide_ref, j, tn(block_ref[...], straight_ref[...]))
        out_ref[part] = take_wide(wide_ref)


def to_peers(values, axis):
    return lax.all_to_all(values, axis, split_axis=0, concat_axis=0, tiled=True)


def turned_exchange(parts):
    received = [parts[0]]
    for turn in range(1, CH_DEVICES):
        pairs = [(i, (i + turn) % CH_DEVICES) for i in range(CH_DEVICES)]
        received.append(lax.ppermute(parts[turn], "ch", pairs))
    return received


def after(value, earlier):
    return lax.optimization_barrier((value, earlier))


def fenced(values, axis, live):
    values, live = lax.optimization_barrier((values, live))
    return lax.optimization_barrier((to_peers(values, axis), live))


def on_device(tile_image, spectral_filter, conv_taps, norm_gain, up_weight, down_weight, upstream):
    channel = lax.axis_index("ch").reshape(1).astype(jnp.int32)
    flat = (LANES, LEN)
    tables = [jnp.asarray(ROW_TABLES), jnp.asarray(TWIDDLES)]
    columns, straight = jnp.asarray(COLUMNS), jnp.asarray(STRAIGHT)
    wide = pltpu.VMEM((2, LANES, 128), F32)
    message, signal = kernel_call(
        columns_kernel,
        "columns",
        [shape((MESSAGE, LANES), BF16), shape(flat, BF16)],
        [wide, pltpu.VMEM(flat, BF16)],
        [tile_image.reshape(flat), columns],
        16,
        2 * MESSAGE * LEN * LANES,
    )
    received = to_peers(message, ROWS)

    (upstream_rows, filter_rows), _ = after(
        (upstream.reshape(flat), spectral_filter.reshape(2, LANES, LEN)), message
    )
    dy, *dy_turned = kernel_call(
        unfold_kernel,
        "unfold",
        [shape(flat, BF16)] + [shape((2 * CH, LEN), BF16)] * CH_DEVICES,
        [wide],
        [channel, upstream_rows],
        16,
        smem=1,
        beside=True,
    )
    (up_own, down_own), _ = after((up_weight, down_weight), dy_turned)
    start = lax.axis_index("core") * HALF_UNITS
    own_up = lax.dynamic_slice_in_dim(up_own, start, HALF_UNITS, axis=1).T
    own_down = lax.dynamic_slice_in_dim(down_own, start, HALF_UNITS, axis=0)
    pack = jnp.concatenate([own_up, own_down], axis=1)
    weights = lax.all_gather(pack, ("core", "ch"), axis=0, tiled=True)
    dy_parts = turned_exchange(dy_turned)
    (main,) = kernel_call(
        filter_kernel,
        "filter",
        [shape((2, LEN, LANES), BF16)],
        [wide],
        [filter_rows, straight],
        16,
        2 * 16 * LEN * LEN * CH,
        beside=True,
    )
    received, dy_parts, main = lax.optimization_barrier((received, dy_parts, main))
    row_scratch = [pltpu.VMEM((MESSAGE, LANES), F32), pltpu.VMEM((MESSAGE, LANES), BF16)]
    row_flops = 4 * MESSAGE * MESSAGE * LANES
    message, seen = kernel_call(
        rows_forward_kernel,
        "rows_forward",
        [shape((MESSAGE, SENT), BF16), shape((2, LEN, LANES), BF16)],
        row_scratch,
        [received, *tables, main],
        20,
        row_flops,
    )
    live = (seen, main, signal, dy, dy_parts, conv_taps, norm_gain)
    received, live = fenced(message, ROWS, live)
    seen, main, signal, dy, dy_parts, conv_taps, norm_gain = live
    (hidden,) = kernel_call(
        hidden_kernel,
        "hidden",
        [shape(flat, BF16)],
        [pltpu.VMEM((SENT, LEN), BF16)],
        [received, columns, conv_taps, signal],
        16,
        2 * MESSAGE * LEN * SENT,
    )
    live = (seen, main, dy, dy_parts, conv_taps, norm_gain.reshape(1, ALL_CH), hidden)
    hidden_tokens, live = fenced(hidden, "ch", live)
    seen, main, dy, dy_parts, conv_taps, gain_row, hidden = live
    *out_turned, grad_message = mlp(channel, hidden_tokens, dy_parts, gain_row, weights)
    grad_mlp, live = fenced(grad_message, "ch", (seen, main, dy, out_turned, conv_taps, hidden))
    seen, main, dy, out_turned, conv_taps, hidden = live
    (message,) = kernel_call(
        gradient_columns_kernel,
        "gradient_columns",
        [shape((MESSAGE, SENT), BF16)],
        [pltpu.VMEM((SENT, LEN), BF16)],
        [dy, grad_mlp, conv_taps, columns],
        16,
        2 * MESSAGE * LEN * SENT,
    )
    live = (seen, main, dy, out_turned, grad_mlp, hidden)
    received, live = fenced(message, ROWS, live)
    seen, main, dy, out_turned, grad_mlp, hidden = live
    message, products = kernel_call(
        rows_backward_kernel,
        "rows_backward",
        [shape((MESSAGE, LANES), BF16), shape((2, LEN, LANES), BF16)],
        row_scratch,
        [received, *tables, main, seen],
        20,
        row_flops,
    )
    (dy, out_turned, grad_mlp, hidden, products), message = after(
        (dy, out_turned, grad_mlp, hidden, products), message
    )
    received = to_peers(message, ROWS)
    out_parts = turned_exchange(out_turned)
    (block_out,) = kernel_call(
        block_out_kernel, "block_out", [shape(flat, BF16)], [wide], [channel, hidden, *out_parts], 16, smem=1, beside=True
    )
    (grad_filter,) = kernel_call(
        grad_filter_kernel,
        "grad_filter",
        [shape((2, LANES, LEN), F32)],
        [pltpu.VMEM((LEN, CH), BF16), wide],
        [products, straight],
        16,
        2 * 16 * LEN * LEN * CH,
        beside=True,
    )
    (grad_image,) = kernel_call(
        image_kernel,
        "image",
        [shape(flat, F32)],
        [wide],
        [received, columns, dy, grad_mlp],
        16,
        2 * MESSAGE * LEN * LANES,
    )
    slab = (CH, SLAB, LEN)
    return (
        block_out.reshape(slab),
        grad_image.reshape(slab),
        grad_filter.reshape(2, CH, SLAB, LEN),
    )


def solution(mesh):
    devices = mesh.devices.reshape(4, 4, 2, CH_DEVICES)
    token = P("ch", ROWS, None)
    frequency = P(None, "ch", ROWS, None)
    return jax.shard_map(
        on_device,
        mesh=jax.sharding.Mesh(devices, (*ROWS, "ch")),
        in_specs=(token, frequency, P("ch", None), P(), P(None, "ch"), P("ch", None), token),
        out_specs=(token, token, frequency),
        check_vma=False,
    )
```
